32 devices in a mesh: dp: 8 (over z, core), vocab: 4 (over y, x).
Axes of the slice: x: 2, y: 2, z: 4, core: 2. Of those that a mesh axis runs over, the one named last changes fastest.
Arguments:
- token_ids: int32 [10240], P(('dp', 'vocab')), may hold values from 0 to 49151
- parents: int32 [32, 13], P(('dp', 'vocab')), may hold values from 0 to 4, as said below
- comp_pos: int32 [32, 80], P(('dp', 'vocab')), may hold values from -1 to 319, as said below
- targets: int32 [32, 80], P(('dp', 'vocab')), may hold values from 0 to 49151
- table: float32 [49152, 768], P('vocab', 'dp')
- table_mean: float32 [49152, 768], P('vocab', 'dp'), may hold values from -2.2888184e-05 to 2.2888184e-05
- table_square: float32 [49152, 768], P('vocab', 'dp'), may hold values from 1.00234017e-13 to 8.0187213e-13
- qkv_proj: float32 [2, 768, 896], P(None, ('dp', 'vocab')), may hold values from -0.21875 to 0.21875
- qkv_mean: float32 [2, 768, 896], P(None, ('dp', 'vocab')), may hold values from -2.2888184e-05 to 2.2888184e-05
- qkv_square: float32 [2, 768, 896], P(None, ('dp', 'vocab')), may hold values from 1.00234017e-13 to 8.0187213e-13
- out_proj: float32 [2, 768, 768], P(None, ('dp', 'vocab')), may hold values from -1.25 to 1.25
- out_mean: float32 [2, 768, 768], P(None, ('dp', 'vocab')), may hold values from -2.2888184e-05 to 2.2888184e-05
- out_square: float32 [2, 768, 768], P(None, ('dp', 'vocab')), may hold values from 1.00234017e-13 to 8.0187213e-13
- up_proj: float32 [2, 768, 3072], P(None, ('dp', 'vocab')), may hold values from -0.21875 to 0.21875
- up_mean: float32 [2, 768, 3072], P(None, ('dp', 'vocab')), may hold values from -2.2888184e-05 to 2.2888184e-05
- up_square: float32 [2, 768, 3072], P(None, ('dp', 'vocab')), may hold values from 1.00234017e-13 to 8.0187213e-13
- down_proj: float32 [2, 3072, 768], P(None, ('dp', 'vocab')), may hold values from -0.109375 to 0.109375
- down_mean: float32 [2, 3072, 768], P(None, ('dp', 'vocab')), may hold values from -2.2888184e-05 to 2.2888184e-05
- down_square: float32 [2, 3072, 768], P(None, ('dp', 'vocab')), may hold values from 1.00234017e-13 to 8.0187213e-13
- vectors: float32 [18560], replicated
- vec_mean: float32 [18560], replicated, may hold values from -9.1552734e-05 to 9.1552734e-05
- vec_square: float32 [18560], replicated, may hold values from 1.6037443e-12 to 1.2829954e-11
- pos_table: float32 [160, 768], replicated, may hold values from -4 to 4
- pos_mean: float32 [160, 768], replicated, may hold values from -2.2888184e-05 to 2.2888184e-05
- pos_square: float32 [160, 768], replicated, may hold values from 1.00234017e-13 to 8.0187213e-13
Outputs:
- loss_sum: float32 [], replicated
- loss_count: float32 [], replicated
- grad_norm: float32 [], replicated
- new_table: float32 [49152, 768], P('vocab', 'dp')
- new_table_mean: float32 [49152, 768], P('vocab', 'dp')
- new_table_square: float32 [49152, 768], P('vocab', 'dp')
- new_qkv: float32 [2, 768, 896], P(None, ('dp', 'vocab'))
- new_qkv_mean: float32 [2, 768, 896], P(None, ('dp', 'vocab'))
- new_qkv_square: float32 [2, 768, 896], P(None, ('dp', 'vocab'))
- new_out: float32 [2, 768, 768], P(None, ('dp', 'vocab'))
- new_out_mean: float32 [2, 768, 768], P(None, ('dp', 'vocab'))
- new_out_square: float32 [2, 768, 768], P(None, ('dp', 'vocab'))
- new_up: float32 [2, 768, 3072], P(None, ('dp', 'vocab'))
- new_up_mean: float32 [2, 768, 3072], P(None, ('dp', 'vocab'))
- new_up_square: float32 [2, 768, 3072], P(None, ('dp', 'vocab'))
- new_down: float32 [2, 3072, 768], P(None, ('dp', 'vocab'))
- new_down_mean: float32 [2, 3072, 768], P(None, ('dp', 'vocab'))
- new_down_square: float32 [2, 3072, 768], P(None, ('dp', 'vocab'))
- new_vectors: float32 [18560], replicated
- new_vec_mean: float32 [18560], replicated
- new_vec_square: float32 [18560], replicated
- new_pos: float32 [160, 768], replicated
- new_pos_mean: float32 [160, 768], replicated
- new_pos_square: float32 [160, 768], replicated
The draws below stay inside these ranges and needn't reach their ends.
Inputs may be any that keep to these rules, and one draw needn't show every extreme that they name: `parents`: in each tree, segment 0 is its own parent, segments 1 to 4 have parent 0, and segments 5 to 12 have a branch (1 to 4) as parent, each branch exactly two leaves. `comp_pos`: each tree's row lists distinct positions of that tree in its first slots, followed by -1; the tree of the highest index fills all 80 slots.
All inputs are finite; a program needn't handle non-finite values.
Results may differ from the reference program's by a relative error of at most 0.0083.
The reference program's roundings to bfloat16 on the way count: a program that leaves them out, or rounds other values in their place, can miss the bound.
Values may be sent and summed in bfloat16 or wider, within the bound.
No kernel may reach another device: no remote copies, remote signals or barrier semaphores. Data moves between devices by JAX's collectives and lax.ppermute only.
A program may use at most 320 MiB of HBM per device.

```python
import math
import jax
import jax.numpy as jnp
import numpy as np
from jax import lax

D = 768
HD = 64
FF = 3072
V = 49152
L = 2
NSEG = 13
STEP = 10
SEG = 16
TREES = 32
TOK_DEV = 320
PATH = 160
COMP = 80
TOKENS = 10240
QKV = 896
NVEC = 18560
NPARAM = 49883264
N_DP = 8
N_VOCAB = 4


def draw_table(key, part):
    key = jax.random.fold_in(key, 11)
    ranks = jnp.arange(V, dtype=jnp.float32)[:, None]
    raw = jax.random.normal(key, (V, D), jnp.float32)
    rise = 1.0 + 2.0 * ranks / (V - 1)
    return raw * rise / math.sqrt(D)


def draw_vectors(key, part):
    key = jax.random.fold_in(key, 12)
    noise = jax.random.normal(key, (NVEC,), jnp.float32)
    ramp = 0.5 + jnp.arange(D, dtype=jnp.float32) / (D - 1)
    blank_model = jnp.zeros((D,), jnp.float32)
    blank_head = jnp.zeros((HD,), jnp.float32)
    blank_hidden = jnp.zeros((FF,), jnp.float32)
    layer_base = jnp.concatenate([ramp, blank_model, blank_model, blank_head, blank_model, ramp, blank_model, blank_hidden, blank_model])
    layer_flag = jnp.concatenate([blank_model + 1.0, blank_model, blank_model, blank_head, blank_model, blank_model + 1.0, blank_model, blank_hidden, blank_model])
    base = jnp.concatenate([jnp.tile(layer_base, L), ramp, blank_model])
    flags = jnp.concatenate([jnp.tile(layer_flag, L), blank_model + 1.0, blank_model])
    return jnp.where(flags > 0.5, base * (1.0 + 0.1 * noise), 0.2 * noise)


def draw_parents(key, part):
    key = jax.random.fold_in(key, 13)
    keys_all = jax.random.split(key, TREES)
    pairs = jnp.array([1, 1, 2, 2, 3, 3, 4, 4], jnp.int32)
    leaves = jax.vmap(lambda sub_key: jax.random.permutation(sub_key, pairs))(keys_all)
    return jnp.concatenate([jnp.zeros((TREES, 5), jnp.int32), leaves.astype(jnp.int32)], 1)


def draw_comp_pos(key, part):
    key = jax.random.fold_in(key, 14)
    first_key, second_key = jax.random.split(key)
    trees_idx = jnp.arange(TREES, dtype=jnp.int32)
    row_dp = trees_idx // N_VOCAB
    row_vocab = trees_idx % N_VOCAB
    span_dp = max(N_DP - 1, 1)
    span_vocab = max(N_VOCAB - 1, 1)
    full = COMP * (span_dp + 2 * row_dp) * (span_vocab + 2 * row_vocab) // (9 * span_dp * span_vocab)
    jitter = jax.random.randint(first_key, (TREES,), 0, max(COMP // 8, 1) + 1)
    jitter = jnp.where(trees_idx == TREES - 1, 0, jitter)
    filled = jnp.clip(full - jitter, 1, COMP)
    keys_all = jax.random.split(second_key, TREES)
    picks = jax.vmap(lambda sub_key: jax.random.permutation(sub_key, TOK_DEV - 1)[:COMP])(keys_all).astype(jnp.int32)
    slots = jnp.arange(COMP, dtype=jnp.int32)
    picks = jnp.where((trees_idx[:, None] == TREES - 1) & (slots[None, :] == 0), TOK_DEV - 1, picks)
    return jnp.where(slots[None, :] < filled[:, None], picks, -1).astype(jnp.int32)


def plant(values, stream_key, smallest, high):
    place = [jax.random.randint(jax.random.fold_in(stream_key, axis), (), 0, length) for axis, length in enumerate(values.shape)]
    main_axis = values.shape.index(max(values.shape))
    next_to = place[:main_axis] + [(place[main_axis] + 1) % values.shape[main_axis]] + place[main_axis + 1:]
    return values.at[tuple(place)].set(smallest).at[tuple(next_to)].set(high)


def level_of(own_key, dims, cuts, least, top_value):
    factor_of, own = 1.0, jax.random.fold_in(own_key, 6)
    for position, blocks in cuts:
        draws = jnp.exp(jax.random.uniform(jax.random.fold_in(own, position), (blocks,), jnp.float32, least / len(cuts), top_value / len(cuts)))
        factor_of = factor_of * jnp.repeat(draws, dims[position] // blocks).reshape([-1 if axis == position else 1 for axis in range(len(dims))])
    return factor_of


def rank_bounds(amount, slope):
    loads = [(1 << 20) // math.isqrt(standing ** slope) + 1 for standing in range(1, amount + 1)]
    scale = 1 + sum(loads) // (1 << 30)
    return np.cumsum(np.array([max(1, weight // scale) for weight in loads]))


def ranked(rng, extent, amount, slope):
    grid = rank_bounds(amount, slope)
    ticket = jax.random.randint(jax.random.fold_in(rng, 1), extent, 0, int(grid[amount - 1]))
    rank = jnp.searchsorted(jnp.asarray(grid, jnp.int32), ticket, side="right")
    return jax.random.permutation(jax.random.fold_in(rng, 2), amount)[rank].astype(jnp.int32)


def normal_values(key, extent, scale, bound, cuts=(), kind=jnp.bfloat16):
    values = jax.random.normal(key, extent, jnp.float32) * scale
    if len(cuts) > 0:
        values = level_of(key, extent, cuts, -0.22, 0.18) * values
    return jnp.clip(values, min=-bound, max=bound).astype(kind)


def setup_inputs(seed: int = 0) -> dict:
    key_of = jax.random.split(jax.random.key(seed), 26)
    return {
        "token_ids": plant(ranked(key_of[0], (TOKENS,), V, 2), jax.random.fold_in(key_of[0], 3), 0, V - 1).astype(jnp.int32),
        "parents": draw_parents(jax.random.fold_in(key_of[25], 71), 0),
        "comp_pos": draw_comp_pos(jax.random.fold_in(key_of[25], 71), 0),
        "targets": plant(ranked(key_of[3], (TREES, COMP), V, 2), jax.random.fold_in(key_of[3], 3), 0, V - 1).astype(jnp.int32),
        "table": draw_table(jax.random.fold_in(key_of[25], 71), 0),
        "table_mean": normal_values(key_of[5], (V, D), (0.011 / NPARAM ** 0.5), 2.288818359375e-05, ((0, 4), (1, 8)), jnp.float32),
        "table_square": jnp.clip(jnp.exp(math.log(8.018721320626754e-13) - 2.0794415 * jax.random.uniform(key_of[6], (V, D), jnp.float32) ** level_of(key_of[6], (V, D), ((0, 4), (1, 8)), -0.2, 0.2)), 1.0023401650783442e-13, 8.018721320626754e-13),
        "qkv_proj": normal_values(key_of[7], (L, D, QKV), D ** -0.5, 0.21875, ((1, 32),), jnp.float32),
        "qkv_mean": normal_values(key_of[8], (L, D, QKV), (0.011 / NPARAM ** 0.5), 2.288818359375e-05, ((1, 32),), jnp.float32),
        "qkv_square": jnp.clip(jnp.exp(math.log(8.018721320626754e-13) - 2.0794415 * jax.random.uniform(key_of[9], (L, D, QKV), jnp.float32) ** level_of(key_of[9], (L, D, QKV), ((1, 32),), -0.2, 0.2)), 1.0023401650783442e-13, 8.018721320626754e-13),
        "out_proj": normal_values(key_of[10], (L, D, D), (D // 32) ** -0.5, 1.25, ((1, 32),), jnp.float32),
        "out_mean": normal_values(key_of[11], (L, D, D), (0.011 / NPARAM ** 0.5), 2.288818359375e-05, ((1, 32),), jnp.float32),
        "out_square": jnp.clip(jnp.exp(math.log(8.018721320626754e-13) - 2.0794415 * jax.random.uniform(key_of[12], (L, D, D), jnp.float32) ** level_of(key_of[12], (L, D, D), ((1, 32),), -0.2, 0.2)), 1.0023401650783442e-13, 8.018721320626754e-13),
        "up_proj": normal_values(key_of[13], (L, D, FF), D ** -0.5, 0.21875, ((1, 32),), jnp.float32),
        "up_mean": normal_values(key_of[14], (L, D, FF), (0.011 / NPARAM ** 0.5), 2.288818359375e-05, ((1, 32),), jnp.float32),
        "up_square": jnp.clip(jnp.exp(math.log(8.018721320626754e-13) - 2.0794415 * jax.random.uniform(key_of[15], (L, D, FF), jnp.float32) ** level_of(key_of[15], (L, D, FF), ((1, 32),), -0.2, 0.2)), 1.0023401650783442e-13, 8.018721320626754e-13),
        "down_proj": normal_values(key_of[16], (L, FF, D), FF ** -0.5, 0.109375, ((1, 32),), jnp.float32),
        "down_mean": normal_values(key_of[17], (L, FF, D), (0.011 / NPARAM ** 0.5), 2.288818359375e-05, ((1, 32),), jnp.float32),
        "down_square": jnp.clip(jnp.exp(math.log(8.018721320626754e-13) - 2.0794415 * jax.random.uniform(key_of[18], (L, FF, D), jnp.float32) ** level_of(key_of[18], (L, FF, D), ((1, 32),), -0.2, 0.2)), 1.0023401650783442e-13, 8.018721320626754e-13),
        "vectors": draw_vectors(jax.random.fold_in(key_of[25], 71), 0),
        "vec_mean": normal_values(key_of[20], (NVEC,), (0.044 / NPARAM ** 0.5), 9.1552734375e-05, (), jnp.float32),
        "vec_square": jnp.clip(jnp.exp(jax.random.uniform(key_of[21], (NVEC,), jnp.float32, math.log(1.6037442641253508e-12), math.log(1.2829954113002806e-11))), 1.6037442641253508e-12, 1.2829954113002806e-11),
        "pos_table": normal_values(key_of[22], (PATH, D), 0.3, 4.0, (), jnp.float32),
        "pos_mean": normal_values(key_of[23], (PATH, D), (0.011 / NPARAM ** 0.5), 2.288818359375e-05, (), jnp.float32),
        "pos_square": jnp.clip(jnp.exp(jax.random.uniform(key_of[24], (PATH, D), jnp.float32, math.log(1.0023401650783442e-13), math.log(8.018721320626754e-13))), 1.0023401650783442e-13, 8.018721320626754e-13),
    }


NORM_EPS = 1e-05
BETA_ONE = 0.9
BETA_TWO = 0.999
ADAM_EPS = 1e-08
LEARN_RATE = 0.1
RATE_VEC = 0.5
WEIGHT_DECAY = 0.1
CLIP_NORM = 0.1
HIGHEST = lax.Precision.HIGHEST

@jax.custom_vjp
def low(v):
    return lax.optimization_barrier(v.astype(jnp.bfloat16)).astype(jnp.float32)

@jax.custom_vjp
def low_back(v):
    return v

def low_keep(v):
    return (low(v), None)

def low_pass(kept, grad):
    return (grad,)

def back_keep(v):
    return (v, None)

def back_low(kept, grad):
    return (low(grad),)
low.defvjp(low_keep, low_pass)
low_back.defvjp(back_keep, back_low)

def low_both(value):
    return low(low_back(value))

def matmul(left, right):
    return jnp.dot(left, right, precision=HIGHEST)

def norm_apply(stream, gain, shift):
    center = stream - lax.optimization_barrier(jnp.mean(stream, -1, keepdims=True))
    spread = lax.optimization_barrier(jnp.mean(center * center, -1, keepdims=True))
    return center * lax.rsqrt(spread + NORM_EPS) * gain + shift

def split_layer(vector_row, model_width, head_size, hidden_width):
    widths = [model_width] * 3 + [head_size] + [model_width] * 3 + [hidden_width, model_width]
    pieces = []
    offset = 0
    for width in widths:
        pieces.append(vector_row[offset:offset + width])
        offset += width
    return pieces

def tree_layout(total, seg_len):
    places = jnp.arange(total, dtype=jnp.int32)
    trunk = 8 * seg_len
    beyond = jnp.maximum(places - trunk, 0) // seg_len
    segment = jnp.where(places < trunk, 0, 1 + beyond)
    offset = places - trunk - beyond * seg_len
    path_depth = jnp.where(places < trunk, places, jnp.where(segment <= 4, trunk + offset, trunk + seg_len + offset))
    return (places, segment.astype(jnp.int32), path_depth.astype(jnp.int32))

def tree_mask(parent_row, places, segment, count):
    labels = jnp.arange(count, dtype=jnp.int32)
    parent_hot = (parent_row[:, None] == labels[None, :]).astype(jnp.float32)
    grand_hot = jnp.dot(parent_hot, parent_hot, precision=HIGHEST)
    ancestor = jnp.eye(count, dtype=jnp.float32) + parent_hot + grand_hot
    seg_hot = (segment[:, None] == labels[None, :]).astype(jnp.float32)
    reach = jnp.dot(jnp.dot(seg_hot, ancestor, precision=HIGHEST), seg_hot.T, precision=HIGHEST)
    return (reach > 0.5) & (places[None, :] <= places[:, None])

def layer_apply(stream, wqkv, wout, wup, wdown, vector_row, allowed):
    model_width = stream.shape[1]
    head_size = (wqkv.shape[1] - model_width) // 2
    heads = model_width // head_size
    gain_one, shift_one, query_bias, value_bias, out_bias, gain_two, shift_two, up_bias, down_bias = split_layer(vector_row, model_width, head_size, wup.shape[1])
    normed = low(norm_apply(stream, gain_one, shift_one))
    mixed = matmul(normed, wqkv)
    queries = low_both(mixed[:, :model_width] + query_bias).reshape(-1, heads, head_size)
    keys_low = low_both(mixed[:, model_width:model_width + head_size])
    values_low = low_both(mixed[:, model_width + head_size:] + value_bias)
    scores = low_back(jnp.einsum('thd,sd->hts', queries, keys_low, precision=HIGHEST) * head_size ** (-0.5))
    scores = jnp.where(allowed[None], scores, -1e+30)
    probs = low(jnp.exp(scores - jax.nn.logsumexp(scores, -1, keepdims=True)))
    attended = low_both(jnp.einsum('hts,sd->thd', probs, values_low, precision=HIGHEST).reshape(-1, model_width))
    middle = stream + low_back(matmul(attended, wout) + out_bias)
    normed_two = low(norm_apply(middle, gain_two, shift_two))
    hidden = low_back(matmul(normed_two, wup) + up_bias)
    active = low(jax.nn.gelu(hidden, approximate=True))
    return middle + low_back(matmul(active, wdown) + down_bias)

def tree_loss(params, tree_ids, parent_row, slots, tree_targets):
    table, wqkv, wout, wup, wdown, vectors, pos_table = params
    model_width = table.shape[1]
    head_size = (wqkv.shape[2] - model_width) // 2
    layer_width = 7 * model_width + head_size + wup.shape[2]
    places, segment, path_depth = tree_layout(tree_ids.shape[0], SEG)
    allowed = tree_mask(parent_row, places, segment, NSEG)
    table_low = low(table)
    stream = low_back(table_low[tree_ids]) + pos_table[path_depth]
    for layer_index in range(L):
        stream = layer_apply(stream, low(wqkv[layer_index]), low(wout[layer_index]), low(wup[layer_index]), low(wdown[layer_index]), vectors[layer_index * layer_width:(layer_index + 1) * layer_width], allowed)
    final = vectors[L * layer_width:]
    finished = low(norm_apply(stream, final[:model_width], final[model_width:]))
    live = slots >= 0
    rows = jnp.where(live[:, None], finished[jnp.maximum(slots, 0)], 0.0)
    logits = low_back(matmul(rows, table_low.T))
    picked = jnp.take_along_axis(logits, tree_targets[:, None], 1)[:, 0]
    return jnp.sum(jnp.where(live, jax.nn.logsumexp(logits, -1) - picked, 0.0))

def adam_update(weight, mean, square, grad, rate):
    mean_new = BETA_ONE * mean + (1.0 - BETA_ONE) * grad
    square_new = BETA_TWO * square + (1.0 - BETA_TWO) * grad * grad
    mean_hat = mean_new / (1.0 - BETA_ONE ** STEP)
    square_hat = square_new / (1.0 - BETA_TWO ** STEP)
    weight_new = weight - rate * (mean_hat / (jnp.sqrt(square_hat) + ADAM_EPS) + WEIGHT_DECAY * weight)
    return (weight_new, mean_new, square_new)

def reference(token_ids, parents, comp_pos, targets, table, table_mean, table_square, qkv_proj, qkv_mean, qkv_square, out_proj, out_mean, out_square, up_proj, up_mean, up_square, down_proj, down_mean, down_square, vectors, vec_mean, vec_square, pos_table, pos_mean, pos_square):
    trees = parents.shape[0]
    tree_ids = token_ids.reshape(trees, -1)
    params = (table, qkv_proj, out_proj, up_proj, down_proj, vectors, pos_table)

    def total_loss(weights):

        def one_tree(carry, inputs):
            return (carry + jax.checkpoint(tree_loss)(weights, *inputs), None)
        result, ignored = lax.scan(one_tree, jnp.zeros((), jnp.float32), (tree_ids, parents, comp_pos, targets))
        return result
    loss_sum, pull = jax.vjp(total_loss, params)
    grads = pull(jnp.ones((), jnp.float32))[0]
    squares = jnp.zeros((), jnp.float32)
    for grad in grads:
        squares = squares + jnp.sum(grad * grad)
    grad_norm = jnp.sqrt(squares)
    factor = jnp.minimum(1.0, CLIP_NORM / grad_norm)
    loss_count = jnp.sum((comp_pos >= 0).astype(jnp.float32))
    states = ((table, table_mean, table_square), (qkv_proj, qkv_mean, qkv_square), (out_proj, out_mean, out_square), (up_proj, up_mean, up_square), (down_proj, down_mean, down_square), (vectors, vec_mean, vec_square), (pos_table, pos_mean, pos_square))
    results = [loss_sum, loss_count, grad_norm]
    for index_state in range(7):
        weight, mean, square = states[index_state]
        rate = RATE_VEC if index_state == 5 else LEARN_RATE
        results.extend(adam_update(weight, mean, square, grads[index_state] * factor, rate))
    return tuple(results)
```

```python
import functools

import jax
import jax.numpy as jnp
from jax import lax
from jax.experimental import pallas as pl
from jax.experimental.pallas import tpu as pltpu
from jax.sharding import PartitionSpec as P

L = 2
NSEG = 13
STEP = 10
SEG = 16


NORM_EPS = 1e-05
BETA_ONE = 0.9
BETA_TWO = 0.999
ADAM_EPS = 1e-08
LEARN_RATE = 0.1
RATE_VEC = 0.5
WEIGHT_DECAY = 0.1
CLIP_NORM = 0.1
HIGHEST = lax.Precision.HIGHEST
GELU_SCALE = 0.7978845608028654
GELU_CUBE = 0.044715
ALL = ("z", "core", "vocab")
CHIPS = ("z", "vocab")
ROWS_STEP = 2560
UNROLL = 16
HEAD_ROWS = 256
TURN = 512
MIB = 1024 * 1024


class Place:
    def __init__(self):
        self.nv = lax.axis_size("vocab")
        self.nz = lax.axis_size("z")
        self.count = self.nv * self.nz * 2
        self.v = lax.axis_index("vocab")
        self.z = lax.axis_index("z")
        self.c = lax.axis_index("core")
        self.where = jnp.stack([self.z, self.c, self.v]).astype(jnp.int32)
        self.bits = [1 << i for i in range(self.nv.bit_length() - 1)]

    def swap(self, a, v=0, c=0, z=0):
        mask = (z * 2 + c) * self.nv + v
        return lax.ppermute(a, ALL, [(i, i ^ mask) for i in range(self.count)])

    def gather_z(self, a):
        return jnp.stack([a] + [self.swap(a, z=m) for m in range(1, self.nz)])

    def gather_v(self, a):
        return jnp.stack([a] + [self.swap(a, v=m) for m in range(1, self.nv)])

    def gather_c(self, a):
        return jnp.stack([a, self.swap(a, c=1)])


def pick(a, index, axis):
    return lax.dynamic_index_in_dim(a, index, axis, False)


def tree_sum(terms):
    while len(terms) > 1:
        terms = [terms[i] + terms[i + 1] for i in range(0, len(terms), 2)]
    return terms[0]


def cost(moved):
    return pl.CostEstimate(flops=0, transcendentals=0, bytes_accessed=moved)


def put_kernel(slots, nv, where_ref, *refs):
    pieces, out = refs[: len(slots)], refs[-1]
    z, c = where_ref[0], where_ref[1]
    v = where_ref[2] if nv > 1 else 0
    for piece, (core, masks) in zip(pieces, slots):
        for k, mask in enumerate(masks):
            for m in range(piece.shape[1]):
                row = ((z ^ m) * 2 + (c ^ core)) * nv + (v ^ mask)
                out[row] = piece[k, m]


def put(place, pieces, slots, nv=None):
    nv = place.nv if nv is None else nv
    count = 2 * place.nz * nv
    rows, width = pieces[0].shape[2:]
    return pl.pallas_call(
        functools.partial(put_kernel, slots, nv),
        out_shape=jax.ShapeDtypeStruct((count, rows, width), pieces[0].dtype),
        in_specs=[pl.BlockSpec(memory_space=pltpu.SMEM)]
        + [pl.BlockSpec(memory_space=pltpu.VMEM)] * len(pieces),
        out_specs=pl.BlockSpec(memory_space=pltpu.VMEM),
        cost_estimate=cost(2 * count * rows * width * pieces[0].dtype.itemsize),
        compiler_params=pltpu.CompilerParams(vmem_limit_bytes=4 * count * rows * width + 4 * MIB),
    )(place.where, *pieces)


def owner_order(place, order):
    if order is None:
        index = jnp.arange(place.nz, dtype=jnp.int32)[:, None] * (2 * place.nv)
        index = index + place.c * place.nv + jnp.arange(place.nv, dtype=jnp.int32)
        return index.reshape(-1)
    index = jnp.zeros((), jnp.int32)
    for size, unit in [(2, place.nv)] + [(2, bit) for bit in order]:
        index = index[..., None] + jnp.arange(size, dtype=jnp.int32) * unit
    index = index[..., None] + jnp.arange(place.nz, dtype=jnp.int32) * (2 * place.nv)
    return index.reshape(-1) ^ ((place.z * 2 + place.c) * place.nv + place.v)


def order_hot(place, width, order):
    part = width // place.count
    columns = owner_order(place, order)[: place.count // 2, None] * part + jnp.arange(part, dtype=jnp.int32)
    return (
        jnp.arange(width, dtype=jnp.int32)[:, None] == columns.reshape(-1)[None, :]
    ).astype(jnp.bfloat16)


def pair_kernel(x_ref, other_ref, hot_ref, y_ref, y_other_ref, out_ref, left_ref, left_other_ref):
    @pl.when(pl.program_id(0) == 0)
    def _():
        hot = hot_ref[...]
        left_ref[...] = jnp.dot(x_ref[...], hot, preferred_element_type=jnp.float32).astype(
            jnp.bfloat16
        )
        left_other_ref[...] = jnp.dot(
            other_ref[...], hot, preferred_element_type=jnp.float32
        ).astype(jnp.bfloat16)

    out_ref[...] = (
        dot_first(left_ref[...], y_ref[...]) + dot_first(left_other_ref[...], y_other_ref[...])
    ).astype(jnp.bfloat16)


def pair_grad(place, x, y, hot):
    length, depth = x.shape
    rows, width = hot.shape[1], y.shape[1]
    block = 768 if width % 768 == 0 else width
    whole = pl.BlockSpec((length, depth), lambda i: (0, 0))
    part = pl.BlockSpec((length, block), lambda i: (0, i))
    return pl.pallas_call(
        pair_kernel,
        out_shape=jax.ShapeDtypeStruct((rows, width), jnp.bfloat16),
        grid=(width // block,),
        in_specs=[whole, whole, pl.BlockSpec((depth, rows), lambda i: (0, 0)), part, part],
        out_specs=pl.BlockSpec((rows, block), lambda i: (0, i)),
        scratch_shapes=[pltpu.VMEM((length, rows), jnp.bfloat16)] * 2,
        cost_estimate=pl.CostEstimate(
            flops=4 * length * rows * (width + depth),
            transcendentals=0,
            bytes_accessed=4 * length * (width + depth) + 2 * rows * width,
        ),
        compiler_params=pltpu.CompilerParams(vmem_limit_bytes=14 * MIB),
    )(x, place.swap(x, c=1), hot, y, place.swap(y, c=1))


def wide_kernel(nv, order, where_ref, x_ref, other_ref, y_ref, y_other_ref, out_ref):
    total = dot_first(x_ref[...], y_ref[...]) + dot_first(other_ref[...], y_other_ref[...])
    rows = total.shape[0] // nv
    if order is None:
        out_ref[0] = total.astype(jnp.bfloat16).reshape(out_ref.shape[1:])
        return
    for v in range(nv):
        apart = where_ref[2] ^ v
        position = 0
        for bit in order:
            position = position * 2 + jnp.where((apart & bit) != 0, 1, 0)
        out_ref[position, 0] = total[v * rows : (v + 1) * rows].astype(jnp.bfloat16)


def pair_grad_wide(place, x, y, order):
    length, depth = x.shape
    width = y.shape[1]
    block = depth // (2 * place.nz)
    rows = block // place.nv
    other = place.swap(x, c=1)
    if block % 128 == 0:
        part = pl.BlockSpec((length, block), lambda i, where: (0, 2 * i + where[1]))
    else:
        x, other = (a.reshape(length, -1, block).transpose(1, 0, 2) for a in (x, other))
        part = pl.BlockSpec((None, length, block), lambda i, where: (2 * i + where[1], 0, 0))
    whole = pl.BlockSpec((length, width), lambda i, where: (0, 0))
    shape, block_shape = (place.nv, place.nz, rows, width), (place.nv, 1, rows, width)
    where_out = lambda i, where: (0, i ^ where[0], 0, 0)
    if order is None:
        shape, block_shape = (place.nz, place.nv, rows, width), (1, place.nv, rows, width)
        where_out = lambda i, where: (i, 0, 0, 0)
    return pl.pallas_call(
        functools.partial(wide_kernel, place.nv, order),
        out_shape=jax.ShapeDtypeStruct(shape, jnp.bfloat16),
        grid_spec=pltpu.PrefetchScalarGridSpec(
            num_scalar_prefetch=1,
            grid=(place.nz,),
            in_specs=[part, part, whole, whole],
            out_specs=pl.BlockSpec(block_shape, where_out),
        ),
        cost_estimate=pl.CostEstimate(
            flops=2 * length * depth * width,
            transcendentals=0,
            bytes_accessed=4 * length * (depth + width) + depth * width,
        ),
        compiler_params=pltpu.CompilerParams(vmem_limit_bytes=14 * MIB),
    )(place.where, x, other, y, place.swap(y, c=1)).reshape(depth // 2, width)


class Reduced:
    def __init__(self, place, grad, order):
        self.place = place
        self.value = grad.reshape(-1, place.nz, grad.shape[0] // (place.nz * place.nv), grad.shape[1])
        self.order = list(order)

    def step(self):
        place, a = self.place, self.value
        if self.order:
            half = a.shape[0] // 2
            self.value = low_sum(a[:half], place.swap(a[half:], v=self.order.pop(0)))
        else:
            a = a[0]
            self.value = tree_sum(
                [a[0].astype(jnp.float32)]
                + [place.swap(a[m], z=m).astype(jnp.float32) for m in range(1, place.nz)]
            )

    def rest(self):
        while self.value.ndim > 2:
            self.step()
        return self.value


class Gathered:
    def __init__(self, place, shard, order):
        self.place = place
        self.shape = shard.shape
        self.order = list(order)
        self.masks = [0]
        self.value = shard
        self.pieces = None
        self.ready = False

    def step(self):
        place, held = self.place, self.value
        if held is not None and held.ndim == 2:
            self.value = place.gather_z(held)[None]
        elif self.order:
            bit = self.order.pop(0)
            got = place.swap(held, v=bit)
            got_masks = [m ^ bit for m in self.masks]
            if self.order:
                self.value = jnp.concatenate([held, got])
                self.masks = self.masks + got_masks
            else:
                self.pieces = [(held, 0, self.masks), (got, 0, got_masks)]
                self.value = got
        else:
            held = (self.pieces[0][0], self.value)
            pieces = [(a, 0, m) for a, (_, _, m) in zip(held, self.pieces)]
            pieces += [(place.swap(a, c=1), 1, m) for a, _, m in pieces]
            out = put(place, [a for a, _, _ in pieces], [(c, m) for _, c, m in pieces])
            self.value = out.reshape(place.count * self.shape[0], self.shape[1])
            self.ready = True

    def rest(self):
        while not self.ready:
            self.step()


def tie(main, *steps):
    main, values = lax.optimization_barrier((main, [s.value for s in steps]))
    for s, value in zip(steps, values):
        s.value = value
    return main


class Held:
    def __init__(self, value):
        self.value = value


def as_wide(a):
    return a.astype(jnp.float32)


def as_low(a):
    return a.astype(jnp.bfloat16)


def low_sum(kept, got):
    return (kept.astype(jnp.float32) + got.astype(jnp.float32)).astype(jnp.bfloat16)


def reduce_flat(place, vector, table):
    length = vector.shape[0]
    first = -(-length // 1024) * 8
    second = table.size // 128
    rows = -(-(first + second) // (place.count * 8)) * 8
    a = jnp.concatenate(
        [jnp.pad(vector, (0, first * 128 - length)).reshape(first, 128), table.reshape(second, 128)]
    )
    a = jnp.pad(a, ((0, place.count * rows - first - second), (0, 0)))
    a = a.reshape(place.nz, 2, place.nv, rows, 128)
    a = pick(a, place.c, 1) + place.swap(pick(a, 1 - place.c, 1), c=1)
    a = tree_sum(
        [pick(a, place.v, 1)]
        + [place.swap(pick(a, place.v ^ m, 1), v=m) for m in range(1, place.nv)]
    )
    return tree_sum(
        [pick(a, place.z, 0)]
        + [place.swap(pick(a, place.z ^ m, 0), z=m) for m in range(1, place.nz)]
    )


def gather_flat(place, own, scalars, vector, table):
    length, rows = vector.shape[0], own.shape[0]
    first, second = -(-length // 1024) * 8, table.size // 128
    own = jnp.concatenate([own, jnp.pad(scalars[None], ((0, 7), (0, 128 - scalars.shape[0])))])
    whole = gather_blocks(place, own)
    scalars = jnp.sum(whole[:, rows, : scalars.shape[0]], 0)
    whole = whole[:, :rows].reshape(-1, 128)
    return (
        scalars,
        whole[:first].reshape(-1)[:length],
        whole[first : first + second].reshape(table.shape),
    )


def gather_blocks(place, block):
    held = place.gather_v(place.gather_z(block))
    masks = list(range(place.nv))
    return put(place, [held, place.swap(held, c=1)], [(0, masks), (1, masks)])


def turned(value, axis):
    size = max(value.shape)
    same = lax.broadcasted_iota(jnp.int32, (size, size), 0) == lax.broadcasted_iota(
        jnp.int32, (size, size), 1
    )
    return jnp.sum(jnp.where(same, value, jnp.zeros((), value.dtype)), axis, keepdims=True)


def hits(first_ref, targets_ref, shape):
    column = turned(targets_ref[...], 1) - first_ref[0]
    return column == lax.broadcasted_iota(jnp.int32, shape, 1)


def logits_kernel(first_ref, rows_ref, table_ref, targets_ref, exps_ref, stats_ref):
    logits = jnp.dot(rows_ref[...], table_ref[...], preferred_element_type=jnp.float32)
    top = jnp.max(logits, 1, keepdims=True)
    exps = jnp.exp(logits - top)
    picked = jnp.where(hits(first_ref, targets_ref, logits.shape), logits, 0.0)
    exps_ref[...] = exps.astype(jnp.bfloat16)
    stats_ref[0:1, :] = turned(top, 0)
    stats_ref[1:2, :] = turned(jnp.sum(exps, 1, keepdims=True), 0)
    stats_ref[2:3, :] = turned(jnp.sum(picked, 1, keepdims=True), 0)


def head_forward(first, rows, table, targets):
    count, width = rows.shape
    size = table.shape[1]
    return pl.pallas_call(
        logits_kernel,
        out_shape=(
            jax.ShapeDtypeStruct((count, size), jnp.bfloat16),
            jax.ShapeDtypeStruct((3, count), jnp.float32),
        ),
        grid=(count // HEAD_ROWS,),
        in_specs=[
            pl.BlockSpec(memory_space=pltpu.SMEM),
            pl.BlockSpec((HEAD_ROWS, width), lambda i: (i, 0)),
            pl.BlockSpec((width, size), lambda i: (0, 0)),
            pl.BlockSpec((1, HEAD_ROWS), lambda i: (0, i)),
        ],
        out_specs=(
            pl.BlockSpec((HEAD_ROWS, size), lambda i: (i, 0)),
            pl.BlockSpec((3, HEAD_ROWS), lambda i: (0, i)),
        ),
        cost_estimate=pl.CostEstimate(
            flops=4 * count * width * size, transcendentals=count * size, bytes_accessed=4 * count * size
        ),
        compiler_params=pltpu.CompilerParams(vmem_limit_bytes=24 * MIB),
    )(first, rows, table, targets)


def slopes_kernel(first_ref, exps_ref, weight_ref, table_ref, targets_ref, slopes_ref, rows_ref):
    exps = exps_ref[...].astype(jnp.float32) * turned(weight_ref[...], 1)
    hit = hits(first_ref, targets_ref, exps.shape)
    slopes = (exps - jnp.where(hit, 1.0, 0.0)).astype(jnp.bfloat16)
    slopes_ref[...] = slopes
    rows_ref[...] = dot_last(slopes, table_ref[...]).astype(jnp.bfloat16)


def head_backward(first, exps, weight, table, targets):
    count, size = exps.shape
    width = table.shape[0]
    return pl.pallas_call(
        slopes_kernel,
        out_shape=(
            jax.ShapeDtypeStruct((count, size), jnp.bfloat16),
            jax.ShapeDtypeStruct((count, width), jnp.bfloat16),
        ),
        grid=(count // HEAD_ROWS,),
        in_specs=[
            pl.BlockSpec(memory_space=pltpu.SMEM),
            pl.BlockSpec((HEAD_ROWS, size), lambda i: (i, 0)),
            pl.BlockSpec((1, HEAD_ROWS), lambda i: (0, i)),
            pl.BlockSpec((width, size), lambda i: (0, 0)),
            pl.BlockSpec((1, HEAD_ROWS), lambda i: (0, i)),
        ],
        out_specs=(
            pl.BlockSpec((HEAD_ROWS, size), lambda i: (i, 0)),
            pl.BlockSpec((HEAD_ROWS, width), lambda i: (i, 0)),
        ),
        cost_estimate=pl.CostEstimate(
            flops=4 * count * width * size, transcendentals=0, bytes_accessed=6 * count * size
        ),
        compiler_params=pltpu.CompilerParams(vmem_limit_bytes=24 * MIB),
    )(first, exps, weight, table, targets)


def cut_kernel(where_ref, columns_ref, out_ref):
    out_ref[0, 0] = columns_ref[...].astype(out_ref.dtype)


def cut(place, columns):
    width, size = columns.shape
    part = size // (2 * place.nz)
    if part % 128:
        order = jnp.arange(2 * place.nz) ^ (place.z * 2 + place.c)
        parts = columns.astype(jnp.bfloat16).reshape(width, 2 * place.nz, part).transpose(1, 0, 2)
        return jnp.take(parts, order, axis=0).reshape(place.nz, 2, width, part)
    return pl.pallas_call(
        cut_kernel,
        out_shape=jax.ShapeDtypeStruct((place.nz, 2, width, part), jnp.bfloat16),
        grid_spec=pltpu.PrefetchScalarGridSpec(
            num_scalar_prefetch=1,
            grid=(2 * place.nz,),
            in_specs=[
                pl.BlockSpec((width, part), lambda i, where: (0, i ^ (where[0] * 2 + where[1])))
            ],
            out_specs=pl.BlockSpec((1, 1, width, part), lambda i, where: (i // 2, i % 2, 0, 0)),
        ),
        cost_estimate=cost(6 * width * size),
    )(place.where, columns)


def find_kernel(ids_ref, columns_ref, out_ref, rows_ref):
    size = columns_ref.shape[1]

    @pl.when(pl.program_id(0) == 0)
    def _():
        def turn(i, carry):
            at = pl.multiple_of(i * TURN, TURN)
            part = columns_ref[:, pl.ds(at, TURN)].astype(jnp.bfloat16).astype(jnp.float32)
            rows_ref[pl.ds(at, TURN), :] = part.T
            return carry

        lax.fori_loop(0, size // TURN, turn, 0)
        rows_ref[pl.ds(size, 8), :] = jnp.zeros((8, rows_ref.shape[1]), jnp.float32)

    first = pl.program_id(0) * out_ref.shape[0]

    def body(i, carry):
        for u in range(UNROLL):
            t = i * UNROLL + u
            out_ref[pl.ds(t, 1), :] = rows_ref[pl.ds(ids_ref[first + t], 1), :]
        return carry

    lax.fori_loop(0, out_ref.shape[0] // UNROLL, body, 0)


def find_rows(ids, columns):
    width, size = columns.shape
    return pl.pallas_call(
        find_kernel,
        out_shape=jax.ShapeDtypeStruct((ids.shape[0], width), jnp.float32),
        grid_spec=pltpu.PrefetchScalarGridSpec(
            num_scalar_prefetch=1,
            grid=(ids.shape[0] // ROWS_STEP,),
            in_specs=[pl.BlockSpec(memory_space=pltpu.VMEM)],
            out_specs=pl.BlockSpec((ROWS_STEP, width), lambda i, ids: (i, 0)),
            scratch_shapes=[pltpu.VMEM((size + 8, width), jnp.float32)],
        ),
        cost_estimate=cost(ids.shape[0] * 7000),
        compiler_params=pltpu.CompilerParams(vmem_limit_bytes=24 * MIB),
    )(ids, columns)


def add_kernel(ids_ref, rows_ref, head_ref, out_ref, *parts):
    step = pl.program_id(0)
    first = step * rows_ref.shape[0]
    size = out_ref.shape[1]

    @pl.when(step == 0)
    def _():
        for part in parts:
            part[...] = jnp.zeros_like(part)

    def body(i, carry):
        for u in range(UNROLL):
            t = i * UNROLL + u
            part = parts[u % len(parts)]
            where = pl.ds(ids_ref[first + t], 1)
            part[where, :] = part[where, :] + rows_ref[pl.ds(t, 1), :]
        return carry

    lax.fori_loop(0, rows_ref.shape[0] // UNROLL, body, 0)

    @pl.when(step == pl.num_programs(0) - 1)
    def _():
        def turn(i, carry):
            at = pl.ds(pl.multiple_of(i * TURN, TURN), TURN)
            total = tree_sum([part[at, :] for part in parts])
            part = head_ref.shape[2]
            head = head_ref[i * TURN // part, :, pl.ds(pl.multiple_of(i * TURN % part, TURN), TURN)]
            out_ref[:, at] = total.T + head.astype(jnp.float32)
            return carry

        lax.fori_loop(0, size // TURN, turn, 0)


def add_rows(ids, rows, head):
    width, size = head.shape[1], head.shape[0] * head.shape[2]
    if head.shape[2] % TURN:
        head = head.transpose(1, 0, 2).reshape(1, width, size)
    return pl.pallas_call(
        add_kernel,
        out_shape=jax.ShapeDtypeStruct((width, size), jnp.float32),
        grid_spec=pltpu.PrefetchScalarGridSpec(
            num_scalar_prefetch=1,
            grid=(ids.shape[0] // ROWS_STEP,),
            in_specs=[
                pl.BlockSpec((ROWS_STEP, width), lambda i, ids: (i, 0)),
                pl.BlockSpec(memory_space=pltpu.VMEM),
            ],
            out_specs=pl.BlockSpec(memory_space=pltpu.VMEM),
            scratch_shapes=[pltpu.VMEM((size + 8, width), jnp.float32)] * 4,
        ),
        cost_estimate=cost(ids.shape[0] * 8000),
        compiler_params=pltpu.CompilerParams(vmem_limit_bytes=40 * MIB),
    )(ids, rows, head)


def norm_apply(stream, gain, shift):
    center = stream - jnp.mean(stream, -1, keepdims=True)
    spread = jnp.mean(center * center, -1, keepdims=True)
    return center * lax.rsqrt(spread + NORM_EPS) * gain + shift


def norm_back(stream, gain, grad):
    center = stream - jnp.mean(stream, -1, keepdims=True)
    scale = lax.rsqrt(jnp.mean(center * center, -1, keepdims=True) + NORM_EPS)
    unit = center * scale
    inner = grad * gain
    part = inner - jnp.mean(inner, -1, keepdims=True)
    part = scale * (part - unit * jnp.mean(inner * unit, -1, keepdims=True))
    return part, jnp.sum(grad * unit, 0, keepdims=True), jnp.sum(grad, 0, keepdims=True)


def gelu_parts(value):
    inner = GELU_SCALE * (value + GELU_CUBE * value * value * value)
    bend = jnp.tanh(inner)
    half = 0.5 * (1.0 + bend)
    slope = GELU_SCALE * (1.0 + 3.0 * GELU_CUBE * value * value)
    return value * half, half + 0.5 * value * (1.0 - bend * bend) * slope


def split_layer(vector_row, model_width, head_size, hidden_width):
    widths = [model_width] * 3 + [head_size] + [model_width] * 3 + [hidden_width, model_width]
    pieces = []
    offset = 0
    for width in widths:
        pieces.append(vector_row[offset : offset + width])
        offset += width
    return pieces


def tree_layout(total, seg_len):
    places = jnp.arange(total, dtype=jnp.int32)
    trunk = 8 * seg_len
    beyond = jnp.maximum(places - trunk, 0) // seg_len
    segment = jnp.where(places < trunk, 0, 1 + beyond)
    offset = places - trunk - beyond * seg_len
    path_depth = jnp.where(
        places < trunk, places, jnp.where(segment <= 4, trunk + offset, trunk + seg_len + offset)
    )
    return (places, segment, path_depth)


def tree_mask(parent_row, places, segment, count):
    labels = jnp.arange(count, dtype=jnp.int32)
    parent_hot = (parent_row[:, None] == labels[None, :]).astype(jnp.float32)
    grand_hot = jnp.dot(parent_hot, parent_hot, precision=HIGHEST)
    ancestor = jnp.eye(count, dtype=jnp.float32) + parent_hot + grand_hot
    seg_hot = (segment[:, None] == labels[None, :]).astype(jnp.float32)
    reach = jnp.dot(jnp.dot(seg_hot, ancestor, precision=HIGHEST), seg_hot.T, precision=HIGHEST)
    return (reach > 0.5) & (places[None, :] <= places[:, None])


def dot_first(left, right):
    return lax.dot_general(
        left, right, (((0,), (0,)), ((), ())), preferred_element_type=jnp.float32
    )


def dot_last(left, right):
    return lax.dot_general(
        left, right, (((1,), (1,)), ((), ())), preferred_element_type=jnp.float32
    )


def column_sum(grad_low):
    return jnp.sum(grad_low.astype(jnp.float32), 0)


def fetch(copies):
    for copy in copies:
        copy.start()
    return copies


def head_probs(mixed_ref, bias, h, keys, size, model_width):
    queries = mixed_ref[:, h * size : (h + 1) * size]
    scores = dot_last(keys, queries) * size ** (-0.5) + bias
    exps = jnp.exp(scores - jnp.max(scores, 0, keepdims=True))
    return queries, exps * (1.0 / jnp.sum(exps, 0, keepdims=True))


def forward_kernel(
    stream_ref,
    row_ref,
    bias_ref,
    wide_ref,
    down_ref,
    result_ref,
    normed_ref,
    mixed_ref,
    attended_ref,
    middle_ref,
    normed_two_ref,
    hidden_ref,
    active_ref,
    qkv_low,
    out_low,
    up_low,
    down_low,
    sems,
):
    model_width = stream_ref.shape[1]
    size = (qkv_low.shape[1] - model_width) // 2
    cuts = (qkv_low.shape[1], qkv_low.shape[1] + model_width)
    copies = fetch(
        [
            pltpu.make_async_copy(wide_ref.at[:, : cuts[0]], qkv_low, sems.at[0]),
            pltpu.make_async_copy(wide_ref.at[:, cuts[0] : cuts[1]], out_low, sems.at[1]),
            pltpu.make_async_copy(wide_ref.at[:, cuts[1] :], up_low, sems.at[2]),
            pltpu.make_async_copy(down_ref, down_low, sems.at[3]),
        ]
    )

    def row(k, width=model_width):
        return row_ref[k : k + 1, :width]

    stream = stream_ref[...]
    normed = norm_apply(stream, row(0), row(1)).astype(jnp.bfloat16)
    normed_ref[...] = normed
    copies[0].wait()
    mixed = jnp.dot(normed, qkv_low[...], preferred_element_type=jnp.float32)
    mixed = (mixed + row(9, mixed.shape[1])).astype(jnp.bfloat16)
    mixed_ref[...] = mixed
    keys, values = mixed[:, model_width : model_width + size], mixed[:, model_width + size :]
    for h in range(model_width // size):
        ignored, probs = head_probs(mixed_ref, bias_ref[...], h, keys, size, model_width)
        attended_ref[:, h * size : (h + 1) * size] = dot_first(
            probs.astype(jnp.bfloat16), values
        ).astype(jnp.bfloat16)
    copies[1].wait()
    middle = stream + jnp.dot(
        attended_ref[...], out_low[...], preferred_element_type=jnp.float32
    )
    middle = middle + row(4)
    middle_ref[...] = middle
    normed_two = norm_apply(middle, row(5), row(6)).astype(jnp.bfloat16)
    normed_two_ref[...] = normed_two
    copies[2].wait()
    copies[3].wait()
    total = middle + row(8)
    for k in range(up_low.shape[1] // model_width):
        at = slice(k * model_width, (k + 1) * model_width)
        hidden = jnp.dot(normed_two, up_low[:, at], preferred_element_type=jnp.float32)
        hidden = hidden + row_ref[7:8, at]
        hidden_ref[:, at] = hidden
        active = gelu_parts(hidden)[0].astype(jnp.bfloat16)
        active_ref[:, at] = active
        total = total + jnp.dot(active, down_low[at, :], preferred_element_type=jnp.float32)
    result_ref[...] = total


def shape_of(shape, kind):
    return jax.ShapeDtypeStruct(shape, kind)


VMEM = pl.BlockSpec(memory_space=pltpu.VMEM)
ANY = pl.BlockSpec(memory_space=pl.ANY)


def layer_forward(stream, row, bias, wide, down):
    length, model_width = stream.shape
    hidden_width = down.shape[0]
    mixed_width = wide.shape[1] - model_width - hidden_width
    f32, low = jnp.float32, jnp.bfloat16
    return pl.pallas_call(
        forward_kernel,
        out_shape=(
            shape_of((length, model_width), f32),
            shape_of((length, model_width), low),
            shape_of((length, mixed_width), low),
            shape_of((length, model_width), low),
            shape_of((length, model_width), f32),
            shape_of((length, model_width), low),
            shape_of((length, hidden_width), f32),
            shape_of((length, hidden_width), low),
        ),
        in_specs=[VMEM, VMEM, VMEM, ANY, ANY],
        out_specs=(VMEM,) * 8,
        scratch_shapes=[
            pltpu.VMEM((model_width, mixed_width), low),
            pltpu.VMEM((model_width, model_width), low),
            pltpu.VMEM((model_width, hidden_width), low),
            pltpu.VMEM((hidden_width, model_width), low),
            pltpu.SemaphoreType.DMA((4,)),
        ],
        cost_estimate=cost(8 * MIB),
        compiler_params=pltpu.CompilerParams(vmem_limit_bytes=36 * MIB),
    )(stream, row, bias, wide, down)


def mlp_kernel(
    grad_ref,
    middle_ref,
    hidden_ref,
    row_ref,
    wide_ref,
    down_ref,
    middle_grad_ref,
    branch_ref,
    hidden_grad_ref,
    vector_ref,
    up_low,
    down_low,
    sems,
):
    model_width = grad_ref.shape[1]
    start = wide_ref.shape[1] - up_low.shape[1]
    copies = fetch(
        [
            pltpu.make_async_copy(down_ref, down_low, sems.at[0]),
            pltpu.make_async_copy(wide_ref.at[:, start:], up_low, sems.at[1]),
        ]
    )
    grad = grad_ref[...]
    branch = grad.astype(jnp.bfloat16)
    branch_ref[...] = branch
    vector_ref[...] = jnp.zeros_like(vector_ref)
    vector_ref[3:4, :model_width] = jnp.sum(branch.astype(jnp.float32), 0, keepdims=True)
    copies[0].wait()
    copies[1].wait()
    total = jnp.zeros_like(grad)
    for k in range(up_low.shape[1] // model_width):
        at = slice(k * model_width, (k + 1) * model_width)
        slope = gelu_parts(hidden_ref[:, at])[1]
        hidden_grad = (slope * dot_last(branch, down_low[at, :])).astype(jnp.bfloat16)
        hidden_grad_ref[:, at] = hidden_grad
        vector_ref[2:3, at] = jnp.sum(hidden_grad.astype(jnp.float32), 0, keepdims=True)
        total = total + dot_last(hidden_grad, up_low[:, at])
    part, gain_grad, shift_grad = norm_back(middle_ref[...], row_ref[5:6, :model_width], total)
    vector_ref[0:1, :model_width] = gain_grad
    vector_ref[1:2, :model_width] = shift_grad
    middle_grad_ref[...] = grad + part


def mlp_backward(grad, middle, hidden, row, wide, down):
    length, model_width = grad.shape
    hidden_width = down.shape[0]
    f32, low = jnp.float32, jnp.bfloat16
    return pl.pallas_call(
        mlp_kernel,
        out_shape=(
            shape_of((length, model_width), f32),
            shape_of((length, model_width), low),
            shape_of((length, hidden_width), low),
            shape_of((8, hidden_width), f32),
        ),
        in_specs=[VMEM, VMEM, VMEM, VMEM, ANY, ANY],
        out_specs=(VMEM,) * 4,
        scratch_shapes=[
            pltpu.VMEM((model_width, hidden_width), low),
            pltpu.VMEM((hidden_width, model_width), low),
            pltpu.SemaphoreType.DMA((2,)),
        ],
        cost_estimate=cost(4 * MIB),
        compiler_params=pltpu.CompilerParams(vmem_limit_bytes=32 * MIB),
    )(grad, middle, hidden, row, wide, down)


def attn_kernel(
    middle_grad_ref,
    stream_ref,
    mixed_ref,
    row_ref,
    bias_ref,
    wide_ref,
    stream_grad_ref,
    out_grad_ref,
    mixed_grad_ref,
    vector_ref,
    qkv_low,
    out_low,
    attended_ref,
    sems,
):
    model_width = stream_ref.shape[1]
    size = (qkv_low.shape[1] - model_width) // 2
    cut = qkv_low.shape[1]
    copies = fetch(
        [
            pltpu.make_async_copy(wide_ref.at[:, cut : cut + model_width], out_low, sems.at[0]),
            pltpu.make_async_copy(wide_ref.at[:, :cut], qkv_low, sems.at[1]),
        ]
    )
    middle_grad = middle_grad_ref[...]
    out_grad = middle_grad.astype(jnp.bfloat16)
    out_grad_ref[...] = out_grad
    vector_ref[...] = jnp.zeros_like(vector_ref)
    vector_ref[3:4, :model_width] = jnp.sum(out_grad.astype(jnp.float32), 0, keepdims=True)
    copies[0].wait()
    attended_ref[...] = dot_last(out_grad, out_low[...]).astype(jnp.bfloat16)
    keys = mixed_ref[:, model_width : model_width + size]
    values = mixed_ref[:, model_width + size :]
    keys_grad = jnp.zeros(keys.shape, jnp.float32)
    values_grad = jnp.zeros(values.shape, jnp.float32)
    for h in range(model_width // size):
        at = slice(h * size, (h + 1) * size)
        queries, probs = head_probs(mixed_ref, bias_ref[...], h, keys, size, model_width)
        grad = attended_ref[:, at]
        values_grad = values_grad + jnp.dot(
            probs.astype(jnp.bfloat16), grad, preferred_element_type=jnp.float32
        )
        probs_grad = dot_last(values, grad)
        scores_grad = probs * (probs_grad - jnp.sum(probs * probs_grad, 0, keepdims=True))
        scores_grad = scores_grad.astype(jnp.bfloat16)
        keys_grad = keys_grad + jnp.dot(
            scores_grad, queries, preferred_element_type=jnp.float32
        )
        mixed_grad_ref[:, at] = (dot_first(scores_grad, keys) * size ** (-0.5)).astype(jnp.bfloat16)
    mixed_grad_ref[:, model_width : model_width + size] = (keys_grad * size ** (-0.5)).astype(
        jnp.bfloat16
    )
    mixed_grad_ref[:, model_width + size :] = values_grad.astype(jnp.bfloat16)
    mixed_grad = mixed_grad_ref[...]
    vector_ref[2:3, :] = jnp.sum(mixed_grad.astype(jnp.float32), 0, keepdims=True)
    copies[1].wait()
    total = dot_last(mixed_grad, qkv_low[...])
    part, gain_grad, shift_grad = norm_back(stream_ref[...], row_ref[0:1, :model_width], total)
    vector_ref[0:1, :model_width] = gain_grad
    vector_ref[1:2, :model_width] = shift_grad
    stream_grad_ref[...] = middle_grad + part


def attn_backward(middle_grad, stream, mixed, row, bias, wide):
    length, model_width = stream.shape
    mixed_width = mixed.shape[1]
    f32, low = jnp.float32, jnp.bfloat16
    return pl.pallas_call(
        attn_kernel,
        out_shape=(
            shape_of((length, model_width), f32),
            shape_of((length, model_width), low),
            shape_of((length, mixed_width), low),
            shape_of((8, mixed_width), f32),
        ),
        in_specs=[VMEM, VMEM, VMEM, VMEM, VMEM, ANY],
        out_specs=(VMEM,) * 4,
        scratch_shapes=[
            pltpu.VMEM((model_width, mixed_width), low),
            pltpu.VMEM((model_width, model_width), low),
            pltpu.VMEM((length, model_width), low),
            pltpu.SemaphoreType.DMA((2,)),
        ],
        cost_estimate=cost(4 * MIB),
        compiler_params=pltpu.CompilerParams(vmem_limit_bytes=24 * MIB),
    )(middle_grad, stream, mixed, row, bias, wide)


def adam_update(weight, mean, square, grad, rate):
    mean_new = BETA_ONE * mean + (1.0 - BETA_ONE) * grad
    square_new = BETA_TWO * square + (1.0 - BETA_TWO) * grad * grad
    mean_hat = mean_new / (1.0 - BETA_ONE**STEP)
    square_hat = square_new / (1.0 - BETA_TWO**STEP)
    weight_new = weight - rate * (
        mean_hat / (jnp.sqrt(square_hat) + ADAM_EPS) + WEIGHT_DECAY * weight
    )
    return (weight_new, mean_new, square_new)


def per_device(
    token_ids,
    parents,
    comp_pos,
    targets,
    table,
    table_mean,
    table_square,
    qkv_proj,
    qkv_mean,
    qkv_square,
    out_proj,
    out_mean,
    out_square,
    up_proj,
    up_mean,
    up_square,
    down_proj,
    down_mean,
    down_square,
    vectors,
    vec_mean,
    vec_square,
    pos_table,
    pos_mean,
    pos_square,
):
    place = Place()
    nv, nz = place.nv, place.nz
    length = token_ids.shape[0]
    model_width = pos_table.shape[1]
    head_size = (qkv_proj.shape[2] - model_width) // 2
    layer_width = 7 * model_width + head_size + up_proj.shape[2]
    slot_count = comp_pos.shape[1]
    shard_size, own_width = table.shape
    slice_size = shard_size // (2 * nz)
    bits = place.bits
    orders = (bits, list(reversed(bits)))

    own_slots = comp_pos[0]
    live = own_slots >= 0
    cut_one, cut_two = qkv_proj.shape[2], qkv_proj.shape[2] + out_proj.shape[2]
    cut_three = cut_two + up_proj.shape[2]
    shard_rows = qkv_proj.shape[1]
    ranks = down_proj.shape[1] // shard_rows

    def wide_shard(i):
        return jnp.concatenate([qkv_proj[i], out_proj[i], up_proj[i]], 1).astype(jnp.bfloat16)

    down_low = down_proj.astype(jnp.bfloat16)
    first_layer = [
        lax.all_gather(shard, ALL, axis=0, tiled=True) for shard in (wide_shard(0), down_low[0])
    ]
    gathers = [Gathered(place, wide_shard(1), orders[0]), Gathered(place, down_low[1], orders[1])]
    meta = jnp.concatenate([token_ids, jnp.where(live, targets[0], -1)])
    meta = place.gather_v(place.gather_z(place.gather_c(meta)))
    for g in gathers:
        g.step()
    parts = cut(place, table.T)
    parts = Held([parts[0]] + [place.swap(parts[m], z=m) for m in range(1, nz)])

    masks = list(range(nv))
    all_targets = put(
        place, [meta[:, :, :1, length:], meta[:, :, 1:, length:]], [(0, masks), (1, masks)]
    ).reshape(1, -1)
    meta = meta.transpose(2, 0, 1, 3)
    all_ids = meta[..., :length].reshape(-1)
    local_ids = all_ids - place.v * shard_size
    inside = (local_ids >= 0) & (local_ids < shard_size)
    safe_ids = jnp.where(inside, local_ids, shard_size)
    found = find_rows(safe_ids, table.T).astype(jnp.bfloat16)
    found = tie(found, *gathers)
    for g in gathers:
        g.step()
    found = found.reshape(2, nv, nz, length, own_width)
    found = tree_sum(
        [found[:, 0]] + [place.swap(found[:, m], v=m) for m in range(1, nv)]
    )
    found = jnp.stack([found[0], place.swap(found[1], c=1)], 1)
    found = jnp.stack([found[0]] + [place.swap(found[m], z=m) for m in range(1, nz)])
    blocks = jnp.arange(2 * nz, dtype=jnp.int32) ^ (place.z * 2 + place.c)
    columns = (blocks[:, None] * own_width + jnp.arange(own_width, dtype=jnp.int32)).reshape(-1)
    column_hot = (
        columns[:, None] == jnp.arange(model_width, dtype=jnp.int32)[None, :]
    ).astype(jnp.bfloat16)
    embedded = jnp.dot(
        found.transpose(2, 0, 1, 3).reshape(length, model_width),
        column_hot,
        preferred_element_type=jnp.float32,
    )
    embedded = tie(embedded, *gathers)
    for g in gathers:
        g.step()

    places, segment, path_depth = tree_layout(length, SEG)
    allowed = tree_mask(parents[0], places, segment, NSEG)
    trunk = 8 * SEG
    pos_rows = jnp.concatenate(
        [
            pos_table[:trunk],
            jnp.tile(pos_table[trunk : trunk + SEG], (4, 1)),
            jnp.tile(pos_table[trunk + SEG :], (8, 1)),
        ]
    )
    stream = embedded + pos_rows
    bias = jnp.where(allowed, 0.0, -1e30).T
    layer_rows = []
    for layer_index in range(L):
        pieces = split_layer(
            vectors[layer_index * layer_width : (layer_index + 1) * layer_width],
            model_width,
            head_size,
            up_proj.shape[2],
        )
        pieces.append(
            jnp.concatenate([pieces[2], jnp.zeros((head_size,), jnp.float32), pieces[3]])
        )
        layer_rows.append(
            jnp.stack([jnp.pad(p, (0, up_proj.shape[2] - p.shape[0])) for p in pieces])
        )
    inputs_kept = []
    matrices = []
    for layer_index in range(L):
        wide, wdown = first_layer if layer_index == 0 else (g.value for g in gathers)
        matrices.append((wide, wdown))
        result, *saved = layer_forward(stream, layer_rows[layer_index], bias, wide, wdown)
        inputs_kept.append((stream, saved))
        stream = result
        if layer_index == 0:
            stream = tie(stream, parts, *gathers)
            for g in gathers:
                g.rest()
            mine = jnp.stack([p[0] for p in parts.value])
            theirs = place.swap(jnp.stack([p[1] for p in parts.value]), c=1)
            slice_low = put(place, [mine[None], theirs[None]], [(0, [0]), (1, [0])], 1)
            slice_low = Held(slice_low.reshape(model_width, slice_size))
            stream = tie(stream, slice_low)
    slice_low = slice_low.value
    final_gain = vectors[L * layer_width : L * layer_width + model_width]
    final_shift = vectors[L * layer_width + model_width :]
    finished = norm_apply(stream, final_gain, final_shift).astype(jnp.bfloat16)
    slot_hot = own_slots[:, None] == jnp.arange(length, dtype=jnp.int32)[None, :]
    rows = jnp.dot(
        slot_hot.astype(jnp.bfloat16), finished, preferred_element_type=jnp.float32
    ).astype(jnp.bfloat16)

    group_rows = gather_blocks(place, rows).reshape(-1, model_width)
    first_entry = place.v * shard_size + (place.z * 2 + place.c) * slice_size
    first_entry = first_entry.astype(jnp.int32).reshape(1)
    exps, stats = head_forward(first_entry, group_rows, slice_low, all_targets)

    def combine(parts):
        top = functools.reduce(jnp.maximum, [p[0] for p in parts])
        return jnp.stack([top, tree_sum([p[1] * jnp.exp(p[0] - top) for p in parts])])

    whole = stats[:2]
    whole = combine([whole, place.swap(whole, c=1)])
    whole = combine([whole] + [place.swap(whole, v=m) for m in range(1, nv)])
    whole = combine([whole] + [place.swap(whole, z=m) for m in range(1, nz)])
    log_total = whole[0] + jnp.log(whole[1])
    weight = jnp.where(all_targets[0] >= 0, jnp.exp(stats[0] - log_total), 0.0)
    own_total = lax.dynamic_slice_in_dim(
        log_total, ((place.z * 2 + place.c) * nv + place.v) * slot_count, slot_count
    )
    loss_local = jnp.sum(jnp.where(live, own_total, 0.0)) - jnp.sum(stats[2])
    count_local = jnp.sum(live.astype(jnp.float32))
    logits_low, rows_part = head_backward(
        first_entry, exps, weight[None], slice_low, all_targets
    )
    rows_part = Held(rows_part)
    logits_low = tie(logits_low, rows_part)
    head_grad = dot_first(group_rows, logits_low).astype(jnp.bfloat16)
    head_grad = head_grad.reshape(nz, 2, own_width, slice_size)
    head_parts = Held(
        [pick(head_grad, place.z, 0)]
        + [place.swap(pick(head_grad, place.z ^ m, 0), z=m) for m in range(1, nz)]
    )
    rows_part = rows_part.value.reshape(nz, 2, nv, slot_count, model_width)
    rows_part = as_wide(pick(rows_part, place.c, 1)) + as_wide(
        place.swap(pick(rows_part, 1 - place.c, 1), c=1)
    )
    rows_part = tree_sum(
        [pick(rows_part, place.v, 1)]
        + [as_wide(place.swap(as_low(pick(rows_part, place.v ^ m, 1)), v=m)) for m in range(1, nv)]
    )
    rows_grad = tree_sum(
        [pick(rows_part, place.z, 0)]
        + [as_wide(place.swap(as_low(pick(rows_part, place.z ^ m, 0)), z=m)) for m in range(1, nz)]
    )
    finished_grad = lax.dot_general(
        slot_hot.astype(jnp.float32),
        rows_grad,
        (((0,), (0,)), ((), ())),
        precision=HIGHEST,
        preferred_element_type=jnp.float32,
    )

    ignored, final_pull = jax.vjp(norm_apply, stream, final_gain, final_shift)
    stream_grad, grad_final_gain, grad_final_shift = final_pull(finished_grad)
    hots = [order_hot(place, model_width, order) for order in orders]
    plain_hot = order_hot(place, model_width, None)
    vector_grads = [None] * L

    def slabs(grad):
        grad = grad.reshape(nz * nv, ranks, shard_rows, model_width)
        return [grad[:, k].reshape(nz * nv * shard_rows, model_width) for k in range(ranks)]

    def unslab(columns):
        return jnp.concatenate(
            [columns[:, k * model_width : (k + 1) * model_width] for k in range(ranks)]
        )

    passing = None
    for layer_index in reversed(range(L)):
        kept_stream, saved = inputs_kept[layer_index]
        wide, wdown = matrices[layer_index]
        normed, mixed, attended, middle, normed_two, hidden, active = saved
        middle_grad, branch_grad, hidden_grad, late_vectors = mlp_backward(
            stream_grad, middle, hidden, layer_rows[layer_index], wide, wdown
        )
        if layer_index == 1:
            g_up = pair_grad(place, normed_two, hidden_grad, plain_hot)
            g_down = slabs(pair_grad_wide(place, active, branch_grad, None))
            both = Held(jnp.concatenate([g_up] + g_down, 1))
            middle_grad = tie(middle_grad, both)
            upper = lax.psum_scatter(both.value, CHIPS, scatter_dimension=0, tiled=True)
        else:
            g_down = slabs(pair_grad_wide(place, active, branch_grad, orders[0]))
            early = Reduced(place, jnp.concatenate(g_down + [passing], 1), orders[0])
            g_up = Held(pair_grad(place, normed_two, hidden_grad, hots[1]))
            middle_grad = tie(middle_grad, early, g_up)
            early.step()
        stream_grad, out_grad, mixed_grad, early_vectors = attn_backward(
            middle_grad, kept_stream, mixed, layer_rows[layer_index], bias, wide
        )
        hot = hots[1 - layer_index]
        g_attn = jnp.concatenate(
            [pair_grad(place, normed, mixed_grad, hot), pair_grad(place, attended, out_grad, hot)], 1
        )
        vector_grads[layer_index] = jnp.concatenate(
            [
                early_vectors[0, :model_width],
                early_vectors[1, :model_width],
                early_vectors[2, :model_width],
                early_vectors[2, model_width + head_size :],
                early_vectors[3, :model_width],
                late_vectors[0, :model_width],
                late_vectors[1, :model_width],
                late_vectors[2],
                late_vectors[3, :model_width],
            ]
        )
        if layer_index == 1:
            passing = Held(g_attn)
            stream_grad = tie(stream_grad, passing, head_parts)
            passing = passing.value
            mine = jnp.stack([pick(p, place.c, 0) for p in head_parts.value])
            theirs = place.swap(jnp.stack([pick(p, 1 - place.c, 0) for p in head_parts.value]), c=1)
            head_grad = put(place, [mine[None], theirs[None]], [(0, [0]), (1, [0])], 1)
        else:
            late = Reduced(place, jnp.concatenate([g_up.value, g_attn], 1), orders[1])
            stream_grad = tie(stream_grad, early, late)
            early.step()
            late.step()

    embedded_grad = lax.dot_general(
        stream_grad.astype(jnp.bfloat16),
        column_hot,
        (((1,), (1,)), ((), ())),
        preferred_element_type=jnp.float32,
    ).astype(jnp.bfloat16)
    sent = embedded_grad.reshape(length, nz, 2, own_width).transpose(1, 2, 0, 3)
    sent = jnp.stack([sent[0]] + [place.swap(sent[m], z=m) for m in range(1, nz)])
    pos_grad = jnp.concatenate(
        [
            stream_grad[:trunk],
            jnp.sum(stream_grad[trunk : trunk + 4 * SEG].reshape(4, SEG, model_width), 0),
            jnp.sum(stream_grad[trunk + 4 * SEG :].reshape(8, SEG, model_width), 0),
        ]
    )
    vector_grad = jnp.concatenate(vector_grads + [grad_final_gain, grad_final_shift])
    flat_own = Held(reduce_flat(place, vector_grad, pos_grad))
    sent = tie(sent, early, late, flat_own)
    early.rest()
    late.step()
    sent = jnp.stack([sent[:, 0], place.swap(sent[:, 1], c=1)])
    sent = place.gather_v(sent)
    sent = tie(sent, late)
    late.rest()
    sent = sent.transpose(1, 0, 2, 3, 4).reshape(-1, own_width).astype(jnp.float32)
    table_grad = add_rows(safe_ids, sent, head_grad)
    early, late, upper = early.value, late.value, upper.astype(jnp.float32)
    down_end = ranks * model_width
    up_end = up_proj.shape[2]
    attn = [late[:, up_end:], early[:, down_end:]]
    grad_qkv = jnp.stack([a[:, :cut_one] for a in attn])
    grad_out = jnp.stack([a[:, cut_one:] for a in attn])
    grad_up = jnp.stack([late[:, :up_end], upper[:, :up_end]])
    grad_down = jnp.stack([unslab(early[:, :down_end]), unslab(upper[:, up_end:])])
    owned_squares = (
        jnp.sum(grad_qkv * grad_qkv)
        + jnp.sum(grad_out * grad_out)
        + jnp.sum(grad_up * grad_up)
        + jnp.sum(grad_down * grad_down)
        + jnp.sum(table_grad * table_grad)
        + jnp.sum(flat_own.value * flat_own.value)
    )
    sums, vector_grad, pos_grad = gather_flat(
        place,
        flat_own.value,
        jnp.stack([owned_squares, loss_local, count_local]),
        vector_grad,
        pos_grad,
    )
    loss_sum, loss_count = sums[1], sums[2]
    grad_norm = jnp.sqrt(sums[0])
    factor = jnp.minimum(1.0, CLIP_NORM / grad_norm)
    states = (
        (table.T, table_mean.T, table_square.T, table_grad, LEARN_RATE),
        (qkv_proj, qkv_mean, qkv_square, grad_qkv, LEARN_RATE),
        (out_proj, out_mean, out_square, grad_out, LEARN_RATE),
        (up_proj, up_mean, up_square, grad_up, LEARN_RATE),
        (down_proj, down_mean, down_square, grad_down, LEARN_RATE),
        (vectors, vec_mean, vec_square, vector_grad, RATE_VEC),
        (pos_table, pos_mean, pos_square, pos_grad, LEARN_RATE),
    )
    results = [loss_sum, loss_count, grad_norm]
    for weight, mean, square, grad, rate in states:
        results.extend(adam_update(weight, mean, square, grad * factor, rate))
    results[3:6] = [a.T for a in results[3:6]]
    return tuple(results)


def solution(mesh):
    chips = mesh.devices.reshape(-1, 2, mesh.shape["vocab"])
    mesh = jax.sharding.Mesh(chips, ALL)
    return jax.shard_map(
        per_device,
        mesh=mesh,
        in_specs=(
            P(ALL),
            P(ALL, None),
            P(ALL, None),
            P(ALL, None),
            P("vocab", ("z", "core")),
            P("vocab", ("z", "core")),
            P("vocab", ("z", "core")),
            P(None, ALL, None),
            P(None, ALL, None),
            P(None, ALL, None),
            P(None, ALL, None),
            P(None, ALL, None),
            P(None, ALL, None),
            P(None, ALL, None),
            P(None, ALL, None),
            P(None, ALL, None),
            P(None, ALL, None),
            P(None, ALL, None),
            P(None, ALL, None),
            P(),
            P(),
            P(),
            P(),
            P(),
            P(),
        ),
        out_specs=(
            P(),
            P(),
            P(),
            P("vocab", ("z", "core")),
            P("vocab", ("z", "core")),
            P("vocab", ("z", "core")),
            P(None, ALL, None),
            P(None, ALL, None),
            P(None, ALL, None),
            P(None, ALL, None),
            P(None, ALL, None),
            P(None, ALL, None),
            P(None, ALL, None),
            P(None, ALL, None),
            P(None, ALL, None),
            P(None, ALL, None),
            P(None, ALL, None),
            P(None, ALL, None),
            P(),
            P(),
            P(),
            P(),
            P(),
            P(),
        ),
        check_vma=False,
    )
```

```python
import functools

import jax
import jax.numpy as jnp
from jax import lax
from jax.experimental import pallas as pl
from jax.experimental.pallas import tpu as pltpu
from jax.sharding import PartitionSpec as P

L = 2
NSEG = 13
STEP = 10
SEG = 16


NORM_EPS = 1e-05
BETA_ONE = 0.9
BETA_TWO = 0.999
ADAM_EPS = 1e-08
LEARN_RATE = 0.1
RATE_VEC = 0.5
WEIGHT_DECAY = 0.1
CLIP_NORM = 0.1
HIGHEST = lax.Precision.HIGHEST
GELU_SCALE = 0.7978845608028654
GELU_CUBE = 0.044715
ALL = ("z", "core", "vocab")
ROWS_STEP = 2560
UNROLL = 16
HEAD_ROWS = 256
TURN = 512
MIB = 1024 * 1024
COST_SCALE = 1e15
LANES = 128


class Place:
    def __init__(self):
        self.nv = lax.axis_size("vocab")
        self.nz = lax.axis_size("z")
        self.count = self.nv * self.nz * 2
        self.v = lax.axis_index("vocab")
        self.z = lax.axis_index("z")
        self.c = lax.axis_index("core")
        self.where = jnp.stack([self.z, self.c, self.v]).astype(jnp.int32)
        self.core_alone = jnp.stack([self.z * 0, self.c, self.v * 0]).astype(jnp.int32)
        self.bits = [1 << i for i in range(self.nv.bit_length() - 1)]

    def swap(self, a, v=0, c=0, z=0):
        mask = (z * 2 + c) * self.nv + v
        return lax.ppermute(a, ALL, [(i, i ^ mask) for i in range(self.count)])

    def gather_z(self, a):
        return jnp.stack([a] + [self.swap(a, z=m) for m in range(1, self.nz)])

    def gather_v(self, a):
        return jnp.stack([a] + [self.swap(a, v=m) for m in range(1, self.nv)])

    def gather_c(self, a):
        return jnp.stack([a, self.swap(a, c=1)])

    def spread_v(self, a, order):
        masks = [0]
        held = a[None]
        for bit in order:
            held = jnp.concatenate([held, self.swap(held, v=bit)])
            masks = masks + [m ^ bit for m in masks]
        if masks == sorted(masks):
            return held
        return jnp.stack([held[masks.index(m)] for m in range(self.nv)])

    def spread_halves(self, held, orders):
        half = self.nz // 2
        return jnp.concatenate(
            [self.spread_v(held[:half], orders[0]), self.spread_v(held[half:], orders[1])], 1
        )

    def trade_z(self, a):
        tail = a.shape[1:]
        count = self.nz.bit_length() - 1
        a = a.reshape((2,) * count + tail)
        for step in range(count):
            axis = count - 1
            send = lax.index_in_dim(a, 1, axis, False)
            a = jnp.stack([lax.index_in_dim(a, 0, axis, False), self.swap(send, z=1 << step)])
        return a.reshape((self.nz,) + tail)

    def reduce_v(self, a, order, axis):
        left = list(reversed(self.bits))
        a = a.reshape(a.shape[:axis] + (2,) * len(left) + a.shape[axis + 1 :])
        for bit in order:
            at = axis + left.index(bit)
            a = lax.index_in_dim(a, 0, at, False) + self.swap(
                lax.index_in_dim(a, 1, at, False), v=bit
            )
            left.remove(bit)
        return a


def pick(a, index, axis):
    return lax.dynamic_index_in_dim(a, index, axis, False)


def tree_sum(terms):
    while len(terms) > 1:
        terms = [terms[i] + terms[i + 1] for i in range(0, len(terms), 2)]
    return terms[0]


def cost(seconds):
    return pl.CostEstimate(flops=int(seconds * COST_SCALE), transcendentals=0, bytes_accessed=0)


def put_kernel(slots, nv, where_ref, *refs):
    pieces, out = refs[: len(slots)], refs[-1]
    z, c = where_ref[0], where_ref[1]
    v = where_ref[2] if nv > 1 else 0
    for piece, (core, masks, z_masks) in zip(pieces, slots):
        for k, mask in enumerate(masks):
            for i, m in enumerate(z_masks):
                row = ((z ^ m) * 2 + (c ^ core)) * nv + (v ^ mask)
                out[row] = piece[k, i]


def put(place, pieces, slots, nv=None):
    nv = place.nv if nv is None else nv
    count = 2 * place.nz * nv
    rows, width = pieces[0].shape[2:]
    return pl.pallas_call(
        functools.partial(put_kernel, slots, nv),
        out_shape=jax.ShapeDtypeStruct((count, rows, width), pieces[0].dtype),
        in_specs=[pl.BlockSpec(memory_space=pltpu.SMEM)]
        + [pl.BlockSpec(memory_space=pltpu.VMEM)] * len(pieces),
        out_specs=pl.BlockSpec(memory_space=pltpu.VMEM),
        cost_estimate=cost(3e-6),
        compiler_params=pltpu.CompilerParams(vmem_limit_bytes=4 * count * rows * width + 4 * MIB),
    )(place.where, *pieces)


def owner_hot(where_ref, depth, rows, nv, nz, order):
    part = rows // (nv * nz)
    column = lax.broadcasted_iota(jnp.int32, (1, rows), 1)
    block = jnp.zeros((1, rows), jnp.int32)
    for k in range(1, nv * nz):
        block = block + jnp.where(column >= k * part, 1, 0)
    apart = jnp.zeros((1, rows), jnp.int32)
    for k, bit in enumerate(reversed(order)):
        apart = apart + jnp.where((block & (nz << k)) != 0, bit, 0)
    owner = ((block & (nz - 1)) ^ where_ref[0]) * 2 + where_ref[1]
    owner = owner * nv + (apart ^ where_ref[2])
    row = owner * part + column - block * part
    return (lax.broadcasted_iota(jnp.int32, (depth, rows), 0) == row).astype(jnp.bfloat16)


def pair_kernel(
    nv, nz, order, where_ref, x_ref, other_ref, y_ref, y_other_ref, out_ref, left_ref, left_other_ref
):
    @pl.when(pl.program_id(0) == 0)
    def _():
        hot = owner_hot(where_ref, x_ref.shape[1], left_ref.shape[1], nv, nz, order)
        left_ref[...] = jnp.dot(x_ref[...], hot, preferred_element_type=jnp.float32).astype(
            jnp.bfloat16
        )
        left_other_ref[...] = jnp.dot(
            other_ref[...], hot, preferred_element_type=jnp.float32
        ).astype(jnp.bfloat16)

    out_ref[...] = (
        dot_first(left_ref[...], y_ref[...]) + dot_first(left_other_ref[...], y_other_ref[...])
    ).astype(jnp.bfloat16)


def pair_grad(place, x, y):
    length, depth = x.shape
    rows, width = depth // 2, y.shape[1]
    block = 768 if width % 768 == 0 else width
    whole = pl.BlockSpec((length, depth), lambda i: (0, 0))
    part = pl.BlockSpec((length, block), lambda i: (0, i))
    return pl.pallas_call(
        functools.partial(pair_kernel, place.nv, place.nz, list(reversed(place.bits))),
        out_shape=jax.ShapeDtypeStruct((rows, width), jnp.bfloat16),
        grid=(width // block,),
        in_specs=[pl.BlockSpec(memory_space=pltpu.SMEM), whole, whole, part, part],
        out_specs=pl.BlockSpec((rows, block), lambda i: (0, i)),
        scratch_shapes=[pltpu.VMEM((length, rows), jnp.bfloat16)] * 2,
        cost_estimate=cost(5e-6),
        compiler_params=pltpu.CompilerParams(vmem_limit_bytes=14 * MIB),
    )(place.core_alone, x, place.swap(x, c=1), y, place.swap(y, c=1))


def wide_kernel(nv, order, where_ref, x_ref, other_ref, y_ref, y_other_ref, out_ref):
    total = dot_first(x_ref[...], y_ref[...]) + dot_first(other_ref[...], y_other_ref[...])
    rows = total.shape[0] // nv
    for v in range(nv):
        apart = where_ref[2] ^ v
        position = 0
        for bit in order:
            position = position * 2 + jnp.where((apart & bit) != 0, 1, 0)
        out_ref[position, 0] = total[v * rows : (v + 1) * rows].astype(jnp.bfloat16)


def pair_grad_wide(place, x, y):
    length, depth = x.shape
    width = y.shape[1]
    block = depth // (2 * place.nz)
    rows = block // place.nv
    other = place.swap(x, c=1)
    if block % 128 == 0:
        part = pl.BlockSpec((length, block), lambda i, where: (0, 2 * i + where[1]))
    else:
        x, other = (a.reshape(length, -1, block).transpose(1, 0, 2) for a in (x, other))
        part = pl.BlockSpec((None, length, block), lambda i, where: (2 * i + where[1], 0, 0))
    whole = pl.BlockSpec((length, width), lambda i, where: (0, 0))
    shape, block_shape = (place.nv, place.nz, rows, width), (place.nv, 1, rows, width)
    where_out = lambda i, where: (0, i ^ where[0], 0, 0)
    return pl.pallas_call(
        functools.partial(wide_kernel, place.nv, list(reversed(place.bits))),
        out_shape=jax.ShapeDtypeStruct(shape, jnp.bfloat16),
        grid_spec=pltpu.PrefetchScalarGridSpec(
            num_scalar_prefetch=1,
            grid=(place.nz,),
            in_specs=[part, part, whole, whole],
            out_specs=pl.BlockSpec(block_shape, where_out),
        ),
        cost_estimate=cost(5e-6),
        compiler_params=pltpu.CompilerParams(vmem_limit_bytes=14 * MIB),
    )(place.core_alone, x, other, y, place.swap(y, c=1)).reshape(depth // 2, width)


def tie(main, *steps):
    main, values = lax.optimization_barrier((main, [s.value for s in steps]))
    for s, value in zip(steps, values):
        s.value = value
    return main


class Traded:
    def __init__(self, place, value):
        self.place = place
        self.tail = value.shape[1:]
        self.count = value.shape[0].bit_length() - 1
        self.left = self.count
        self.value = value.reshape((2,) * self.count + self.tail)

    def step(self):
        axis = self.count - 1
        a = self.value
        send = lax.index_in_dim(a, 1, axis, False)
        got = self.place.swap(send, z=1 << (self.count - self.left))
        self.value = jnp.stack([lax.index_in_dim(a, 0, axis, False), got])
        self.left -= 1

    def rest(self):
        while self.left:
            self.step()
        return self.value.reshape((1 << self.count,) + self.tail)


def quarters(place, value):
    part = value.shape[-1] // 4
    return [Traded(place, value[..., k * part : (k + 1) * part]) for k in range(4)]


def advance(main, *trades):
    main = tie(main, *trades)
    for t in trades:
        if t.left:
            t.step()
    return main


def joined(trades):
    return jnp.concatenate([t.rest() for t in trades], -1)


class Held:
    def __init__(self, value):
        self.value = value


def as_wide(a):
    return a.astype(jnp.float32)


def as_low(a):
    return a.astype(jnp.bfloat16)


def reduce_flat_core(place, vector, table):
    length = vector.shape[0]
    first = -(-length // 1024) * 8
    second = table.size // 128
    rows = -(-(first + second) // (place.count * 8)) * 8
    a = jnp.concatenate(
        [jnp.pad(vector, (0, first * 128 - length)).reshape(first, 128), table.reshape(second, 128)]
    )
    a = jnp.pad(a, ((0, place.count * rows - first - second), (0, 0)))
    a = a.reshape(place.nz, 2, place.nv, rows, 128)
    return pick(a, place.c, 1) + place.swap(pick(a, 1 - place.c, 1), c=1)


def reduce_flat_plane(place, a):
    bits = list(reversed(place.bits))
    a = a.reshape((place.nz,) + (2,) * len(bits) + a.shape[2:])
    for bit in bits:
        mine = (place.v // bit) % 2
        a = pick(a, mine, 1) + place.swap(pick(a, 1 - mine, 1), v=bit)
    return a


def reduce_flat_z(place, a):
    count = place.nz.bit_length() - 1
    a = a.reshape((2,) * count + a.shape[1:])
    for step in reversed(range(count)):
        mine = (place.z >> step) % 2
        a = pick(a, mine, 0) + place.swap(pick(a, 1 - mine, 0), z=1 << step)
    return a


def unslab_kernel(slabs_ref, out_ref):
    ranks = out_ref.shape[1] // slabs_ref.shape[1]
    rows, width = slabs_ref.shape[1], out_ref.shape[2]
    for k in range(ranks):
        out_ref[:, k * rows : (k + 1) * rows, :] = slabs_ref[:, :, k * width : (k + 1) * width]


def unslab_rows(place, gathered, ranks, width, layer_index):
    count, total = place.count, ranks * width
    rows = gathered.shape[0] // count
    if rows % 8:
        slabs = gathered[:, layer_index * total : (layer_index + 1) * total]
        slabs = slabs.reshape(count, rows, ranks, width)
        return slabs.transpose(0, 2, 1, 3).reshape(-1, width)
    return pl.pallas_call(
        unslab_kernel,
        out_shape=jax.ShapeDtypeStruct((count, rows * ranks, width), gathered.dtype),
        grid=(count // 4,),
        in_specs=[pl.BlockSpec((4, rows, total), lambda i: (i, 0, layer_index))],
        out_specs=pl.BlockSpec((4, rows * ranks, width), lambda i: (i, 0, 0)),
        cost_estimate=cost(7e-6),
    )(gathered.reshape(count, rows, -1)).reshape(-1, width)


def gather_flat(place, own, scalars, vector, table):
    length, rows = vector.shape[0], own.shape[0]
    first, second = -(-length // 1024) * 8, table.size // 128
    own = jnp.concatenate([own, jnp.pad(scalars[None], ((0, 7), (0, 128 - scalars.shape[0])))])
    whole = gather_blocks(place, own)
    scalars = jnp.sum(whole[:, rows, : scalars.shape[0]], 0)
    whole = whole[:, :rows].reshape(-1, 128)
    return (
        scalars,
        whole[:first].reshape(-1)[:length],
        whole[first : first + second].reshape(table.shape),
    )


def put_blocks(place, held):
    everyone = list(range(place.nz))
    masks = list(range(place.nv))
    return put(place, [held, place.swap(held, c=1)], [(0, masks, everyone), (1, masks, everyone)])


def gather_blocks(place, block):
    return put_blocks(place, place.gather_v(place.gather_z(block)))


def column_hot(where_ref, part, width, total):
    first = (part ^ (where_ref[0] * 2 + where_ref[1])) * width
    rows = lax.broadcasted_iota(jnp.int32, (width, total), 0) + first
    return (rows == lax.broadcasted_iota(jnp.int32, (width, total), 1)).astype(jnp.bfloat16)


def embed_kernel(where_ref, table_ref, *refs):
    pieces, out_ref = refs[:-1], refs[-1]
    total_width = out_ref.shape[1]
    width = total_width // (2 * len(pieces))
    total = jnp.zeros(out_ref.shape, jnp.float32)
    for m, piece in enumerate(pieces):
        for c in range(2):
            hot = column_hot(where_ref, 2 * m + c, width, total_width)
            total = total + jnp.dot(
                piece[c, :, :width], hot, preferred_element_type=jnp.float32
            )
    out_ref[...] = total
    trunk = 8 * SEG
    out_ref[:trunk, :] += table_ref[:trunk, :]
    for k in range(12):
        at = trunk + k * SEG
        row = trunk if k < 4 else trunk + SEG
        out_ref[at : at + SEG, :] += table_ref[row : row + SEG, :]


def embed(place, pieces, table):
    length, width = pieces[0].shape[1:]
    return pl.pallas_call(
        embed_kernel,
        out_shape=jax.ShapeDtypeStruct((length, table.shape[1]), jnp.float32),
        in_specs=[pl.BlockSpec(memory_space=pltpu.SMEM)]
        + [pl.BlockSpec(memory_space=pltpu.VMEM)] * (1 + len(pieces)),
        out_specs=pl.BlockSpec(memory_space=pltpu.VMEM),
        cost_estimate=cost(1.7e-6),
        compiler_params=pltpu.CompilerParams(vmem_limit_bytes=16 * MIB),
    )(place.where, table, *pieces)


def part_kernel(where_ref, grad_ref, out_ref):
    grad = grad_ref[...].astype(jnp.bfloat16)
    nz = out_ref.shape[0]
    width = grad.shape[1] // (2 * nz)
    out_ref[...] = jnp.zeros_like(out_ref)
    for m in range(nz):
        for c in range(2):
            hot = column_hot(where_ref, 2 * m + c, width, grad.shape[1])
            out_ref[m, c, :, :width] = dot_last(grad, hot).astype(jnp.bfloat16)


def part_columns(place, grad):
    length, total = grad.shape
    return pl.pallas_call(
        part_kernel,
        out_shape=jax.ShapeDtypeStruct((place.nz, 2, length, LANES), jnp.bfloat16),
        in_specs=[
            pl.BlockSpec(memory_space=pltpu.SMEM),
            pl.BlockSpec(memory_space=pltpu.VMEM),
        ],
        out_specs=pl.BlockSpec(memory_space=pltpu.VMEM),
        cost_estimate=cost(1.8e-6),
        compiler_params=pltpu.CompilerParams(vmem_limit_bytes=16 * MIB),
    )(place.where, grad)


def turned(value, axis):
    size = max(value.shape)
    same = lax.broadcasted_iota(jnp.int32, (size, size), 0) == lax.broadcasted_iota(
        jnp.int32, (size, size), 1
    )
    return jnp.sum(jnp.where(same, value, jnp.zeros((), value.dtype)), axis, keepdims=True)


def hits(first_ref, targets_ref, shape):
    column = turned(targets_ref[...], 1) - first_ref[0]
    return column == lax.broadcasted_iota(jnp.int32, shape, 1)


def logits_kernel(first_ref, rows_ref, table_ref, targets_ref, stats_ref):
    logits = jnp.dot(rows_ref[...], table_ref[...], preferred_element_type=jnp.float32)
    top = jnp.max(logits, 1, keepdims=True)
    exps = jnp.exp(logits - top)
    picked = jnp.where(hits(first_ref, targets_ref, logits.shape), logits, 0.0)
    stats_ref[0:1, :] = turned(top, 0)
    stats_ref[1:2, :] = turned(jnp.sum(exps, 1, keepdims=True), 0)
    stats_ref[2:3, :] = turned(jnp.sum(picked, 1, keepdims=True), 0)


def head_forward(first, rows, table, targets):
    count, width = rows.shape
    size = table.shape[1]
    return pl.pallas_call(
        logits_kernel,
        out_shape=jax.ShapeDtypeStruct((3, count), jnp.float32),
        grid=(count // HEAD_ROWS,),
        in_specs=[
            pl.BlockSpec(memory_space=pltpu.SMEM),
            pl.BlockSpec((HEAD_ROWS, width), lambda i: (i, 0)),
            pl.BlockSpec((width, size), lambda i: (0, 0)),
            pl.BlockSpec((1, HEAD_ROWS), lambda i: (0, i)),
        ],
        out_specs=pl.BlockSpec((3, HEAD_ROWS), lambda i: (0, i)),
        cost_estimate=cost(11.6e-6),
        compiler_params=pltpu.CompilerParams(vmem_limit_bytes=24 * MIB),
    )(first, rows, table, targets)


def slopes_kernel(first_ref, rows_in_ref, total_ref, table_ref, targets_ref, slopes_ref, rows_ref):
    logits = jnp.dot(rows_in_ref[...], table_ref[...], preferred_element_type=jnp.float32)
    exps = jnp.exp(logits - turned(total_ref[...], 1))
    hit = hits(first_ref, targets_ref, exps.shape)
    alive = turned(targets_ref[...], 1) >= 0
    slopes = jnp.where(alive, exps - jnp.where(hit, 1.0, 0.0), 0.0).astype(jnp.bfloat16)
    slopes_ref[...] = slopes
    rows_ref[...] = dot_last(slopes, table_ref[...]).astype(jnp.bfloat16)


def head_backward(first, rows, total, table, targets):
    count, width = rows.shape
    size = table.shape[1]
    return pl.pallas_call(
        slopes_kernel,
        out_shape=(
            jax.ShapeDtypeStruct((count, size), jnp.bfloat16),
            jax.ShapeDtypeStruct((count, width), jnp.bfloat16),
        ),
        grid=(count // HEAD_ROWS,),
        in_specs=[
            pl.BlockSpec(memory_space=pltpu.SMEM),
            pl.BlockSpec((HEAD_ROWS, width), lambda i: (i, 0)),
            pl.BlockSpec((1, HEAD_ROWS), lambda i: (0, i)),
            pl.BlockSpec((width, size), lambda i: (0, 0)),
            pl.BlockSpec((1, HEAD_ROWS), lambda i: (0, i)),
        ],
        out_specs=(
            pl.BlockSpec((HEAD_ROWS, size), lambda i: (i, 0)),
            pl.BlockSpec((HEAD_ROWS, width), lambda i: (i, 0)),
        ),
        cost_estimate=cost(16e-6),
        compiler_params=pltpu.CompilerParams(vmem_limit_bytes=24 * MIB),
    )(first, rows, total, table, targets)


def cut_kernel(where_ref, columns_ref, out_ref):
    out_ref[0, 0] = columns_ref[...].astype(out_ref.dtype)


def cut(place, columns):
    width, size = columns.shape
    part = size // (2 * place.nz)
    if part % 128:
        order = jnp.arange(2 * place.nz) ^ (place.z * 2 + place.c)
        parts = columns.astype(jnp.bfloat16).reshape(width, 2 * place.nz, part).transpose(1, 0, 2)
        return jnp.take(parts, order, axis=0).reshape(place.nz, 2, width, part)
    return pl.pallas_call(
        cut_kernel,
        out_shape=jax.ShapeDtypeStruct((place.nz, 2, width, part), jnp.bfloat16),
        grid_spec=pltpu.PrefetchScalarGridSpec(
            num_scalar_prefetch=1,
            grid=(2 * place.nz,),
            in_specs=[
                pl.BlockSpec((width, part), lambda i, where: (0, i ^ (where[0] * 2 + where[1])))
            ],
            out_specs=pl.BlockSpec((1, 1, width, part), lambda i, where: (i // 2, i % 2, 0, 0)),
        ),
        cost_estimate=cost(7e-6),
    )(place.where, columns)


def find_kernel(ids_ref, columns_ref, out_ref, rows_ref, found_ref):
    size = columns_ref.shape[1]

    @pl.when(pl.program_id(0) == 0)
    def _():
        def turn(i, carry):
            at = pl.multiple_of(i * TURN, TURN)
            part = columns_ref[:, pl.ds(at, TURN)].astype(jnp.bfloat16).astype(jnp.float32)
            rows_ref[pl.ds(at, TURN), : part.shape[0]] = part.T
            return carry

        rows_ref[:, columns_ref.shape[0] :] = jnp.zeros(
            (rows_ref.shape[0], LANES - columns_ref.shape[0]), jnp.float32
        )

        lax.fori_loop(0, size // TURN, turn, 0)
        rows_ref[pl.ds(size, 8), :] = jnp.zeros((8, rows_ref.shape[1]), jnp.float32)

    first = pl.program_id(0) * out_ref.shape[0]

    def body(i, carry):
        for u in range(UNROLL):
            t = i * UNROLL + u
            found_ref[pl.ds(t, 1), :] = rows_ref[pl.ds(ids_ref[first + t], 1), :]
        return carry

    lax.fori_loop(0, out_ref.shape[0] // UNROLL, body, 0)
    out_ref[...] = found_ref[...].astype(out_ref.dtype)


def find_rows(ids, columns):
    width, size = columns.shape
    return pl.pallas_call(
        find_kernel,
        out_shape=jax.ShapeDtypeStruct((ids.shape[0], LANES), jnp.bfloat16),
        grid_spec=pltpu.PrefetchScalarGridSpec(
            num_scalar_prefetch=1,
            grid=(ids.shape[0] // ROWS_STEP,),
            in_specs=[pl.BlockSpec(memory_space=pltpu.VMEM)],
            out_specs=pl.BlockSpec((ROWS_STEP, LANES), lambda i, ids: (i, 0)),
            scratch_shapes=[
                pltpu.VMEM((size + 8, LANES), jnp.float32),
                pltpu.VMEM((ROWS_STEP, LANES), jnp.float32),
            ],
        ),
        cost_estimate=cost(18e-6),
        compiler_params=pltpu.CompilerParams(vmem_limit_bytes=24 * MIB),
    )(ids, columns)


def add_kernel(ids_ref, low_ref, more_ref, head_ref, out_ref, rows_ref, *parts):
    step = pl.program_id(0)
    first = step * rows_ref.shape[0]
    size = out_ref.shape[1]
    early = step < pl.num_programs(0) // 2
    rows_ref[...] = jnp.where(early, low_ref[...], more_ref[...]).astype(jnp.float32)

    @pl.when(step == 0)
    def _():
        for part in parts:
            part[...] = jnp.zeros_like(part)

    def body(i, carry):
        for u in range(UNROLL):
            t = i * UNROLL + u
            part = parts[u % len(parts)]
            where = pl.ds(ids_ref[first + t], 1)
            part[where, :] = part[where, :] + rows_ref[pl.ds(t, 1), :]
        return carry

    lax.fori_loop(0, rows_ref.shape[0] // UNROLL, body, 0)

    @pl.when(step == pl.num_programs(0) - 1)
    def _():
        def turn(i, carry):
            at = pl.ds(pl.multiple_of(i * TURN, TURN), TURN)
            total = tree_sum([part[at, :] for part in parts])
            part = head_ref.shape[2]
            head = head_ref[i * TURN // part, :, pl.ds(pl.multiple_of(i * TURN % part, TURN), TURN)]
            out_ref[:, at] = total.T[: out_ref.shape[0]] + head.astype(jnp.float32)
            return carry

        lax.fori_loop(0, size // TURN, turn, 0)


def add_rows(ids, rows, more, head):
    width, size = head.shape[1], head.shape[0] * head.shape[2]
    if head.shape[2] % TURN:
        head = head.transpose(1, 0, 2).reshape(1, width, size)
    steps = rows.shape[0] // ROWS_STEP
    return pl.pallas_call(
        add_kernel,
        out_shape=jax.ShapeDtypeStruct((width, size), jnp.float32),
        grid_spec=pltpu.PrefetchScalarGridSpec(
            num_scalar_prefetch=1,
            grid=(ids.shape[0] // ROWS_STEP,),
            in_specs=[
                pl.BlockSpec((ROWS_STEP, LANES), lambda i, ids: (jnp.minimum(i, steps - 1), 0)),
                pl.BlockSpec((ROWS_STEP, LANES), lambda i, ids: (jnp.maximum(i - steps, 0), 0)),
                pl.BlockSpec(memory_space=pltpu.VMEM),
            ],
            out_specs=pl.BlockSpec(memory_space=pltpu.VMEM),
            scratch_shapes=[pltpu.VMEM((ROWS_STEP, LANES), jnp.float32)]
            + [pltpu.VMEM((size + 8, LANES), jnp.float32)] * 4,
        ),
        cost_estimate=cost(25e-6),
        compiler_params=pltpu.CompilerParams(vmem_limit_bytes=40 * MIB),
    )(ids, rows, more, head)


def norm_apply(stream, gain, shift):
    center = stream - jnp.mean(stream, -1, keepdims=True)
    spread = jnp.mean(center * center, -1, keepdims=True)
    return center * lax.rsqrt(spread + NORM_EPS) * gain + shift


def norm_back(stream, gain, grad):
    center = stream - jnp.mean(stream, -1, keepdims=True)
    scale = lax.rsqrt(jnp.mean(center * center, -1, keepdims=True) + NORM_EPS)
    unit = center * scale
    inner = grad * gain
    part = inner - jnp.mean(inner, -1, keepdims=True)
    part = scale * (part - unit * jnp.mean(inner * unit, -1, keepdims=True))
    return part, jnp.sum(grad * unit, 0, keepdims=True), jnp.sum(grad, 0, keepdims=True)


def gelu_parts(value):
    inner = GELU_SCALE * (value + GELU_CUBE * value * value * value)
    bend = jnp.tanh(inner)
    half = 0.5 * (1.0 + bend)
    slope = GELU_SCALE * (1.0 + 3.0 * GELU_CUBE * value * value)
    return value * half, half + 0.5 * value * (1.0 - bend * bend) * slope


def split_layer(vector_row, model_width, head_size, hidden_width):
    widths = [model_width] * 3 + [head_size] + [model_width] * 3 + [hidden_width, model_width]
    pieces = []
    offset = 0
    for width in widths:
        pieces.append(vector_row[offset : offset + width])
        offset += width
    return pieces


def tree_layout(total, seg_len):
    places = jnp.arange(total, dtype=jnp.int32)
    trunk = 8 * seg_len
    beyond = jnp.maximum(places - trunk, 0) // seg_len
    segment = jnp.where(places < trunk, 0, 1 + beyond)
    offset = places - trunk - beyond * seg_len
    path_depth = jnp.where(
        places < trunk, places, jnp.where(segment <= 4, trunk + offset, trunk + seg_len + offset)
    )
    return (places, segment, path_depth)


def tree_mask(parent_row, places, segment, count):
    labels = jnp.arange(count, dtype=jnp.int32)
    parent_hot = (parent_row[:, None] == labels[None, :]).astype(jnp.float32)
    grand_hot = jnp.dot(parent_hot, parent_hot, precision=HIGHEST)
    ancestor = jnp.eye(count, dtype=jnp.float32) + parent_hot + grand_hot
    seg_hot = (segment[:, None] == labels[None, :]).astype(jnp.float32)
    reach = jnp.dot(jnp.dot(seg_hot, ancestor, precision=HIGHEST), seg_hot.T, precision=HIGHEST)
    return (reach > 0.5) & (places[None, :] <= places[:, None])


def dot_first(left, right):
    return lax.dot_general(
        left, right, (((0,), (0,)), ((), ())), preferred_element_type=jnp.float32
    )


def dot_last(left, right):
    return lax.dot_general(
        left, right, (((1,), (1,)), ((), ())), preferred_element_type=jnp.float32
    )


def column_sum(grad_low):
    return jnp.sum(grad_low.astype(jnp.float32), 0)


def fetch(copies):
    for copy in copies:
        copy.start()
    return copies


def head_probs(mixed_ref, bias, h, keys, size, model_width):
    queries = mixed_ref[:, h * size : (h + 1) * size]
    scores = dot_last(keys, queries) * size ** (-0.5) + bias
    exps = jnp.exp(scores - jnp.max(scores, 0, keepdims=True))
    return queries, exps * (1.0 / jnp.sum(exps, 0, keepdims=True))


def forward_kernel(
    base,
    stream_ref,
    row_ref,
    bias_ref,
    wide_ref,
    down_ref,
    result_ref,
    normed_ref,
    mixed_ref,
    attended_ref,
    middle_ref,
    normed_two_ref,
    hidden_ref,
    active_ref,
    qkv_low,
    out_low,
    up_low,
    down_low,
    sems,
):
    model_width = stream_ref.shape[1]
    size = (qkv_low.shape[1] - model_width) // 2
    cuts = (qkv_low.shape[1], qkv_low.shape[1] + model_width)
    copies = fetch(
        [
            pltpu.make_async_copy(wide_ref.at[:, pl.ds(base, cuts[0])], qkv_low, sems.at[0]),
            pltpu.make_async_copy(
                wide_ref.at[:, pl.ds(base + cuts[0], model_width)], out_low, sems.at[1]
            ),
            pltpu.make_async_copy(
                wide_ref.at[:, pl.ds(base + cuts[1], up_low.shape[1])], up_low, sems.at[2]
            ),
            pltpu.make_async_copy(down_ref, down_low, sems.at[3]),
        ]
    )

    def row(k, width=model_width):
        return row_ref[k : k + 1, :width]

    stream = stream_ref[...]
    normed = norm_apply(stream, row(0), row(1)).astype(jnp.bfloat16)
    normed_ref[...] = normed
    copies[0].wait()
    mixed = jnp.dot(normed, qkv_low[...], preferred_element_type=jnp.float32)
    mixed = (mixed + row(9, mixed.shape[1])).astype(jnp.bfloat16)
    mixed_ref[...] = mixed
    keys, values = mixed[:, model_width : model_width + size], mixed[:, model_width + size :]
    for h in range(model_width // size):
        ignored, probs = head_probs(mixed_ref, bias_ref[...], h, keys, size, model_width)
        attended_ref[:, h * size : (h + 1) * size] = dot_first(
            probs.astype(jnp.bfloat16), values
        ).astype(jnp.bfloat16)
    copies[1].wait()
    middle = stream + jnp.dot(
        attended_ref[...], out_low[...], preferred_element_type=jnp.float32
    )
    middle = middle + row(4)
    middle_ref[...] = middle
    normed_two = norm_apply(middle, row(5), row(6)).astype(jnp.bfloat16)
    normed_two_ref[...] = normed_two
    copies[2].wait()
    copies[3].wait()
    total = middle + row(8)
    for k in range(up_low.shape[1] // model_width):
        at = slice(k * model_width, (k + 1) * model_width)
        hidden = jnp.dot(normed_two, up_low[:, at], preferred_element_type=jnp.float32)
        hidden = hidden + row_ref[7:8, at]
        hidden_ref[:, at] = hidden
        active = gelu_parts(hidden)[0].astype(jnp.bfloat16)
        active_ref[:, at] = active
        total = total + jnp.dot(active, down_low[at, :], preferred_element_type=jnp.float32)
    result_ref[...] = total


def shape_of(shape, kind):
    return jax.ShapeDtypeStruct(shape, kind)


VMEM = pl.BlockSpec(memory_space=pltpu.VMEM)
ANY = pl.BlockSpec(memory_space=pltpu.HBM)


def layer_forward(stream, row, bias, wide, down, base, row_width):
    length, model_width = stream.shape
    hidden_width = down.shape[0]
    mixed_width = row_width
    f32, low = jnp.float32, jnp.bfloat16
    return pl.pallas_call(
        functools.partial(forward_kernel, base),
        out_shape=(
            shape_of((length, model_width), f32),
            shape_of((length, model_width), low),
            shape_of((length, mixed_width), low),
            shape_of((length, model_width), low),
            shape_of((length, model_width), f32),
            shape_of((length, model_width), low),
            shape_of((length, hidden_width), f32),
            shape_of((length, hidden_width), low),
        ),
        in_specs=[VMEM, VMEM, VMEM, ANY, ANY],
        out_specs=(VMEM,) * 8,
        scratch_shapes=[
            pltpu.VMEM((model_width, mixed_width), low),
            pltpu.VMEM((model_width, model_width), low),
            pltpu.VMEM((model_width, hidden_width), low),
            pltpu.VMEM((hidden_width, model_width), low),
            pltpu.SemaphoreType.DMA((4,)),
        ],
        cost_estimate=cost(12e-6),
        compiler_params=pltpu.CompilerParams(vmem_limit_bytes=46 * MIB),
    )(stream, row, bias, wide, down)


def mlp_kernel(
    first,
    grad_ref,
    middle_ref,
    hidden_ref,
    row_ref,
    wide_ref,
    down_ref,
    middle_grad_ref,
    branch_ref,
    hidden_grad_ref,
    vector_ref,
    up_low,
    down_low,
    sems,
):
    model_width = grad_ref.shape[1]
    start = first
    copies = fetch(
        [
            pltpu.make_async_copy(down_ref, down_low, sems.at[0]),
            pltpu.make_async_copy(
                wide_ref.at[:, start : start + up_low.shape[1]], up_low, sems.at[1]
            ),
        ]
    )
    grad = grad_ref[...]
    branch = grad.astype(jnp.bfloat16)
    branch_ref[...] = branch
    vector_ref[...] = jnp.zeros_like(vector_ref)
    vector_ref[3:4, :model_width] = jnp.sum(branch.astype(jnp.float32), 0, keepdims=True)
    copies[0].wait()
    copies[1].wait()
    total = jnp.zeros_like(grad)
    for k in range(up_low.shape[1] // model_width):
        at = slice(k * model_width, (k + 1) * model_width)
        slope = gelu_parts(hidden_ref[:, at])[1]
        hidden_grad = (slope * dot_last(branch, down_low[at, :])).astype(jnp.bfloat16)
        hidden_grad_ref[:, at] = hidden_grad
        vector_ref[2:3, at] = jnp.sum(hidden_grad.astype(jnp.float32), 0, keepdims=True)
        total = total + dot_last(hidden_grad, up_low[:, at])
    part, gain_grad, shift_grad = norm_back(middle_ref[...], row_ref[5:6, :model_width], total)
    vector_ref[0:1, :model_width] = gain_grad
    vector_ref[1:2, :model_width] = shift_grad
    middle_grad_ref[...] = grad + part


def mlp_backward(grad, middle, hidden, row, wide, down, first):
    length, model_width = grad.shape
    hidden_width = down.shape[0]
    f32, low = jnp.float32, jnp.bfloat16
    return pl.pallas_call(
        functools.partial(mlp_kernel, first),
        out_shape=(
            shape_of((length, model_width), f32),
            shape_of((length, model_width), low),
            shape_of((length, hidden_width), low),
            shape_of((8, hidden_width), f32),
        ),
        in_specs=[VMEM, VMEM, VMEM, VMEM, ANY, ANY],
        out_specs=(VMEM,) * 4,
        scratch_shapes=[
            pltpu.VMEM((model_width, hidden_width), low),
            pltpu.VMEM((hidden_width, model_width), low),
            pltpu.SemaphoreType.DMA((2,)),
        ],
        cost_estimate=cost(6.5e-6),
        compiler_params=pltpu.CompilerParams(vmem_limit_bytes=46 * MIB),
    )(grad, middle, hidden, row, wide, down)


def attn_kernel(
    base,
    middle_grad_ref,
    stream_ref,
    mixed_ref,
    row_ref,
    bias_ref,
    wide_ref,
    stream_grad_ref,
    out_grad_ref,
    mixed_grad_ref,
    vector_ref,
    qkv_low,
    out_low,
    attended_ref,
    sems,
):
    model_width = stream_ref.shape[1]
    size = (qkv_low.shape[1] - model_width) // 2
    cut = qkv_low.shape[1]
    copies = fetch(
        [
            pltpu.make_async_copy(
                wide_ref.at[:, pl.ds(base + cut, model_width)], out_low, sems.at[0]
            ),
            pltpu.make_async_copy(wide_ref.at[:, pl.ds(base, cut)], qkv_low, sems.at[1]),
        ]
    )
    middle_grad = middle_grad_ref[...]
    out_grad = middle_grad.astype(jnp.bfloat16)
    out_grad_ref[...] = out_grad
    vector_ref[...] = jnp.zeros_like(vector_ref)
    vector_ref[3:4, :model_width] = jnp.sum(out_grad.astype(jnp.float32), 0, keepdims=True)
    copies[0].wait()
    attended_ref[...] = dot_last(out_grad, out_low[...]).astype(jnp.bfloat16)
    keys = mixed_ref[:, model_width : model_width + size]
    values = mixed_ref[:, model_width + size :]
    keys_grad = jnp.zeros(keys.shape, jnp.float32)
    values_grad = jnp.zeros(values.shape, jnp.float32)
    for h in range(model_width // size):
        at = slice(h * size, (h + 1) * size)
        queries, probs = head_probs(mixed_ref, bias_ref[...], h, keys, size, model_width)
        grad = attended_ref[:, at]
        values_grad = values_grad + jnp.dot(
            probs.astype(jnp.bfloat16), grad, preferred_element_type=jnp.float32
        )
        probs_grad = dot_last(values, grad)
        scores_grad = probs * (probs_grad - jnp.sum(probs * probs_grad, 0, keepdims=True))
        scores_grad = scores_grad.astype(jnp.bfloat16)
        keys_grad = keys_grad + jnp.dot(
            scores_grad, queries, preferred_element_type=jnp.float32
        )
        mixed_grad_ref[:, at] = (dot_first(scores_grad, keys) * size ** (-0.5)).astype(jnp.bfloat16)
    mixed_grad_ref[:, model_width : model_width + size] = (keys_grad * size ** (-0.5)).astype(
        jnp.bfloat16
    )
    mixed_grad_ref[:, model_width + size :] = values_grad.astype(jnp.bfloat16)
    mixed_grad = mixed_grad_ref[...]
    vector_ref[2:3, :] = jnp.sum(mixed_grad.astype(jnp.float32), 0, keepdims=True)
    copies[1].wait()
    total = dot_last(mixed_grad, qkv_low[...])
    part, gain_grad, shift_grad = norm_back(stream_ref[...], row_ref[0:1, :model_width], total)
    vector_ref[0:1, :model_width] = gain_grad
    vector_ref[1:2, :model_width] = shift_grad
    stream_grad_ref[...] = middle_grad + part


def attn_backward(middle_grad, stream, mixed, row, bias, wide, base):
    length, model_width = stream.shape
    mixed_width = mixed.shape[1]
    f32, low = jnp.float32, jnp.bfloat16
    return pl.pallas_call(
        functools.partial(attn_kernel, base),
        out_shape=(
            shape_of((length, model_width), f32),
            shape_of((length, model_width), low),
            shape_of((length, mixed_width), low),
            shape_of((8, mixed_width), f32),
        ),
        in_specs=[VMEM, VMEM, VMEM, VMEM, VMEM, ANY],
        out_specs=(VMEM,) * 4,
        scratch_shapes=[
            pltpu.VMEM((model_width, mixed_width), low),
            pltpu.VMEM((model_width, model_width), low),
            pltpu.VMEM((length, model_width), low),
            pltpu.SemaphoreType.DMA((2,)),
        ],
        cost_estimate=cost(11e-6),
        compiler_params=pltpu.CompilerParams(vmem_limit_bytes=46 * MIB),
    )(middle_grad, stream, mixed, row, bias, wide)


def adam_update(weight, mean, square, grad, rate):
    mean_new = BETA_ONE * mean + (1.0 - BETA_ONE) * grad
    square_new = BETA_TWO * square + (1.0 - BETA_TWO) * grad * grad
    mean_hat = mean_new / (1.0 - BETA_ONE**STEP)
    square_hat = square_new / (1.0 - BETA_TWO**STEP)
    weight_new = weight - rate * (
        mean_hat / (jnp.sqrt(square_hat) + ADAM_EPS) + WEIGHT_DECAY * weight
    )
    return (weight_new, mean_new, square_new)


def per_device(
    token_ids,
    parents,
    comp_pos,
    targets,
    table,
    table_mean,
    table_square,
    qkv_proj,
    qkv_mean,
    qkv_square,
    out_proj,
    out_mean,
    out_square,
    up_proj,
    up_mean,
    up_square,
    down_proj,
    down_mean,
    down_square,
    vectors,
    vec_mean,
    vec_square,
    pos_table,
    pos_mean,
    pos_square,
):
    place = Place()
    nv, nz = place.nv, place.nz
    length = token_ids.shape[0]
    model_width = pos_table.shape[1]
    head_size = (qkv_proj.shape[2] - model_width) // 2
    layer_width = 7 * model_width + head_size + up_proj.shape[2]
    slot_count = comp_pos.shape[1]
    shard_size, own_width = table.shape
    slice_size = shard_size // (2 * nz)
    bits = place.bits
    orders = (bits, list(reversed(bits)))

    own_slots = comp_pos[0]
    live = own_slots >= 0
    cut_one, cut_two = qkv_proj.shape[2], qkv_proj.shape[2] + out_proj.shape[2]
    cut_three = cut_two + up_proj.shape[2]
    shard_rows = qkv_proj.shape[1]
    ranks = down_proj.shape[1] // shard_rows

    everyone = list(range(nz))
    down_low = down_proj.astype(jnp.bfloat16)
    weights = lax.all_gather(
        jnp.concatenate(
            [
                down_low[i, k * shard_rows : (k + 1) * shard_rows]
                for i in range(L)
                for k in range(ranks)
            ]
            + [a[i].astype(jnp.bfloat16) for i in range(L) for a in (qkv_proj, out_proj, up_proj)],
            1,
        ),
        ALL,
        axis=0,
        tiled=True,
    )
    meta = jnp.concatenate([token_ids, jnp.where(live, targets[0], -1)])
    meta = place.gather_v(place.gather_z(place.gather_c(meta)))

    masks = list(range(nv))
    all_targets = put(
        place, [meta[:, :, :1, length:], meta[:, :, 1:, length:]], [(0, masks, everyone), (1, masks, everyone)]
    ).reshape(1, -1)
    meta = meta.transpose(2, 0, 1, 3)
    all_ids = meta[..., :length].reshape(-1)
    local_ids = all_ids - place.v * shard_size
    inside = (local_ids >= 0) & (local_ids < shard_size)
    safe_ids = jnp.where(inside, local_ids, shard_size)
    found = find_rows(safe_ids, table.T)
    found = found.reshape(2, nv, nz, length, LANES)
    found = jnp.stack([place.reduce_v(found[c], orders[c], 0) for c in range(2)])
    found = jnp.stack([found[0], place.swap(found[1], c=1)], 1)
    found = [found[0]] + [place.swap(found[m], z=m) for m in range(1, nz)]
    stream = embed(place, found, pos_table)
    stream, columns = tie((stream, table.T))
    stream, columns = tie((stream, cut(place, columns)))
    wdowns = [unslab_rows(place, weights, ranks, model_width, 0)]
    wdowns, columns = tie((wdowns, columns))
    parts = quarters(place, columns)
    parts[0].step()
    parts[1].step()
    wdowns += [unslab_rows(place, weights, ranks, model_width, i) for i in range(1, L)]

    places, segment, path_depth = tree_layout(length, SEG)
    allowed = tree_mask(parents[0], places, segment, NSEG)
    trunk = 8 * SEG
    bias = jnp.where(allowed, 0.0, -1e30).T
    layer_rows = []
    for layer_index in range(L):
        pieces = split_layer(
            vectors[layer_index * layer_width : (layer_index + 1) * layer_width],
            model_width,
            head_size,
            up_proj.shape[2],
        )
        pieces.append(
            jnp.concatenate([pieces[2], jnp.zeros((head_size,), jnp.float32), pieces[3]])
        )
        layer_rows.append(
            jnp.stack([jnp.pad(p, (0, up_proj.shape[2] - p.shape[0])) for p in pieces])
        )
    inputs_kept = []
    matrices = []
    for layer_index in range(L):
        base = L * ranks * model_width + layer_index * cut_three
        wide = weights
        if layer_index == 0:
            stream, wdowns = tie((stream, wdowns), *parts)
            parts[0].step()
            parts[2].step()
        wdown = wdowns[layer_index]
        matrices.append((wide, wdown, base))
        result, *saved = layer_forward(
            stream, layer_rows[layer_index], bias, wide, wdown, base, cut_one
        )
        inputs_kept.append((stream, saved))
        stream = result
        if layer_index == 0:
            stream = tie(stream, *parts)
            parts[1].step()
            parts[3].step()
    stream = tie(stream, *parts)
    final_gain = vectors[L * layer_width : L * layer_width + model_width]
    final_shift = vectors[L * layer_width + model_width :]
    finished = norm_apply(stream, final_gain, final_shift).astype(jnp.bfloat16)
    slot_hot = own_slots[:, None] == jnp.arange(length, dtype=jnp.int32)[None, :]
    rows = jnp.dot(
        slot_hot.astype(jnp.bfloat16), finished, preferred_element_type=jnp.float32
    ).astype(jnp.bfloat16)

    held = tie(place.gather_z(rows), *parts)
    parts[2].step()
    held = place.spread_halves(held, orders)
    held = tie(held, *parts)
    parts[3].step()
    group_rows = put_blocks(place, held).reshape(-1, model_width)
    parts = joined(parts)
    mine = parts[:, 0]
    theirs = place.swap(parts[:, 1], c=1)
    slice_low = put(place, [mine[None], theirs[None]], [(0, [0], everyone), (1, [0], everyone)], 1)
    slice_low = slice_low.reshape(model_width, slice_size)
    first_entry = place.v * shard_size + (place.z * 2 + place.c) * slice_size
    first_entry = first_entry.astype(jnp.int32).reshape(1)
    stats = head_forward(first_entry, group_rows, slice_low, all_targets)

    def combine(parts):
        top = functools.reduce(jnp.maximum, [p[0] for p in parts])
        return jnp.stack([top, tree_sum([p[1] * jnp.exp(p[0] - top) for p in parts])])

    whole = stats[:2]
    whole = combine([whole, place.swap(whole, c=1)])
    whole = combine([whole] + [place.swap(whole, v=m) for m in range(1, nv)])
    whole = combine([whole] + [place.swap(whole, z=m) for m in range(1, nz)])
    log_total = whole[0] + jnp.log(whole[1])
    own_total = lax.dynamic_slice_in_dim(
        log_total, ((place.z * 2 + place.c) * nv + place.v) * slot_count, slot_count
    )
    loss_local = jnp.sum(jnp.where(live, own_total, 0.0)) - jnp.sum(stats[2])
    count_local = jnp.sum(live.astype(jnp.float32))
    logits_low, rows_part = head_backward(
        first_entry, group_rows, log_total[None], slice_low, all_targets
    )
    rows_part = rows_part.reshape(nz, 2, nv, slot_count, model_width)
    rows_part = as_wide(pick(rows_part, place.c, 1)) + as_wide(
        place.swap(pick(rows_part, 1 - place.c, 1), c=1)
    )
    own_part = Held(rows_part)
    logits_low = tie(logits_low, own_part)
    rows_part = own_part.value
    head_grad = dot_first(group_rows, logits_low).astype(jnp.bfloat16)
    head_grad = head_grad.reshape(nz, 2, own_width, slice_size)
    head_parts = quarters(place, jnp.stack([pick(head_grad, place.z ^ m, 0) for m in range(nz)]))
    head_parts[0].step()
    head_parts[1].step()
    rows_part = tree_sum(
        [pick(rows_part, place.v, 1)]
        + [as_wide(place.swap(as_low(pick(rows_part, place.v ^ m, 1)), v=m)) for m in range(1, nv)]
    )
    rows_part = tie(rows_part, *head_parts)
    rows_grad = tree_sum(
        [pick(rows_part, place.z, 0)]
        + [as_wide(place.swap(as_low(pick(rows_part, place.z ^ m, 0)), z=m)) for m in range(1, nz)]
    )
    rows_grad = tie(rows_grad, *head_parts)
    finished_grad = lax.dot_general(
        slot_hot.astype(jnp.float32),
        rows_grad,
        (((0,), (0,)), ((), ())),
        precision=HIGHEST,
        preferred_element_type=jnp.float32,
    )

    ignored, final_pull = jax.vjp(norm_apply, stream, final_gain, final_shift)
    stream_grad, grad_final_gain, grad_final_shift = final_pull(finished_grad)
    vector_parts = [None] * L

    def slabs(grad):
        grad = grad.reshape(nz * nv, ranks, shard_rows, model_width)
        return [grad[:, k].reshape(nz * nv * shard_rows, model_width) for k in range(ranks)]

    def unslab(columns):
        return jnp.concatenate(
            [columns[:, k * model_width : (k + 1) * model_width] for k in range(ranks)]
        )

    summed = [None] * L
    for layer_index in reversed(range(L)):
        kept_stream, saved = inputs_kept[layer_index]
        wide, wdown, base = matrices[layer_index]
        normed, mixed, attended, middle, normed_two, hidden, active = saved
        for part in head_parts[2:] if layer_index == 1 else head_parts[1:2]:
            part.step()
        middle_grad, branch_grad, hidden_grad, late_vectors = mlp_backward(
            stream_grad, middle, hidden, layer_rows[layer_index], wide, wdown, base + cut_two
        )
        middle_grad, branch_grad, hidden_grad = tie(
            (middle_grad, branch_grad, hidden_grad), *head_parts
        )
        g_up = pair_grad(place, normed_two, hidden_grad)
        g_down = slabs(pair_grad_wide(place, active, branch_grad))
        g_mlp = Held([g_up] + g_down)
        middle_grad = tie(middle_grad, g_mlp, *head_parts)
        head_parts[0 if layer_index == 1 else 2].step()
        stream_grad, out_grad, mixed_grad, early_vectors = attn_backward(
            middle_grad, kept_stream, mixed, layer_rows[layer_index], bias, wide, base
        )
        stream_grad, out_grad, mixed_grad = tie((stream_grad, out_grad, mixed_grad), *head_parts)
        grads = Held(
            jnp.concatenate(
                g_mlp.value
                + [
                    pair_grad(place, normed, mixed_grad),
                    pair_grad(place, attended, out_grad),
                ],
                1,
            )
        )
        stream_grad = tie(stream_grad, grads, *head_parts)
        summed[layer_index] = lax.psum_scatter(
            grads.value, "vocab", scatter_dimension=0, tiled=True
        )
        vector_parts[layer_index] = (early_vectors, late_vectors)

    stream_grad, vector_parts = tie((stream_grad, vector_parts))
    vector_grads = [
        jnp.concatenate(
            [
                early_vectors[0, :model_width],
                early_vectors[1, :model_width],
                early_vectors[2, :model_width],
                early_vectors[2, model_width + head_size :],
                early_vectors[3, :model_width],
                late_vectors[0, :model_width],
                late_vectors[1, :model_width],
                late_vectors[2],
                late_vectors[3, :model_width],
            ]
        )
        for early_vectors, late_vectors in vector_parts
    ]
    sent = part_columns(place, stream_grad)
    sent = Traded(place, sent)
    sent.step()
    pos_grad = jnp.concatenate(
        [
            stream_grad[:trunk],
            jnp.sum(stream_grad[trunk : trunk + 4 * SEG].reshape(4, SEG, model_width), 0),
            jnp.sum(stream_grad[trunk + 4 * SEG :].reshape(8, SEG, model_width), 0),
        ]
    )
    vector_grad = jnp.concatenate(vector_grads + [grad_final_gain, grad_final_shift])
    flat = reduce_flat_core(place, vector_grad, pos_grad)
    flat, upper = tie((flat, summed[1]), sent, *head_parts)
    sent.step()
    flat = reduce_flat_plane(place, flat)
    flat, upper = tie((flat, upper), sent, *head_parts)
    sent = sent.rest()
    sent = [sent[:, 0], place.swap(sent[:, 1], c=1)]
    sent = Held([place.spread_v(a, order) for a, order in zip(sent, orders)])
    flat_own = Held(reduce_flat_z(place, flat))
    upper = tie(upper, flat_own)
    head_parts[3].step()
    bits = nz.bit_length() - 1
    upper = upper.reshape((2,) * bits + (-1, upper.shape[1]))
    for step in reversed(range(bits)):
        mine = (place.z >> step) % 2
        upper = as_wide(pick(upper, mine, 0)) + as_wide(
            place.swap(as_low(pick(upper, 1 - mine, 0)), z=1 << step)
        )
    lower, upper = tie((summed[0], upper), sent, flat_own, *head_parts)
    lower = lower.reshape(nz, -1, lower.shape[1])
    lower = [pick(lower, place.z, 0)] + [
        place.swap(pick(lower, place.z ^ m, 0), z=m) for m in range(1, nz)
    ]
    head_parts = joined(head_parts)
    mine = pick(head_parts, place.c, 1)
    theirs = place.swap(pick(head_parts, 1 - place.c, 1), c=1)
    head_grad = put(place, [mine[None], theirs[None]], [(0, [0], everyone), (1, [0], everyone)], 1)
    table_grad = add_rows(safe_ids, *[a.reshape(-1, LANES) for a in sent.value], head_grad)
    table_grad, lower = tie((table_grad, lower))
    summed = [tree_sum([as_wide(a) for a in lower]), upper]
    up_end = up_proj.shape[2]
    down_end = up_end + ranks * model_width
    grad_up = jnp.stack([a[:, :up_end] for a in summed])
    grad_down = jnp.stack([unslab(a[:, up_end:down_end]) for a in summed])
    grad_qkv = jnp.stack([a[:, down_end : down_end + cut_one] for a in summed])
    grad_out = jnp.stack([a[:, down_end + cut_one :] for a in summed])
    owned_squares = (
        jnp.sum(grad_qkv * grad_qkv)
        + jnp.sum(grad_out * grad_out)
        + jnp.sum(grad_up * grad_up)
        + jnp.sum(grad_down * grad_down)
        + jnp.sum(table_grad * table_grad)
        + jnp.sum(flat_own.value * flat_own.value)
    )
    sums, vector_grad, pos_grad = gather_flat(
        place,
        flat_own.value,
        jnp.stack([owned_squares, loss_local, count_local]),
        vector_grad,
        pos_grad,
    )
    loss_sum, loss_count = sums[1], sums[2]
    grad_norm = jnp.sqrt(sums[0])
    factor = jnp.minimum(1.0, CLIP_NORM / grad_norm)
    states = (
        (table.T, table_mean.T, table_square.T, table_grad, LEARN_RATE),
        (qkv_proj, qkv_mean, qkv_square, grad_qkv, LEARN_RATE),
        (out_proj, out_mean, out_square, grad_out, LEARN_RATE),
        (up_proj, up_mean, up_square, grad_up, LEARN_RATE),
        (down_proj, down_mean, down_square, grad_down, LEARN_RATE),
        (vectors, vec_mean, vec_square, vector_grad, RATE_VEC),
        (pos_table, pos_mean, pos_square, pos_grad, LEARN_RATE),
    )
    results = [loss_sum, loss_count, grad_norm]
    for weight, mean, square, grad, rate in states:
        results.extend(adam_update(weight, mean, square, grad * factor, rate))
    results[3:6] = [a.T for a in results[3:6]]
    return tuple(results)


def solution(mesh):
    chips = mesh.devices.reshape(-1, 2, mesh.shape["vocab"])
    mesh = jax.sharding.Mesh(chips, ALL)
    return jax.shard_map(
        per_device,
        mesh=mesh,
        in_specs=(
            P(ALL),
            P(ALL, None),
            P(ALL, None),
            P(ALL, None),
            P("vocab", ("z", "core")),
            P("vocab", ("z", "core")),
            P("vocab", ("z", "core")),
            P(None, ALL, None),
            P(None, ALL, None),
            P(None, ALL, None),
            P(None, ALL, None),
            P(None, ALL, None),
            P(None, ALL, None),
            P(None, ALL, None),
            P(None, ALL, None),
            P(None, ALL, None),
            P(None, ALL, None),
            P(None, ALL, None),
            P(None, ALL, None),
            P(),
            P(),
            P(),
            P(),
            P(),
            P(),
        ),
        out_specs=(
            P(),
            P(),
            P(),
            P("vocab", ("z", "core")),
            P("vocab", ("z", "core")),
            P("vocab", ("z", "core")),
            P(None, ALL, None),
            P(None, ALL, None),
            P(None, ALL, None),
            P(None, ALL, None),
            P(None, ALL, None),
            P(None, ALL, None),
            P(None, ALL, None),
            P(None, ALL, None),
            P(None, ALL, None),
            P(None, ALL, None),
            P(None, ALL, None),
            P(None, ALL, None),
            P(),
            P(),
            P(),
            P(),
            P(),
            P(),
        ),
        check_vma=False,
    )
```

```python
import functools

import jax
import jax.numpy as jnp
from jax import lax
from jax.experimental import pallas as pl
from jax.experimental.pallas import tpu as pltpu
from jax.sharding import PartitionSpec as P

L = 2
NSEG = 13
STEP = 10
SEG = 16


NORM_EPS = 1e-05
BETA_ONE = 0.9
BETA_TWO = 0.999
ADAM_EPS = 1e-08
LEARN_RATE = 0.1
RATE_VEC = 0.5
WEIGHT_DECAY = 0.1
CLIP_NORM = 0.1
HIGHEST = lax.Precision.HIGHEST
GELU_SCALE = 0.7978845608028654
GELU_CUBE = 0.044715
ALL = ("z", "core", "vocab")
ROWS_STEP = 2560
UNROLL = 16
HEAD_ROWS = 256
TURN = 512
MIB = 1024 * 1024
COST_SCALE = 1e15
LANES = 128


class Place:
    def __init__(self):
        self.nv = lax.axis_size("vocab")
        self.nz = lax.axis_size("z")
        self.count = self.nv * self.nz * 2
        self.v = lax.axis_index("vocab")
        self.z = lax.axis_index("z")
        self.c = lax.axis_index("core")
        self.where = jnp.stack([self.z, self.c, self.v]).astype(jnp.int32)
        self.core_alone = jnp.stack([self.z * 0, self.c, self.v * 0]).astype(jnp.int32)
        self.bits = [1 << i for i in range(self.nv.bit_length() - 1)]

    def swap(self, a, v=0, c=0, z=0):
        mask = (z * 2 + c) * self.nv + v
        return lax.ppermute(a, ALL, [(i, i ^ mask) for i in range(self.count)])

    def gather_z(self, a):
        return jnp.stack([a] + [self.swap(a, z=m) for m in range(1, self.nz)])

    def gather_v(self, a):
        return jnp.stack([a] + [self.swap(a, v=m) for m in range(1, self.nv)])

    def gather_c(self, a):
        return jnp.stack([a, self.swap(a, c=1)])

    def spread_v(self, a, order):
        masks = [0]
        held = a[None]
        for bit in order:
            held = jnp.concatenate([held, self.swap(held, v=bit)])
            masks = masks + [m ^ bit for m in masks]
        if masks == sorted(masks):
            return held
        return jnp.stack([held[masks.index(m)] for m in range(self.nv)])

    def spread_halves(self, held, orders):
        half = self.nz // 2
        return jnp.concatenate(
            [self.spread_v(held[:half], orders[0]), self.spread_v(held[half:], orders[1])], 1
        )

    def reduce_v(self, a, order, axis):
        left = list(reversed(self.bits))
        a = a.reshape(a.shape[:axis] + (2,) * len(left) + a.shape[axis + 1 :])
        for bit in order:
            at = axis + left.index(bit)
            a = lax.index_in_dim(a, 0, at, False) + self.swap(
                lax.index_in_dim(a, 1, at, False), v=bit
            )
            left.remove(bit)
        return a


def pick(a, index, axis):
    return lax.dynamic_index_in_dim(a, index, axis, False)


def tree_sum(terms):
    while len(terms) > 1:
        terms = [terms[i] + terms[i + 1] for i in range(0, len(terms), 2)]
    return terms[0]


def cost(seconds):
    return pl.CostEstimate(flops=int(seconds * COST_SCALE), transcendentals=0, bytes_accessed=0)


def put_kernel(slots, nv, where_ref, *refs):
    pieces, out = refs[: len(slots)], refs[-1]
    z, c = where_ref[0], where_ref[1]
    v = where_ref[2] if nv > 1 else 0
    for piece, (core, masks, z_masks) in zip(pieces, slots):
        for k, mask in enumerate(masks):
            for i, m in enumerate(z_masks):
                row = ((z ^ m) * 2 + (c ^ core)) * nv + (v ^ mask)
                out[row] = piece[k, i]


def put(place, pieces, slots, nv=None):
    nv = place.nv if nv is None else nv
    count = 2 * place.nz * nv
    rows, width = pieces[0].shape[2:]
    return pl.pallas_call(
        functools.partial(put_kernel, slots, nv),
        out_shape=jax.ShapeDtypeStruct((count, rows, width), pieces[0].dtype),
        in_specs=[pl.BlockSpec(memory_space=pltpu.SMEM)]
        + [pl.BlockSpec(memory_space=pltpu.VMEM)] * len(pieces),
        out_specs=pl.BlockSpec(memory_space=pltpu.VMEM),
        cost_estimate=cost(3e-6),
        compiler_params=pltpu.CompilerParams(vmem_limit_bytes=4 * count * rows * width + 4 * MIB),
    )(place.where, *pieces)


def owner_hot(where_ref, depth, rows, nv, nz, order):
    part = rows // (nv * nz)
    column = lax.broadcasted_iota(jnp.int32, (1, rows), 1)
    block = jnp.zeros((1, rows), jnp.int32)
    for k in range(1, nv * nz):
        block = block + jnp.where(column >= k * part, 1, 0)
    apart = jnp.zeros((1, rows), jnp.int32)
    for k, bit in enumerate(reversed(order)):
        apart = apart + jnp.where((block & (nz << k)) != 0, bit, 0)
    owner = ((block & (nz - 1)) ^ where_ref[0]) * 2 + where_ref[1]
    owner = owner * nv + (apart ^ where_ref[2])
    row = owner * part + column - block * part
    return (lax.broadcasted_iota(jnp.int32, (depth, rows), 0) == row).astype(jnp.bfloat16)


def pair_kernel(
    nv, nz, order, where_ref, x_ref, other_ref, y_ref, y_other_ref, out_ref, left_ref, left_other_ref
):
    @pl.when(pl.program_id(0) == 0)
    def _():
        hot = owner_hot(where_ref, x_ref.shape[1], left_ref.shape[1], nv, nz, order)
        left_ref[...] = jnp.dot(x_ref[...], hot, preferred_element_type=jnp.float32).astype(
            jnp.bfloat16
        )
        left_other_ref[...] = jnp.dot(
            other_ref[...], hot, preferred_element_type=jnp.float32
        ).astype(jnp.bfloat16)

    out_ref[...] = (
        dot_first(left_ref[...], y_ref[...]) + dot_first(left_other_ref[...], y_other_ref[...])
    ).astype(jnp.bfloat16)


def pair_grad(place, x, y):
    length, depth = x.shape
    rows, width = depth // 2, y.shape[1]
    block = 768 if width % 768 == 0 else width
    whole = pl.BlockSpec((length, depth), lambda i: (0, 0))
    part = pl.BlockSpec((length, block), lambda i: (0, i))
    return pl.pallas_call(
        functools.partial(pair_kernel, place.nv, place.nz, list(reversed(place.bits))),
        out_shape=jax.ShapeDtypeStruct((rows, width), jnp.bfloat16),
        grid=(width // block,),
        in_specs=[pl.BlockSpec(memory_space=pltpu.SMEM), whole, whole, part, part],
        out_specs=pl.BlockSpec((rows, block), lambda i: (0, i)),
        scratch_shapes=[pltpu.VMEM((length, rows), jnp.bfloat16)] * 2,
        cost_estimate=cost(5e-6),
        compiler_params=pltpu.CompilerParams(vmem_limit_bytes=14 * MIB),
    )(place.core_alone, x, place.swap(x, c=1), y, place.swap(y, c=1))


def wide_kernel(nv, order, where_ref, x_ref, other_ref, y_ref, y_other_ref, out_ref):
    total = dot_first(x_ref[...], y_ref[...]) + dot_first(other_ref[...], y_other_ref[...])
    rows = total.shape[0] // nv
    for v in range(nv):
        apart = where_ref[2] ^ v
        position = 0
        for bit in order:
            position = position * 2 + jnp.where((apart & bit) != 0, 1, 0)
        out_ref[position, 0] = total[v * rows : (v + 1) * rows].astype(jnp.bfloat16)


def pair_grad_wide(place, x, y):
    length, depth = x.shape
    width = y.shape[1]
    block = depth // (2 * place.nz)
    rows = block // place.nv
    other = place.swap(x, c=1)
    if block % 128 == 0:
        part = pl.BlockSpec((length, block), lambda i, where: (0, 2 * i + where[1]))
    else:
        x, other = (a.reshape(length, -1, block).transpose(1, 0, 2) for a in (x, other))
        part = pl.BlockSpec((None, length, block), lambda i, where: (2 * i + where[1], 0, 0))
    whole = pl.BlockSpec((length, width), lambda i, where: (0, 0))
    shape, block_shape = (place.nv, place.nz, rows, width), (place.nv, 1, rows, width)
    where_out = lambda i, where: (0, i ^ where[0], 0, 0)
    return pl.pallas_call(
        functools.partial(wide_kernel, place.nv, list(reversed(place.bits))),
        out_shape=jax.ShapeDtypeStruct(shape, jnp.bfloat16),
        grid_spec=pltpu.PrefetchScalarGridSpec(
            num_scalar_prefetch=1,
            grid=(place.nz,),
            in_specs=[part, part, whole, whole],
            out_specs=pl.BlockSpec(block_shape, where_out),
        ),
        cost_estimate=cost(5e-6),
        compiler_params=pltpu.CompilerParams(vmem_limit_bytes=14 * MIB),
    )(place.core_alone, x, other, y, place.swap(y, c=1)).reshape(depth // 2, width)


def tie(main, *steps):
    main, values = lax.optimization_barrier((main, [s.value for s in steps]))
    for s, value in zip(steps, values):
        s.value = value
    return main


class Traded:
    def __init__(self, place, value):
        self.place = place
        self.value = value

    def step(self):
        place, a = self.place, self.value
        self.value = [a[0]] + [place.swap(a[m], z=m) for m in range(1, place.nz)]

    def rest(self):
        return jnp.stack(self.value)


def quarters(place, value):
    part = value.shape[-1] // 4
    return [Traded(place, value[..., k * part : (k + 1) * part]) for k in range(4)]


def spread_z(place, a):
    a = a.reshape(place.nz, -1, a.shape[1])
    return [pick(a, place.z, 0)] + [
        place.swap(pick(a, place.z ^ m, 0), z=m) for m in range(1, place.nz)
    ]


def joined(trades):
    return jnp.concatenate([t.rest() for t in trades], -1)


class Held:
    def __init__(self, value):
        self.value = value


def as_wide(a):
    return a.astype(jnp.float32)


def as_low(a):
    return a.astype(jnp.bfloat16)


def reduce_flat_core(place, vector, table):
    length = vector.shape[0]
    first = -(-length // 1024) * 8
    second = table.size // 128
    rows = -(-(first + second) // (place.count * 8)) * 8
    a = jnp.concatenate(
        [jnp.pad(vector, (0, first * 128 - length)).reshape(first, 128), table.reshape(second, 128)]
    )
    a = jnp.pad(a, ((0, place.count * rows - first - second), (0, 0)))
    a = a.reshape(place.nz, 2, place.nv, rows, 128)
    return pick(a, place.c, 1) + place.swap(pick(a, 1 - place.c, 1), c=1)


def reduce_flat_plane(place, a):
    bits = list(reversed(place.bits))
    a = a.reshape((place.nz,) + (2,) * len(bits) + a.shape[2:])
    for bit in bits:
        mine = (place.v // bit) % 2
        a = pick(a, mine, 1) + place.swap(pick(a, 1 - mine, 1), v=bit)
    return a


def reduce_flat_z(place, a):
    count = place.nz.bit_length() - 1
    a = a.reshape((2,) * count + a.shape[1:])
    for step in reversed(range(count)):
        mine = (place.z >> step) % 2
        a = pick(a, mine, 0) + place.swap(pick(a, 1 - mine, 0), z=1 << step)
    return a


def unslab_kernel(slabs_ref, out_ref):
    ranks = out_ref.shape[1] // slabs_ref.shape[1]
    rows, width = slabs_ref.shape[1], out_ref.shape[2]
    for k in range(ranks):
        out_ref[:, k * rows : (k + 1) * rows, :] = slabs_ref[:, :, k * width : (k + 1) * width]


def unslab_rows(place, gathered, ranks, width, layer_index):
    count, total = place.count, ranks * width
    rows = gathered.shape[0] // count
    if rows % 8:
        slabs = gathered[:, layer_index * total : (layer_index + 1) * total]
        slabs = slabs.reshape(count, rows, ranks, width)
        return slabs.transpose(0, 2, 1, 3).reshape(-1, width)
    return pl.pallas_call(
        unslab_kernel,
        out_shape=jax.ShapeDtypeStruct((count, rows * ranks, width), gathered.dtype),
        grid=(count // 4,),
        in_specs=[pl.BlockSpec((4, rows, total), lambda i: (i, 0, layer_index))],
        out_specs=pl.BlockSpec((4, rows * ranks, width), lambda i: (i, 0, 0)),
        cost_estimate=cost(7e-6),
    )(gathered.reshape(count, rows, -1)).reshape(-1, width)


def gather_flat(place, own, scalars, vector, table):
    length, rows = vector.shape[0], own.shape[0]
    first, second = -(-length // 1024) * 8, table.size // 128
    own = jnp.concatenate([own, jnp.pad(scalars[None], ((0, 7), (0, 128 - scalars.shape[0])))])
    whole = gather_blocks(place, own)
    scalars = jnp.sum(whole[:, rows, : scalars.shape[0]], 0)
    whole = whole[:, :rows].reshape(-1, 128)
    return (
        scalars,
        whole[:first].reshape(-1)[:length],
        whole[first : first + second].reshape(table.shape),
    )


def put_blocks(place, held):
    everyone = list(range(place.nz))
    masks = list(range(place.nv))
    return put(place, [held, place.swap(held, c=1)], [(0, masks, everyone), (1, masks, everyone)])


def gather_blocks(place, block):
    return put_blocks(place, place.gather_v(place.gather_z(block)))


def column_hot(where_ref, part, width, total):
    first = (part ^ (where_ref[0] * 2 + where_ref[1])) * width
    rows = lax.broadcasted_iota(jnp.int32, (width, total), 0) + first
    return (rows == lax.broadcasted_iota(jnp.int32, (width, total), 1)).astype(jnp.bfloat16)


def embed_kernel(where_ref, table_ref, *refs):
    pieces, out_ref = refs[:-1], refs[-1]
    total_width = out_ref.shape[1]
    width = total_width // (2 * len(pieces))
    total = jnp.zeros(out_ref.shape, jnp.float32)
    for m, piece in enumerate(pieces):
        for c in range(2):
            hot = column_hot(where_ref, 2 * m + c, width, total_width)
            total = total + jnp.dot(
                piece[c, :, :width], hot, preferred_element_type=jnp.float32
            )
    out_ref[...] = total
    trunk = 8 * SEG
    out_ref[:trunk, :] += table_ref[:trunk, :]
    for k in range(12):
        at = trunk + k * SEG
        row = trunk if k < 4 else trunk + SEG
        out_ref[at : at + SEG, :] += table_ref[row : row + SEG, :]


def embed(place, pieces, table):
    length, width = pieces[0].shape[1:]
    return pl.pallas_call(
        embed_kernel,
        out_shape=jax.ShapeDtypeStruct((length, table.shape[1]), jnp.float32),
        in_specs=[pl.BlockSpec(memory_space=pltpu.SMEM)]
        + [pl.BlockSpec(memory_space=pltpu.VMEM)] * (1 + len(pieces)),
        out_specs=pl.BlockSpec(memory_space=pltpu.VMEM),
        cost_estimate=cost(1.7e-6),
        compiler_params=pltpu.CompilerParams(vmem_limit_bytes=16 * MIB),
    )(place.where, table, *pieces)


def part_kernel(where_ref, grad_ref, out_ref):
    grad = grad_ref[...].astype(jnp.bfloat16)
    nz = out_ref.shape[0]
    width = grad.shape[1] // (2 * nz)
    out_ref[...] = jnp.zeros_like(out_ref)
    for m in range(nz):
        for c in range(2):
            hot = column_hot(where_ref, 2 * m + c, width, grad.shape[1])
            out_ref[m, c, :, :width] = dot_last(grad, hot).astype(jnp.bfloat16)


def part_columns(place, grad):
    length, total = grad.shape
    return pl.pallas_call(
        part_kernel,
        out_shape=jax.ShapeDtypeStruct((place.nz, 2, length, LANES), jnp.bfloat16),
        in_specs=[
            pl.BlockSpec(memory_space=pltpu.SMEM),
            pl.BlockSpec(memory_space=pltpu.VMEM),
        ],
        out_specs=pl.BlockSpec(memory_space=pltpu.VMEM),
        cost_estimate=cost(1.8e-6),
        compiler_params=pltpu.CompilerParams(vmem_limit_bytes=16 * MIB),
    )(place.where, grad)


def turned(value, axis):
    size = max(value.shape)
    same = lax.broadcasted_iota(jnp.int32, (size, size), 0) == lax.broadcasted_iota(
        jnp.int32, (size, size), 1
    )
    return jnp.sum(jnp.where(same, value, jnp.zeros((), value.dtype)), axis, keepdims=True)


def hits(first_ref, targets_ref, shape):
    column = turned(targets_ref[...], 1) - first_ref[0]
    return column == lax.broadcasted_iota(jnp.int32, shape, 1)


def logits_kernel(first_ref, rows_ref, table_ref, targets_ref, stats_ref):
    logits = jnp.dot(rows_ref[...], table_ref[...], preferred_element_type=jnp.float32)
    top = jnp.max(logits, 1, keepdims=True)
    exps = jnp.exp(logits - top)
    picked = jnp.where(hits(first_ref, targets_ref, logits.shape), logits, 0.0)
    stats_ref[0:1, :] = turned(top, 0)
    stats_ref[1:2, :] = turned(jnp.sum(exps, 1, keepdims=True), 0)
    stats_ref[2:3, :] = turned(jnp.sum(picked, 1, keepdims=True), 0)


def head_forward(first, rows, table, targets):
    count, width = rows.shape
    size = table.shape[1]
    return pl.pallas_call(
        logits_kernel,
        out_shape=jax.ShapeDtypeStruct((3, count), jnp.float32),
        grid=(count // HEAD_ROWS,),
        in_specs=[
            pl.BlockSpec(memory_space=pltpu.SMEM),
            pl.BlockSpec((HEAD_ROWS, width), lambda i: (i, 0)),
            pl.BlockSpec((width, size), lambda i: (0, 0)),
            pl.BlockSpec((1, HEAD_ROWS), lambda i: (0, i)),
        ],
        out_specs=pl.BlockSpec((3, HEAD_ROWS), lambda i: (0, i)),
        cost_estimate=cost(11.6e-6),
        compiler_params=pltpu.CompilerParams(vmem_limit_bytes=24 * MIB),
    )(first, rows, table, targets)


def slopes_kernel(first_ref, rows_in_ref, total_ref, table_ref, targets_ref, slopes_ref, rows_ref):
    logits = jnp.dot(rows_in_ref[...], table_ref[...], preferred_element_type=jnp.float32)
    exps = jnp.exp(logits - turned(total_ref[...], 1))
    hit = hits(first_ref, targets_ref, exps.shape)
    alive = turned(targets_ref[...], 1) >= 0
    slopes = jnp.where(alive, exps - jnp.where(hit, 1.0, 0.0), 0.0).astype(jnp.bfloat16)
    slopes_ref[...] = slopes
    rows_ref[...] = dot_last(slopes, table_ref[...]).astype(jnp.bfloat16)


def head_backward(first, rows, total, table, targets):
    count, width = rows.shape
    size = table.shape[1]
    return pl.pallas_call(
        slopes_kernel,
        out_shape=(
            jax.ShapeDtypeStruct((count, size), jnp.bfloat16),
            jax.ShapeDtypeStruct((count, width), jnp.bfloat16),
        ),
        grid=(count // HEAD_ROWS,),
        in_specs=[
            pl.BlockSpec(memory_space=pltpu.SMEM),
            pl.BlockSpec((HEAD_ROWS, width), lambda i: (i, 0)),
            pl.BlockSpec((1, HEAD_ROWS), lambda i: (0, i)),
            pl.BlockSpec((width, size), lambda i: (0, 0)),
            pl.BlockSpec((1, HEAD_ROWS), lambda i: (0, i)),
        ],
        out_specs=(
            pl.BlockSpec((HEAD_ROWS, size), lambda i: (i, 0)),
            pl.BlockSpec((HEAD_ROWS, width), lambda i: (i, 0)),
        ),
        cost_estimate=cost(16e-6),
        compiler_params=pltpu.CompilerParams(vmem_limit_bytes=24 * MIB),
    )(first, rows, total, table, targets)


def cut_kernel(where_ref, columns_ref, out_ref):
    out_ref[0, 0] = columns_ref[...].astype(out_ref.dtype)


def cut(place, columns):
    width, size = columns.shape
    part = size // (2 * place.nz)
    if part % 128:
        order = jnp.arange(2 * place.nz) ^ (place.z * 2 + place.c)
        parts = columns.astype(jnp.bfloat16).reshape(width, 2 * place.nz, part).transpose(1, 0, 2)
        return jnp.take(parts, order, axis=0).reshape(place.nz, 2, width, part)
    return pl.pallas_call(
        cut_kernel,
        out_shape=jax.ShapeDtypeStruct((place.nz, 2, width, part), jnp.bfloat16),
        grid_spec=pltpu.PrefetchScalarGridSpec(
            num_scalar_prefetch=1,
            grid=(2 * place.nz,),
            in_specs=[
                pl.BlockSpec((width, part), lambda i, where: (0, i ^ (where[0] * 2 + where[1])))
            ],
            out_specs=pl.BlockSpec((1, 1, width, part), lambda i, where: (i // 2, i % 2, 0, 0)),
        ),
        cost_estimate=cost(7e-6),
    )(place.where, columns)


def find_kernel(ids_ref, columns_ref, out_ref, rows_ref, found_ref):
    size = columns_ref.shape[1]

    @pl.when(pl.program_id(0) == 0)
    def _():
        def turn(i, carry):
            at = pl.multiple_of(i * TURN, TURN)
            part = columns_ref[:, pl.ds(at, TURN)].astype(jnp.bfloat16).astype(jnp.float32)
            rows_ref[pl.ds(at, TURN), : part.shape[0]] = part.T
            return carry

        rows_ref[:, columns_ref.shape[0] :] = jnp.zeros(
            (rows_ref.shape[0], LANES - columns_ref.shape[0]), jnp.float32
        )

        lax.fori_loop(0, size // TURN, turn, 0)
        rows_ref[pl.ds(size, 8), :] = jnp.zeros((8, rows_ref.shape[1]), jnp.float32)

    first = pl.program_id(0) * out_ref.shape[0]

    def body(i, carry):
        for u in range(UNROLL):
            t = i * UNROLL + u
            found_ref[pl.ds(t, 1), :] = rows_ref[pl.ds(ids_ref[first + t], 1), :]
        return carry

    lax.fori_loop(0, out_ref.shape[0] // UNROLL, body, 0)
    out_ref[...] = found_ref[...].astype(out_ref.dtype)


def find_rows(ids, columns):
    width, size = columns.shape
    return pl.pallas_call(
        find_kernel,
        out_shape=jax.ShapeDtypeStruct((ids.shape[0], LANES), jnp.bfloat16),
        grid_spec=pltpu.PrefetchScalarGridSpec(
            num_scalar_prefetch=1,
            grid=(ids.shape[0] // ROWS_STEP,),
            in_specs=[pl.BlockSpec(memory_space=pltpu.VMEM)],
            out_specs=pl.BlockSpec((ROWS_STEP, LANES), lambda i, ids: (i, 0)),
            scratch_shapes=[
                pltpu.VMEM((size + 8, LANES), jnp.float32),
                pltpu.VMEM((ROWS_STEP, LANES), jnp.float32),
            ],
        ),
        cost_estimate=cost(18e-6),
        compiler_params=pltpu.CompilerParams(vmem_limit_bytes=24 * MIB),
    )(ids, columns)


def add_kernel(ids_ref, low_ref, more_ref, head_ref, out_ref, rows_ref, *parts):
    step = pl.program_id(0)
    first = step * rows_ref.shape[0]
    size = out_ref.shape[1]
    early = step < pl.num_programs(0) // 2
    rows_ref[...] = jnp.where(early, low_ref[...], more_ref[...]).astype(jnp.float32)

    @pl.when(step == 0)
    def _():
        for part in parts:
            part[...] = jnp.zeros_like(part)

    def body(i, carry):
        for u in range(UNROLL):
            t = i * UNROLL + u
            part = parts[u % len(parts)]
            where = pl.ds(ids_ref[first + t], 1)
            part[where, :] = part[where, :] + rows_ref[pl.ds(t, 1), :]
        return carry

    lax.fori_loop(0, rows_ref.shape[0] // UNROLL, body, 0)

    @pl.when(step == pl.num_programs(0) - 1)
    def _():
        def turn(i, carry):
            at = pl.ds(pl.multiple_of(i * TURN, TURN), TURN)
            total = tree_sum([part[at, :] for part in parts])
            part = head_ref.shape[2]
            head = head_ref[i * TURN // part, :, pl.ds(pl.multiple_of(i * TURN % part, TURN), TURN)]
            out_ref[:, at] = total.T[: out_ref.shape[0]] + head.astype(jnp.float32)
            return carry

        lax.fori_loop(0, size // TURN, turn, 0)


def add_rows(ids, rows, more, head):
    width, size = head.shape[1], head.shape[0] * head.shape[2]
    if head.shape[2] % TURN:
        head = head.transpose(1, 0, 2).reshape(1, width, size)
    steps = rows.shape[0] // ROWS_STEP
    return pl.pallas_call(
        add_kernel,
        out_shape=jax.ShapeDtypeStruct((width, size), jnp.float32),
        grid_spec=pltpu.PrefetchScalarGridSpec(
            num_scalar_prefetch=1,
            grid=(ids.shape[0] // ROWS_STEP,),
            in_specs=[
                pl.BlockSpec((ROWS_STEP, LANES), lambda i, ids: (jnp.minimum(i, steps - 1), 0)),
                pl.BlockSpec((ROWS_STEP, LANES), lambda i, ids: (jnp.maximum(i - steps, 0), 0)),
                pl.BlockSpec(memory_space=pltpu.VMEM),
            ],
            out_specs=pl.BlockSpec(memory_space=pltpu.VMEM),
            scratch_shapes=[pltpu.VMEM((ROWS_STEP, LANES), jnp.float32)]
            + [pltpu.VMEM((size + 8, LANES), jnp.float32)] * 4,
        ),
        cost_estimate=cost(25e-6),
        compiler_params=pltpu.CompilerParams(vmem_limit_bytes=40 * MIB),
    )(ids, rows, more, head)


def norm_apply(stream, gain, shift):
    center = stream - jnp.mean(stream, -1, keepdims=True)
    spread = jnp.mean(center * center, -1, keepdims=True)
    return center * lax.rsqrt(spread + NORM_EPS) * gain + shift


def norm_back(stream, gain, grad):
    center = stream - jnp.mean(stream, -1, keepdims=True)
    scale = lax.rsqrt(jnp.mean(center * center, -1, keepdims=True) + NORM_EPS)
    unit = center * scale
    inner = grad * gain
    part = inner - jnp.mean(inner, -1, keepdims=True)
    part = scale * (part - unit * jnp.mean(inner * unit, -1, keepdims=True))
    return part, jnp.sum(grad * unit, 0, keepdims=True), jnp.sum(grad, 0, keepdims=True)


def gelu_parts(value):
    inner = GELU_SCALE * (value + GELU_CUBE * value * value * value)
    bend = jnp.tanh(inner)
    half = 0.5 * (1.0 + bend)
    slope = GELU_SCALE * (1.0 + 3.0 * GELU_CUBE * value * value)
    return value * half, half + 0.5 * value * (1.0 - bend * bend) * slope


def split_layer(vector_row, model_width, head_size, hidden_width):
    widths = [model_width] * 3 + [head_size] + [model_width] * 3 + [hidden_width, model_width]
    pieces = []
    offset = 0
    for width in widths:
        pieces.append(vector_row[offset : offset + width])
        offset += width
    return pieces


def tree_layout(total, seg_len):
    places = jnp.arange(total, dtype=jnp.int32)
    trunk = 8 * seg_len
    beyond = jnp.maximum(places - trunk, 0) // seg_len
    segment = jnp.where(places < trunk, 0, 1 + beyond)
    offset = places - trunk - beyond * seg_len
    path_depth = jnp.where(
        places < trunk, places, jnp.where(segment <= 4, trunk + offset, trunk + seg_len + offset)
    )
    return (places, segment, path_depth)


def tree_mask(parent_row, places, segment, count):
    labels = jnp.arange(count, dtype=jnp.int32)
    parent_hot = (parent_row[:, None] == labels[None, :]).astype(jnp.float32)
    grand_hot = jnp.dot(parent_hot, parent_hot, precision=HIGHEST)
    ancestor = jnp.eye(count, dtype=jnp.float32) + parent_hot + grand_hot
    seg_hot = (segment[:, None] == labels[None, :]).astype(jnp.float32)
    reach = jnp.dot(jnp.dot(seg_hot, ancestor, precision=HIGHEST), seg_hot.T, precision=HIGHEST)
    return (reach > 0.5) & (places[None, :] <= places[:, None])


def dot_first(left, right):
    return lax.dot_general(
        left, right, (((0,), (0,)), ((), ())), preferred_element_type=jnp.float32
    )


def dot_last(left, right):
    return lax.dot_general(
        left, right, (((1,), (1,)), ((), ())), preferred_element_type=jnp.float32
    )


def column_sum(grad_low):
    return jnp.sum(grad_low.astype(jnp.float32), 0)


def fetch(copies):
    for copy in copies:
        copy.start()
    return copies


def head_probs(mixed_ref, bias, h, keys, size, model_width):
    queries = mixed_ref[:, h * size : (h + 1) * size]
    scores = dot_last(keys, queries) * size ** (-0.5) + bias
    exps = jnp.exp(scores - jnp.max(scores, 0, keepdims=True))
    return queries, exps * (1.0 / jnp.sum(exps, 0, keepdims=True))


def forward_kernel(
    base,
    stream_ref,
    row_ref,
    bias_ref,
    wide_ref,
    down_ref,
    result_ref,
    normed_ref,
    mixed_ref,
    attended_ref,
    middle_ref,
    normed_two_ref,
    hidden_ref,
    active_ref,
    qkv_low,
    out_low,
    up_low,
    down_low,
    sems,
):
    model_width = stream_ref.shape[1]
    size = (qkv_low.shape[1] - model_width) // 2
    cuts = (qkv_low.shape[1], qkv_low.shape[1] + model_width)
    copies = fetch(
        [
            pltpu.make_async_copy(wide_ref.at[:, pl.ds(base, cuts[0])], qkv_low, sems.at[0]),
            pltpu.make_async_copy(
                wide_ref.at[:, pl.ds(base + cuts[0], model_width)], out_low, sems.at[1]
            ),
            pltpu.make_async_copy(
                wide_ref.at[:, pl.ds(base + cuts[1], up_low.shape[1])], up_low, sems.at[2]
            ),
            pltpu.make_async_copy(down_ref, down_low, sems.at[3]),
        ]
    )

    def row(k, width=model_width):
        return row_ref[k : k + 1, :width]

    stream = stream_ref[...]
    normed = norm_apply(stream, row(0), row(1)).astype(jnp.bfloat16)
    normed_ref[...] = normed
    copies[0].wait()
    mixed = jnp.dot(normed, qkv_low[...], preferred_element_type=jnp.float32)
    mixed = (mixed + row(9, mixed.shape[1])).astype(jnp.bfloat16)
    mixed_ref[...] = mixed
    keys, values = mixed[:, model_width : model_width + size], mixed[:, model_width + size :]
    for h in range(model_width // size):
        ignored, probs = head_probs(mixed_ref, bias_ref[...], h, keys, size, model_width)
        attended_ref[:, h * size : (h + 1) * size] = dot_first(
            probs.astype(jnp.bfloat16), values
        ).astype(jnp.bfloat16)
    copies[1].wait()
    middle = stream + jnp.dot(
        attended_ref[...], out_low[...], preferred_element_type=jnp.float32
    )
    middle = middle + row(4)
    middle_ref[...] = middle
    normed_two = norm_apply(middle, row(5), row(6)).astype(jnp.bfloat16)
    normed_two_ref[...] = normed_two
    copies[2].wait()
    copies[3].wait()
    total = middle + row(8)
    for k in range(up_low.shape[1] // model_width):
        at = slice(k * model_width, (k + 1) * model_width)
        hidden = jnp.dot(normed_two, up_low[:, at], preferred_element_type=jnp.float32)
        hidden = hidden + row_ref[7:8, at]
        hidden_ref[:, at] = hidden
        active = gelu_parts(hidden)[0].astype(jnp.bfloat16)
        active_ref[:, at] = active
        total = total + jnp.dot(active, down_low[at, :], preferred_element_type=jnp.float32)
    result_ref[...] = total


def shape_of(shape, kind):
    return jax.ShapeDtypeStruct(shape, kind)


VMEM = pl.BlockSpec(memory_space=pltpu.VMEM)
ANY = pl.BlockSpec(memory_space=pltpu.HBM)


def layer_forward(stream, row, bias, wide, down, base, row_width):
    length, model_width = stream.shape
    hidden_width = down.shape[0]
    mixed_width = row_width
    f32, low = jnp.float32, jnp.bfloat16
    return pl.pallas_call(
        functools.partial(forward_kernel, base),
        out_shape=(
            shape_of((length, model_width), f32),
            shape_of((length, model_width), low),
            shape_of((length, mixed_width), low),
            shape_of((length, model_width), low),
            shape_of((length, model_width), f32),
            shape_of((length, model_width), low),
            shape_of((length, hidden_width), f32),
            shape_of((length, hidden_width), low),
        ),
        in_specs=[VMEM, VMEM, VMEM, ANY, ANY],
        out_specs=(VMEM,) * 8,
        scratch_shapes=[
            pltpu.VMEM((model_width, mixed_width), low),
            pltpu.VMEM((model_width, model_width), low),
            pltpu.VMEM((model_width, hidden_width), low),
            pltpu.VMEM((hidden_width, model_width), low),
            pltpu.SemaphoreType.DMA((4,)),
        ],
        cost_estimate=cost(12e-6),
        compiler_params=pltpu.CompilerParams(vmem_limit_bytes=46 * MIB),
    )(stream, row, bias, wide, down)


def mlp_kernel(
    first,
    grad_ref,
    middle_ref,
    hidden_ref,
    row_ref,
    wide_ref,
    down_ref,
    middle_grad_ref,
    branch_ref,
    hidden_grad_ref,
    vector_ref,
    up_low,
    down_low,
    sems,
):
    model_width = grad_ref.shape[1]
    start = first
    copies = fetch(
        [
            pltpu.make_async_copy(down_ref, down_low, sems.at[0]),
            pltpu.make_async_copy(
                wide_ref.at[:, start : start + up_low.shape[1]], up_low, sems.at[1]
            ),
        ]
    )
    grad = grad_ref[...]
    branch = grad.astype(jnp.bfloat16)
    branch_ref[...] = branch
    vector_ref[...] = jnp.zeros_like(vector_ref)
    vector_ref[3:4, :model_width] = jnp.sum(branch.astype(jnp.float32), 0, keepdims=True)
    copies[0].wait()
    copies[1].wait()
    total = jnp.zeros_like(grad)
    for k in range(up_low.shape[1] // model_width):
        at = slice(k * model_width, (k + 1) * model_width)
        slope = gelu_parts(hidden_ref[:, at])[1]
        hidden_grad = (slope * dot_last(branch, down_low[at, :])).astype(jnp.bfloat16)
        hidden_grad_ref[:, at] = hidden_grad
        vector_ref[2:3, at] = jnp.sum(hidden_grad.astype(jnp.float32), 0, keepdims=True)
        total = total + dot_last(hidden_grad, up_low[:, at])
    part, gain_grad, shift_grad = norm_back(middle_ref[...], row_ref[5:6, :model_width], total)
    vector_ref[0:1, :model_width] = gain_grad
    vector_ref[1:2, :model_width] = shift_grad
    middle_grad_ref[...] = grad + part


def mlp_backward(grad, middle, hidden, row, wide, down, first):
    length, model_width = grad.shape
    hidden_width = down.shape[0]
    f32, low = jnp.float32, jnp.bfloat16
    return pl.pallas_call(
        functools.partial(mlp_kernel, first),
        out_shape=(
            shape_of((length, model_width), f32),
            shape_of((length, model_width), low),
            shape_of((length, hidden_width), low),
            shape_of((8, hidden_width), f32),
        ),
        in_specs=[VMEM, VMEM, VMEM, VMEM, ANY, ANY],
        out_specs=(VMEM,) * 4,
        scratch_shapes=[
            pltpu.VMEM((model_width, hidden_width), low),
            pltpu.VMEM((hidden_width, model_width), low),
            pltpu.SemaphoreType.DMA((2,)),
        ],
        cost_estimate=cost(6.5e-6),
        compiler_params=pltpu.CompilerParams(vmem_limit_bytes=46 * MIB),
    )(grad, middle, hidden, row, wide, down)


def attn_kernel(
    base,
    middle_grad_ref,
    stream_ref,
    mixed_ref,
    row_ref,
    bias_ref,
    wide_ref,
    stream_grad_ref,
    out_grad_ref,
    mixed_grad_ref,
    vector_ref,
    qkv_low,
    out_low,
    attended_ref,
    sems,
):
    model_width = stream_ref.shape[1]
    size = (qkv_low.shape[1] - model_width) // 2
    cut = qkv_low.shape[1]
    copies = fetch(
        [
            pltpu.make_async_copy(
                wide_ref.at[:, pl.ds(base + cut, model_width)], out_low, sems.at[0]
            ),
            pltpu.make_async_copy(wide_ref.at[:, pl.ds(base, cut)], qkv_low, sems.at[1]),
        ]
    )
    middle_grad = middle_grad_ref[...]
    out_grad = middle_grad.astype(jnp.bfloat16)
    out_grad_ref[...] = out_grad
    vector_ref[...] = jnp.zeros_like(vector_ref)
    vector_ref[3:4, :model_width] = jnp.sum(out_grad.astype(jnp.float32), 0, keepdims=True)
    copies[0].wait()
    attended_ref[...] = dot_last(out_grad, out_low[...]).astype(jnp.bfloat16)
    keys = mixed_ref[:, model_width : model_width + size]
    values = mixed_ref[:, model_width + size :]
    keys_grad = jnp.zeros(keys.shape, jnp.float32)
    values_grad = jnp.zeros(values.shape, jnp.float32)
    for h in range(model_width // size):
        at = slice(h * size, (h + 1) * size)
        queries, probs = head_probs(mixed_ref, bias_ref[...], h, keys, size, model_width)
        grad = attended_ref[:, at]
        values_grad = values_grad + jnp.dot(
            probs.astype(jnp.bfloat16), grad, preferred_element_type=jnp.float32
        )
        probs_grad = dot_last(values, grad)
        scores_grad = probs * (probs_grad - jnp.sum(probs * probs_grad, 0, keepdims=True))
        scores_grad = scores_grad.astype(jnp.bfloat16)
        keys_grad = keys_grad + jnp.dot(
            scores_grad, queries, preferred_element_type=jnp.float32
        )
        mixed_grad_ref[:, at] = (dot_first(scores_grad, keys) * size ** (-0.5)).astype(jnp.bfloat16)
    mixed_grad_ref[:, model_width : model_width + size] = (keys_grad * size ** (-0.5)).astype(
        jnp.bfloat16
    )
    mixed_grad_ref[:, model_width + size :] = values_grad.astype(jnp.bfloat16)
    mixed_grad = mixed_grad_ref[...]
    vector_ref[2:3, :] = jnp.sum(mixed_grad.astype(jnp.float32), 0, keepdims=True)
    copies[1].wait()
    total = dot_last(mixed_grad, qkv_low[...])
    part, gain_grad, shift_grad = norm_back(stream_ref[...], row_ref[0:1, :model_width], total)
    vector_ref[0:1, :model_width] = gain_grad
    vector_ref[1:2, :model_width] = shift_grad
    stream_grad_ref[...] = middle_grad + part


def attn_backward(middle_grad, stream, mixed, row, bias, wide, base):
    length, model_width = stream.shape
    mixed_width = mixed.shape[1]
    f32, low = jnp.float32, jnp.bfloat16
    return pl.pallas_call(
        functools.partial(attn_kernel, base),
        out_shape=(
            shape_of((length, model_width), f32),
            shape_of((length, model_width), low),
            shape_of((length, mixed_width), low),
            shape_of((8, mixed_width), f32),
        ),
        in_specs=[VMEM, VMEM, VMEM, VMEM, VMEM, ANY],
        out_specs=(VMEM,) * 4,
        scratch_shapes=[
            pltpu.VMEM((model_width, mixed_width), low),
            pltpu.VMEM((model_width, model_width), low),
            pltpu.VMEM((length, model_width), low),
            pltpu.SemaphoreType.DMA((2,)),
        ],
        cost_estimate=cost(11e-6),
        compiler_params=pltpu.CompilerParams(vmem_limit_bytes=46 * MIB),
    )(middle_grad, stream, mixed, row, bias, wide)


def adam_update(weight, mean, square, grad, rate):
    mean_new = BETA_ONE * mean + (1.0 - BETA_ONE) * grad
    square_new = BETA_TWO * square + (1.0 - BETA_TWO) * grad * grad
    mean_hat = mean_new / (1.0 - BETA_ONE**STEP)
    square_hat = square_new / (1.0 - BETA_TWO**STEP)
    weight_new = weight - rate * (
        mean_hat / (jnp.sqrt(square_hat) + ADAM_EPS) + WEIGHT_DECAY * weight
    )
    return (weight_new, mean_new, square_new)


def per_device(
    token_ids,
    parents,
    comp_pos,
    targets,
    table,
    table_mean,
    table_square,
    qkv_proj,
    qkv_mean,
    qkv_square,
    out_proj,
    out_mean,
    out_square,
    up_proj,
    up_mean,
    up_square,
    down_proj,
    down_mean,
    down_square,
    vectors,
    vec_mean,
    vec_square,
    pos_table,
    pos_mean,
    pos_square,
):
    place = Place()
    nv, nz = place.nv, place.nz
    length = token_ids.shape[0]
    model_width = pos_table.shape[1]
    head_size = (qkv_proj.shape[2] - model_width) // 2
    layer_width = 7 * model_width + head_size + up_proj.shape[2]
    slot_count = comp_pos.shape[1]
    shard_size, own_width = table.shape
    slice_size = shard_size // (2 * nz)
    bits = place.bits
    orders = (bits, list(reversed(bits)))

    own_slots = comp_pos[0]
    live = own_slots >= 0
    cut_one, cut_two = qkv_proj.shape[2], qkv_proj.shape[2] + out_proj.shape[2]
    cut_three = cut_two + up_proj.shape[2]
    shard_rows = qkv_proj.shape[1]
    ranks = down_proj.shape[1] // shard_rows

    everyone = list(range(nz))
    down_low = down_proj.astype(jnp.bfloat16)
    weights = lax.all_gather(
        jnp.concatenate(
            [
                down_low[i, k * shard_rows : (k + 1) * shard_rows]
                for i in range(L)
                for k in range(ranks)
            ]
            + [a[i].astype(jnp.bfloat16) for i in range(L) for a in (qkv_proj, out_proj, up_proj)],
            1,
        ),
        ALL,
        axis=0,
        tiled=True,
    )
    meta = jnp.concatenate([token_ids, jnp.where(live, targets[0], -1)])
    meta = place.gather_v(place.gather_z(place.gather_c(meta)))

    masks = list(range(nv))
    all_targets = put(
        place, [meta[:, :, :1, length:], meta[:, :, 1:, length:]], [(0, masks, everyone), (1, masks, everyone)]
    ).reshape(1, -1)
    meta = meta.transpose(2, 0, 1, 3)
    all_ids = meta[..., :length].reshape(-1)
    local_ids = all_ids - place.v * shard_size
    inside = (local_ids >= 0) & (local_ids < shard_size)
    safe_ids = jnp.where(inside, local_ids, shard_size)
    found = find_rows(safe_ids, table.T)
    found = found.reshape(2, nv, nz, length, LANES)
    found = jnp.stack([place.reduce_v(found[c], orders[c], 0) for c in range(2)])
    found = jnp.stack([found[0], place.swap(found[1], c=1)], 1)
    found = [found[0]] + [place.swap(found[m], z=m) for m in range(1, nz)]
    stream = embed(place, found, pos_table)
    stream, columns = tie((stream, table.T))
    stream, columns = tie((stream, cut(place, columns)))
    wdowns = [unslab_rows(place, weights, ranks, model_width, 0)]
    wdowns, columns = tie((wdowns, columns))
    parts = quarters(place, columns)
    parts[0].step()
    wdowns += [unslab_rows(place, weights, ranks, model_width, i) for i in range(1, L)]

    places, segment, path_depth = tree_layout(length, SEG)
    allowed = tree_mask(parents[0], places, segment, NSEG)
    trunk = 8 * SEG
    bias = jnp.where(allowed, 0.0, -1e30).T
    layer_rows = []
    for layer_index in range(L):
        pieces = split_layer(
            vectors[layer_index * layer_width : (layer_index + 1) * layer_width],
            model_width,
            head_size,
            up_proj.shape[2],
        )
        pieces.append(
            jnp.concatenate([pieces[2], jnp.zeros((head_size,), jnp.float32), pieces[3]])
        )
        layer_rows.append(
            jnp.stack([jnp.pad(p, (0, up_proj.shape[2] - p.shape[0])) for p in pieces])
        )
    inputs_kept = []
    matrices = []
    for layer_index in range(L):
        base = L * ranks * model_width + layer_index * cut_three
        wide = weights
        if layer_index == 0:
            stream, wdowns = tie((stream, wdowns), *parts)
            parts[1].step()
        wdown = wdowns[layer_index]
        matrices.append((wide, wdown, base))
        result, *saved = layer_forward(
            stream, layer_rows[layer_index], bias, wide, wdown, base, cut_one
        )
        inputs_kept.append((stream, saved))
        stream = result
        if layer_index == 0:
            stream = tie(stream, *parts)
            parts[2].step()
    stream = tie(stream, *parts)
    final_gain = vectors[L * layer_width : L * layer_width + model_width]
    final_shift = vectors[L * layer_width + model_width :]
    finished = norm_apply(stream, final_gain, final_shift).astype(jnp.bfloat16)
    slot_hot = own_slots[:, None] == jnp.arange(length, dtype=jnp.int32)[None, :]
    rows = jnp.dot(
        slot_hot.astype(jnp.bfloat16), finished, preferred_element_type=jnp.float32
    ).astype(jnp.bfloat16)

    held = tie(place.gather_z(rows), *parts)
    parts[3].step()
    held = place.spread_halves(held, orders)
    held = tie(held, *parts)
    group_rows = put_blocks(place, held).reshape(-1, model_width)
    parts = joined(parts)
    mine = parts[:, 0]
    theirs = place.swap(parts[:, 1], c=1)
    slice_low = put(place, [mine[None], theirs[None]], [(0, [0], everyone), (1, [0], everyone)], 1)
    slice_low = slice_low.reshape(model_width, slice_size)
    first_entry = place.v * shard_size + (place.z * 2 + place.c) * slice_size
    first_entry = first_entry.astype(jnp.int32).reshape(1)
    stats = head_forward(first_entry, group_rows, slice_low, all_targets)

    def combine(parts):
        top = functools.reduce(jnp.maximum, [p[0] for p in parts])
        return jnp.stack([top, tree_sum([p[1] * jnp.exp(p[0] - top) for p in parts])])

    whole = stats[:2]
    whole = combine([whole, place.swap(whole, c=1)])
    whole = combine([whole] + [place.swap(whole, v=m) for m in range(1, nv)])
    whole = combine([whole] + [place.swap(whole, z=m) for m in range(1, nz)])
    log_total = whole[0] + jnp.log(whole[1])
    own_total = lax.dynamic_slice_in_dim(
        log_total, ((place.z * 2 + place.c) * nv + place.v) * slot_count, slot_count
    )
    loss_local = jnp.sum(jnp.where(live, own_total, 0.0)) - jnp.sum(stats[2])
    count_local = jnp.sum(live.astype(jnp.float32))
    logits_low, rows_part = head_backward(
        first_entry, group_rows, log_total[None], slice_low, all_targets
    )
    rows_part = rows_part.reshape(nz, 2, nv, slot_count, model_width)
    rows_part = as_wide(pick(rows_part, place.c, 1)) + as_wide(
        place.swap(pick(rows_part, 1 - place.c, 1), c=1)
    )
    own_part = Held(rows_part)
    logits_low = tie(logits_low, own_part)
    rows_part = own_part.value
    head_grad = dot_first(group_rows, logits_low).astype(jnp.bfloat16)
    head_grad = head_grad.reshape(nz, 2, own_width, slice_size)
    head_parts = quarters(place, jnp.stack([pick(head_grad, place.z ^ m, 0) for m in range(nz)]))
    head_parts[0].step()
    rows_part = tree_sum(
        [pick(rows_part, place.v, 1)]
        + [as_wide(place.swap(as_low(pick(rows_part, place.v ^ m, 1)), v=m)) for m in range(1, nv)]
    )
    rows_part = tie(rows_part, *head_parts)
    rows_grad = tree_sum(
        [pick(rows_part, place.z, 0)]
        + [as_wide(place.swap(as_low(pick(rows_part, place.z ^ m, 0)), z=m)) for m in range(1, nz)]
    )
    rows_grad = tie(rows_grad, *head_parts)
    finished_grad = lax.dot_general(
        slot_hot.astype(jnp.float32),
        rows_grad,
        (((0,), (0,)), ((), ())),
        precision=HIGHEST,
        preferred_element_type=jnp.float32,
    )

    ignored, final_pull = jax.vjp(norm_apply, stream, final_gain, final_shift)
    stream_grad, grad_final_gain, grad_final_shift = final_pull(finished_grad)
    vector_parts = [None] * L

    def slabs(grad):
        grad = grad.reshape(nz * nv, ranks, shard_rows, model_width)
        return [grad[:, k].reshape(nz * nv * shard_rows, model_width) for k in range(ranks)]

    def unslab(columns):
        return jnp.concatenate(
            [columns[:, k * model_width : (k + 1) * model_width] for k in range(ranks)]
        )

    summed = [None] * L
    for layer_index in reversed(range(L)):
        kept_stream, saved = inputs_kept[layer_index]
        wide, wdown, base = matrices[layer_index]
        normed, mixed, attended, middle, normed_two, hidden, active = saved
        head_parts[1 if layer_index == 1 else 3].step()
        middle_grad, branch_grad, hidden_grad, late_vectors = mlp_backward(
            stream_grad, middle, hidden, layer_rows[layer_index], wide, wdown, base + cut_two
        )
        middle_grad, branch_grad, hidden_grad = tie(
            (middle_grad, branch_grad, hidden_grad), *head_parts
        )
        g_up = pair_grad(place, normed_two, hidden_grad)
        g_down = slabs(pair_grad_wide(place, active, branch_grad))
        g_mlp = Held([g_up] + g_down)
        middle_grad = tie(middle_grad, g_mlp, *head_parts)
        if layer_index == 1:
            head_parts[2].step()
        stream_grad, out_grad, mixed_grad, early_vectors = attn_backward(
            middle_grad, kept_stream, mixed, layer_rows[layer_index], bias, wide, base
        )
        stream_grad, out_grad, mixed_grad = tie((stream_grad, out_grad, mixed_grad), *head_parts)
        grads = Held(
            jnp.concatenate(
                g_mlp.value
                + [
                    pair_grad(place, normed, mixed_grad),
                    pair_grad(place, attended, out_grad),
                ],
                1,
            )
        )
        stream_grad = tie(stream_grad, grads, *head_parts)
        summed[layer_index] = lax.psum_scatter(
            grads.value, "vocab", scatter_dimension=0, tiled=True
        )
        vector_parts[layer_index] = (early_vectors, late_vectors)

    stream_grad, vector_parts = tie((stream_grad, vector_parts))
    vector_grads = [
        jnp.concatenate(
            [
                early_vectors[0, :model_width],
                early_vectors[1, :model_width],
                early_vectors[2, :model_width],
                early_vectors[2, model_width + head_size :],
                early_vectors[3, :model_width],
                late_vectors[0, :model_width],
                late_vectors[1, :model_width],
                late_vectors[2],
                late_vectors[3, :model_width],
            ]
        )
        for early_vectors, late_vectors in vector_parts
    ]
    sent = part_columns(place, stream_grad)
    sent = Traded(place, sent)
    sent.step()
    pos_grad = jnp.concatenate(
        [
            stream_grad[:trunk],
            jnp.sum(stream_grad[trunk : trunk + 4 * SEG].reshape(4, SEG, model_width), 0),
            jnp.sum(stream_grad[trunk + 4 * SEG :].reshape(8, SEG, model_width), 0),
        ]
    )
    vector_grad = jnp.concatenate(vector_grads + [grad_final_gain, grad_final_shift])
    flat = reduce_flat_core(place, vector_grad, pos_grad)
    flat, upper = tie((reduce_flat_plane(place, flat), summed[1]), sent, *head_parts)
    sent = sent.rest()
    sent = [sent[:, 0], place.swap(sent[:, 1], c=1)]
    sent = Held([place.spread_v(a, order) for a, order in zip(sent, orders)])
    flat_own = Held(reduce_flat_z(place, flat))
    upper = tie(upper, flat_own)
    upper = Held(spread_z(place, upper))
    lower = spread_z(place, tie(summed[0], sent, flat_own, upper))
    head_parts = joined(head_parts)
    mine = pick(head_parts, place.c, 1)
    theirs = place.swap(pick(head_parts, 1 - place.c, 1), c=1)
    head_grad = put(place, [mine[None], theirs[None]], [(0, [0], everyone), (1, [0], everyone)], 1)
    table_grad = add_rows(safe_ids, *[a.reshape(-1, LANES) for a in sent.value], head_grad)
    table_grad, lower = tie((table_grad, lower))
    summed = [tree_sum([as_wide(a) for a in parts]) for parts in (lower, upper.value)]
    up_end = up_proj.shape[2]
    down_end = up_end + ranks * model_width
    grad_up = jnp.stack([a[:, :up_end] for a in summed])
    grad_down = jnp.stack([unslab(a[:, up_end:down_end]) for a in summed])
    grad_qkv = jnp.stack([a[:, down_end : down_end + cut_one] for a in summed])
    grad_out = jnp.stack([a[:, down_end + cut_one :] for a in summed])
    owned_squares = (
        jnp.sum(grad_qkv * grad_qkv)
        + jnp.sum(grad_out * grad_out)
        + jnp.sum(grad_up * grad_up)
        + jnp.sum(grad_down * grad_down)
        + jnp.sum(table_grad * table_grad)
        + jnp.sum(flat_own.value * flat_own.value)
    )
    sums, vector_grad, pos_grad = gather_flat(
        place,
        flat_own.value,
        jnp.stack([owned_squares, loss_local, count_local]),
        vector_grad,
        pos_grad,
    )
    loss_sum, loss_count = sums[1], sums[2]
    grad_norm = jnp.sqrt(sums[0])
    factor = jnp.minimum(1.0, CLIP_NORM / grad_norm)
    states = (
        (table.T, table_mean.T, table_square.T, table_grad, LEARN_RATE),
        (qkv_proj, qkv_mean, qkv_square, grad_qkv, LEARN_RATE),
        (out_proj, out_mean, out_square, grad_out, LEARN_RATE),
        (up_proj, up_mean, up_square, grad_up, LEARN_RATE),
        (down_proj, down_mean, down_square, grad_down, LEARN_RATE),
        (vectors, vec_mean, vec_square, vector_grad, RATE_VEC),
        (pos_table, pos_mean, pos_square, pos_grad, LEARN_RATE),
    )
    results = [loss_sum, loss_count, grad_norm]
    for weight, mean, square, grad, rate in states:
        results.extend(adam_update(weight, mean, square, grad * factor, rate))
    results[3:6] = [a.T for a in results[3:6]]
    return tuple(results)


def solution(mesh):
    chips = mesh.devices.reshape(-1, 2, mesh.shape["vocab"])
    mesh = jax.sharding.Mesh(chips, ALL)
    return jax.shard_map(
        per_device,
        mesh=mesh,
        in_specs=(
            P(ALL),
            P(ALL, None),
            P(ALL, None),
            P(ALL, None),
            P("vocab", ("z", "core")),
            P("vocab", ("z", "core")),
            P("vocab", ("z", "core")),
            P(None, ALL, None),
            P(None, ALL, None),
            P(None, ALL, None),
            P(None, ALL, None),
            P(None, ALL, None),
            P(None, ALL, None),
            P(None, ALL, None),
            P(None, ALL, None),
            P(None, ALL, None),
            P(None, ALL, None),
            P(None, ALL, None),
            P(None, ALL, None),
            P(),
            P(),
            P(),
            P(),
            P(),
            P(),
        ),
        out_specs=(
            P(),
            P(),
            P(),
            P("vocab", ("z", "core")),
            P("vocab", ("z", "core")),
            P("vocab", ("z", "core")),
            P(None, ALL, None),
            P(None, ALL, None),
            P(None, ALL, None),
            P(None, ALL, None),
            P(None, ALL, None),
            P(None, ALL, None),
            P(None, ALL, None),
            P(None, ALL, None),
            P(None, ALL, None),
            P(None, ALL, None),
            P(None, ALL, None),
            P(None, ALL, None),
            P(),
            P(),
            P(),
            P(),
            P(),
            P(),
        ),
        check_vma=False,
    )
```

```python
import functools

import jax
import jax.numpy as jnp
from jax import lax
from jax.experimental import pallas as pl
from jax.experimental.pallas import tpu as pltpu
from jax.sharding import PartitionSpec as P

L = 2
NSEG = 13
STEP = 10
SEG = 16


NORM_EPS = 1e-05
BETA_ONE = 0.9
BETA_TWO = 0.999
ADAM_EPS = 1e-08
LEARN_RATE = 0.1
RATE_VEC = 0.5
WEIGHT_DECAY = 0.1
CLIP_NORM = 0.1
HIGHEST = lax.Precision.HIGHEST
GELU_SCALE = 0.7978845608028654
GELU_CUBE = 0.044715
ALL = ("z", "core", "vocab")
ROWS_STEP = 2560
UNROLL = 16
HEAD_ROWS = 256
TURN = 512
MIB = 1024 * 1024
COST_SCALE = 1e15
LANES = 128


class Place:
    def __init__(self):
        self.nv = lax.axis_size("vocab")
        self.nz = lax.axis_size("z")
        self.count = self.nv * self.nz * 2
        self.v = lax.axis_index("vocab")
        self.z = lax.axis_index("z")
        self.c = lax.axis_index("core")
        self.where = jnp.stack([self.z, self.c, self.v]).astype(jnp.int32)
        self.core_alone = jnp.stack([self.z * 0, self.c, self.v * 0]).astype(jnp.int32)
        self.bits = [1 << i for i in range(self.nv.bit_length() - 1)]

    def swap(self, a, v=0, c=0, z=0):
        mask = (z * 2 + c) * self.nv + v
        return lax.ppermute(a, ALL, [(i, i ^ mask) for i in range(self.count)])

    def gather_z(self, a):
        return jnp.stack([a] + [self.swap(a, z=m) for m in range(1, self.nz)])

    def gather_v(self, a):
        return jnp.stack([a] + [self.swap(a, v=m) for m in range(1, self.nv)])

    def gather_c(self, a):
        return jnp.stack([a, self.swap(a, c=1)])

    def spread_v(self, a, order):
        masks = [0]
        held = a[None]
        for bit in order:
            held = jnp.concatenate([held, self.swap(held, v=bit)])
            masks = masks + [m ^ bit for m in masks]
        if masks == sorted(masks):
            return held
        return jnp.stack([held[masks.index(m)] for m in range(self.nv)])

    def spread_halves(self, held, orders):
        half = self.nz // 2
        return jnp.concatenate(
            [self.spread_v(held[:half], orders[0]), self.spread_v(held[half:], orders[1])], 1
        )

    def reduce_v(self, a, order, axis):
        left = list(reversed(self.bits))
        a = a.reshape(a.shape[:axis] + (2,) * len(left) + a.shape[axis + 1 :])
        for bit in order:
            at = axis + left.index(bit)
            a = lax.index_in_dim(a, 0, at, False) + self.swap(
                lax.index_in_dim(a, 1, at, False), v=bit
            )
            left.remove(bit)
        return a


def pick(a, index, axis):
    return lax.dynamic_index_in_dim(a, index, axis, False)


def tree_sum(terms):
    while len(terms) > 1:
        terms = [terms[i] + terms[i + 1] for i in range(0, len(terms), 2)]
    return terms[0]


def cost(seconds):
    return pl.CostEstimate(flops=int(seconds * COST_SCALE), transcendentals=0, bytes_accessed=0)


def put_kernel(slots, nv, where_ref, *refs):
    pieces, out = refs[: len(slots)], refs[-1]
    z, c = where_ref[0], where_ref[1]
    v = where_ref[2] if nv > 1 else 0
    for piece, (core, masks, z_masks) in zip(pieces, slots):
        for k, mask in enumerate(masks):
            for i, m in enumerate(z_masks):
                row = ((z ^ m) * 2 + (c ^ core)) * nv + (v ^ mask)
                out[row] = piece[k, i]


def put(place, pieces, slots, nv=None):
    nv = place.nv if nv is None else nv
    count = 2 * place.nz * nv
    rows, width = pieces[0].shape[2:]
    return pl.pallas_call(
        functools.partial(put_kernel, slots, nv),
        out_shape=jax.ShapeDtypeStruct((count, rows, width), pieces[0].dtype),
        in_specs=[pl.BlockSpec(memory_space=pltpu.SMEM)]
        + [pl.BlockSpec(memory_space=pltpu.VMEM)] * len(pieces),
        out_specs=pl.BlockSpec(memory_space=pltpu.VMEM),
        cost_estimate=cost(3e-6),
        compiler_params=pltpu.CompilerParams(vmem_limit_bytes=4 * count * rows * width + 4 * MIB),
    )(place.where, *pieces)


def owner_hot(where_ref, depth, rows, nv, nz, order):
    part = rows // (nv * nz)
    column = lax.broadcasted_iota(jnp.int32, (1, rows), 1)
    block = jnp.zeros((1, rows), jnp.int32)
    for k in range(1, nv * nz):
        block = block + jnp.where(column >= k * part, 1, 0)
    apart = jnp.zeros((1, rows), jnp.int32)
    for k, bit in enumerate(reversed(order)):
        apart = apart + jnp.where((block & (nz << k)) != 0, bit, 0)
    owner = ((block & (nz - 1)) ^ where_ref[0]) * 2 + where_ref[1]
    owner = owner * nv + (apart ^ where_ref[2])
    row = owner * part + column - block * part
    return (lax.broadcasted_iota(jnp.int32, (depth, rows), 0) == row).astype(jnp.bfloat16)


def pair_kernel(
    nv, nz, order, where_ref, x_ref, other_ref, y_ref, y_other_ref, out_ref, left_ref, left_other_ref
):
    @pl.when(pl.program_id(0) == 0)
    def _():
        hot = owner_hot(where_ref, x_ref.shape[1], left_ref.shape[1], nv, nz, order)
        left_ref[...] = jnp.dot(x_ref[...], hot, preferred_element_type=jnp.float32).astype(
            jnp.bfloat16
        )
        left_other_ref[...] = jnp.dot(
            other_ref[...], hot, preferred_element_type=jnp.float32
        ).astype(jnp.bfloat16)

    out_ref[...] = (
        dot_first(left_ref[...], y_ref[...]) + dot_first(left_other_ref[...], y_other_ref[...])
    ).astype(jnp.bfloat16)


def pair_grad(place, x, y):
    length, depth = x.shape
    rows, width = depth // 2, y.shape[1]
    block = 768 if width % 768 == 0 else width
    whole = pl.BlockSpec((length, depth), lambda i: (0, 0))
    part = pl.BlockSpec((length, block), lambda i: (0, i))
    return pl.pallas_call(
        functools.partial(pair_kernel, place.nv, place.nz, list(reversed(place.bits))),
        out_shape=jax.ShapeDtypeStruct((rows, width), jnp.bfloat16),
        grid=(width // block,),
        in_specs=[pl.BlockSpec(memory_space=pltpu.SMEM), whole, whole, part, part],
        out_specs=pl.BlockSpec((rows, block), lambda i: (0, i)),
        scratch_shapes=[pltpu.VMEM((length, rows), jnp.bfloat16)] * 2,
        cost_estimate=cost(5e-6),
        compiler_params=pltpu.CompilerParams(vmem_limit_bytes=14 * MIB),
    )(place.core_alone, x, place.swap(x, c=1), y, place.swap(y, c=1))


def wide_kernel(nv, order, where_ref, x_ref, other_ref, y_ref, y_other_ref, out_ref):
    total = dot_first(x_ref[...], y_ref[...]) + dot_first(other_ref[...], y_other_ref[...])
    rows = total.shape[0] // nv
    for v in range(nv):
        apart = where_ref[2] ^ v
        position = 0
        for bit in order:
            position = position * 2 + jnp.where((apart & bit) != 0, 1, 0)
        out_ref[position, 0] = total[v * rows : (v + 1) * rows].astype(jnp.bfloat16)


def pair_grad_wide(place, x, y):
    length, depth = x.shape
    width = y.shape[1]
    block = depth // (2 * place.nz)
    rows = block // place.nv
    other = place.swap(x, c=1)
    if block % 128 == 0:
        part = pl.BlockSpec((length, block), lambda i, where: (0, 2 * i + where[1]))
    else:
        x, other = (a.reshape(length, -1, block).transpose(1, 0, 2) for a in (x, other))
        part = pl.BlockSpec((None, length, block), lambda i, where: (2 * i + where[1], 0, 0))
    whole = pl.BlockSpec((length, width), lambda i, where: (0, 0))
    shape, block_shape = (place.nv, place.nz, rows, width), (place.nv, 1, rows, width)
    where_out = lambda i, where: (0, i ^ where[0], 0, 0)
    return pl.pallas_call(
        functools.partial(wide_kernel, place.nv, list(reversed(place.bits))),
        out_shape=jax.ShapeDtypeStruct(shape, jnp.bfloat16),
        grid_spec=pltpu.PrefetchScalarGridSpec(
            num_scalar_prefetch=1,
            grid=(place.nz,),
            in_specs=[part, part, whole, whole],
            out_specs=pl.BlockSpec(block_shape, where_out),
        ),
        cost_estimate=cost(5e-6),
        compiler_params=pltpu.CompilerParams(vmem_limit_bytes=14 * MIB),
    )(place.core_alone, x, other, y, place.swap(y, c=1)).reshape(depth // 2, width)


def tie(main, *steps):
    main, values = lax.optimization_barrier((main, [s.value for s in steps]))
    for s, value in zip(steps, values):
        s.value = value
    return main


class Traded:
    def __init__(self, place, value):
        self.place = place
        self.value = value

    def step(self):
        place, a = self.place, self.value
        self.value = [a[0]] + [place.swap(a[m], z=m) for m in range(1, place.nz)]

    def rest(self):
        return jnp.stack(self.value)


def quarters(place, value):
    part = value.shape[-1] // 4
    return [Traded(place, value[..., k * part : (k + 1) * part]) for k in range(4)]


def spread_z(place, a):
    a = a.reshape(place.nz, -1, a.shape[1])
    return [pick(a, place.z, 0)] + [
        place.swap(pick(a, place.z ^ m, 0), z=m) for m in range(1, place.nz)
    ]


def joined(trades):
    return jnp.concatenate([t.rest() for t in trades], -1)


class Held:
    def __init__(self, value):
        self.value = value


def as_wide(a):
    return a.astype(jnp.float32)


def as_low(a):
    return a.astype(jnp.bfloat16)


def reduce_flat_core(place, vector, table):
    length = vector.shape[0]
    first = -(-length // 1024) * 8
    second = table.size // 128
    rows = -(-(first + second) // (place.count * 8)) * 8
    a = jnp.concatenate(
        [jnp.pad(vector, (0, first * 128 - length)).reshape(first, 128), table.reshape(second, 128)]
    )
    a = jnp.pad(a, ((0, place.count * rows - first - second), (0, 0)))
    a = a.reshape(place.nz, 2, place.nv, rows, 128)
    return pick(a, place.c, 1) + place.swap(pick(a, 1 - place.c, 1), c=1)


def reduce_flat_plane(place, a):
    bits = list(reversed(place.bits))
    a = a.reshape((place.nz,) + (2,) * len(bits) + a.shape[2:])
    for bit in bits:
        mine = (place.v // bit) % 2
        a = pick(a, mine, 1) + place.swap(pick(a, 1 - mine, 1), v=bit)
    return a


def reduce_flat_z(place, a):
    count = place.nz.bit_length() - 1
    a = a.reshape((2,) * count + a.shape[1:])
    for step in reversed(range(count)):
        mine = (place.z >> step) % 2
        a = pick(a, mine, 0) + place.swap(pick(a, 1 - mine, 0), z=1 << step)
    return a


def unslab_kernel(slabs_ref, out_ref):
    ranks = out_ref.shape[1] // slabs_ref.shape[1]
    rows, width = slabs_ref.shape[1], out_ref.shape[2]
    for k in range(ranks):
        out_ref[:, k * rows : (k + 1) * rows, :] = slabs_ref[:, :, k * width : (k + 1) * width]


def unslab_rows(place, gathered, ranks, width):
    count, total = place.count, ranks * width
    rows = gathered.shape[0] // count
    if rows % 8:
        slabs = gathered[:, :total].reshape(count, rows, ranks, width)
        return slabs.transpose(0, 2, 1, 3).reshape(-1, width)
    return pl.pallas_call(
        unslab_kernel,
        out_shape=jax.ShapeDtypeStruct((count, rows * ranks, width), gathered.dtype),
        grid=(count // 4,),
        in_specs=[pl.BlockSpec((4, rows, total), lambda i: (i, 0, 0))],
        out_specs=pl.BlockSpec((4, rows * ranks, width), lambda i: (i, 0, 0)),
        cost_estimate=cost(7e-6),
    )(gathered.reshape(count, rows, -1)).reshape(-1, width)


def gather_flat(place, own, scalars, vector, table):
    length, rows = vector.shape[0], own.shape[0]
    first, second = -(-length // 1024) * 8, table.size // 128
    own = jnp.concatenate([own, jnp.pad(scalars[None], ((0, 7), (0, 128 - scalars.shape[0])))])
    whole = gather_blocks(place, own)
    scalars = jnp.sum(whole[:, rows, : scalars.shape[0]], 0)
    whole = whole[:, :rows].reshape(-1, 128)
    return (
        scalars,
        whole[:first].reshape(-1)[:length],
        whole[first : first + second].reshape(table.shape),
    )


def put_blocks(place, held):
    everyone = list(range(place.nz))
    masks = list(range(place.nv))
    return put(place, [held, place.swap(held, c=1)], [(0, masks, everyone), (1, masks, everyone)])


def gather_blocks(place, block):
    return put_blocks(place, place.gather_v(place.gather_z(block)))


def column_hot(where_ref, part, width, total):
    first = (part ^ (where_ref[0] * 2 + where_ref[1])) * width
    rows = lax.broadcasted_iota(jnp.int32, (width, total), 0) + first
    return (rows == lax.broadcasted_iota(jnp.int32, (width, total), 1)).astype(jnp.bfloat16)


def embed_kernel(where_ref, table_ref, *refs):
    pieces, out_ref = refs[:-1], refs[-1]
    total_width = out_ref.shape[1]
    width = total_width // (2 * len(pieces))
    total = jnp.zeros(out_ref.shape, jnp.float32)
    for m, piece in enumerate(pieces):
        for c in range(2):
            hot = column_hot(where_ref, 2 * m + c, width, total_width)
            total = total + jnp.dot(
                piece[c, :, :width], hot, preferred_element_type=jnp.float32
            )
    out_ref[...] = total
    trunk = 8 * SEG
    out_ref[:trunk, :] += table_ref[:trunk, :]
    for k in range(12):
        at = trunk + k * SEG
        row = trunk if k < 4 else trunk + SEG
        out_ref[at : at + SEG, :] += table_ref[row : row + SEG, :]


def embed(place, pieces, table):
    length, width = pieces[0].shape[1:]
    return pl.pallas_call(
        embed_kernel,
        out_shape=jax.ShapeDtypeStruct((length, table.shape[1]), jnp.float32),
        in_specs=[pl.BlockSpec(memory_space=pltpu.SMEM)]
        + [pl.BlockSpec(memory_space=pltpu.VMEM)] * (1 + len(pieces)),
        out_specs=pl.BlockSpec(memory_space=pltpu.VMEM),
        cost_estimate=cost(1.7e-6),
        compiler_params=pltpu.CompilerParams(vmem_limit_bytes=16 * MIB),
    )(place.where, table, *pieces)


def part_kernel(where_ref, grad_ref, out_ref):
    grad = grad_ref[...].astype(jnp.bfloat16)
    nz = out_ref.shape[0]
    width = grad.shape[1] // (2 * nz)
    out_ref[...] = jnp.zeros_like(out_ref)
    for m in range(nz):
        for c in range(2):
            hot = column_hot(where_ref, 2 * m + c, width, grad.shape[1])
            out_ref[m, c, :, :width] = dot_last(grad, hot).astype(jnp.bfloat16)


def part_columns(place, grad):
    length, total = grad.shape
    return pl.pallas_call(
        part_kernel,
        out_shape=jax.ShapeDtypeStruct((place.nz, 2, length, LANES), jnp.bfloat16),
        in_specs=[
            pl.BlockSpec(memory_space=pltpu.SMEM),
            pl.BlockSpec(memory_space=pltpu.VMEM),
        ],
        out_specs=pl.BlockSpec(memory_space=pltpu.VMEM),
        cost_estimate=cost(1.8e-6),
        compiler_params=pltpu.CompilerParams(vmem_limit_bytes=16 * MIB),
    )(place.where, grad)


def turned(value, axis):
    size = max(value.shape)
    same = lax.broadcasted_iota(jnp.int32, (size, size), 0) == lax.broadcasted_iota(
        jnp.int32, (size, size), 1
    )
    return jnp.sum(jnp.where(same, value, jnp.zeros((), value.dtype)), axis, keepdims=True)


def hits(first_ref, targets_ref, shape):
    column = turned(targets_ref[...], 1) - first_ref[0]
    return column == lax.broadcasted_iota(jnp.int32, shape, 1)


def logits_kernel(first_ref, rows_ref, table_ref, targets_ref, stats_ref):
    logits = jnp.dot(rows_ref[...], table_ref[...], preferred_element_type=jnp.float32)
    top = jnp.max(logits, 1, keepdims=True)
    exps = jnp.exp(logits - top)
    picked = jnp.where(hits(first_ref, targets_ref, logits.shape), logits, 0.0)
    stats_ref[0:1, :] = turned(top, 0)
    stats_ref[1:2, :] = turned(jnp.sum(exps, 1, keepdims=True), 0)
    stats_ref[2:3, :] = turned(jnp.sum(picked, 1, keepdims=True), 0)


def head_forward(first, rows, table, targets):
    count, width = rows.shape
    size = table.shape[1]
    return pl.pallas_call(
        logits_kernel,
        out_shape=jax.ShapeDtypeStruct((3, count), jnp.float32),
        grid=(count // HEAD_ROWS,),
        in_specs=[
            pl.BlockSpec(memory_space=pltpu.SMEM),
            pl.BlockSpec((HEAD_ROWS, width), lambda i: (i, 0)),
            pl.BlockSpec((width, size), lambda i: (0, 0)),
            pl.BlockSpec((1, HEAD_ROWS), lambda i: (0, i)),
        ],
        out_specs=pl.BlockSpec((3, HEAD_ROWS), lambda i: (0, i)),
        cost_estimate=cost(11.6e-6),
        compiler_params=pltpu.CompilerParams(vmem_limit_bytes=24 * MIB),
    )(first, rows, table, targets)


def slopes_kernel(first_ref, rows_in_ref, total_ref, table_ref, targets_ref, slopes_ref, rows_ref):
    logits = jnp.dot(rows_in_ref[...], table_ref[...], preferred_element_type=jnp.float32)
    exps = jnp.exp(logits - turned(total_ref[...], 1))
    hit = hits(first_ref, targets_ref, exps.shape)
    alive = turned(targets_ref[...], 1) >= 0
    slopes = jnp.where(alive, exps - jnp.where(hit, 1.0, 0.0), 0.0).astype(jnp.bfloat16)
    slopes_ref[...] = slopes
    rows_ref[...] = dot_last(slopes, table_ref[...]).astype(jnp.bfloat16)


def head_backward(first, rows, total, table, targets):
    count, width = rows.shape
    size = table.shape[1]
    return pl.pallas_call(
        slopes_kernel,
        out_shape=(
            jax.ShapeDtypeStruct((count, size), jnp.bfloat16),
            jax.ShapeDtypeStruct((count, width), jnp.bfloat16),
        ),
        grid=(count // HEAD_ROWS,),
        in_specs=[
            pl.BlockSpec(memory_space=pltpu.SMEM),
            pl.BlockSpec((HEAD_ROWS, width), lambda i: (i, 0)),
            pl.BlockSpec((1, HEAD_ROWS), lambda i: (0, i)),
            pl.BlockSpec((width, size), lambda i: (0, 0)),
            pl.BlockSpec((1, HEAD_ROWS), lambda i: (0, i)),
        ],
        out_specs=(
            pl.BlockSpec((HEAD_ROWS, size), lambda i: (i, 0)),
            pl.BlockSpec((HEAD_ROWS, width), lambda i: (i, 0)),
        ),
        cost_estimate=cost(16e-6),
        compiler_params=pltpu.CompilerParams(vmem_limit_bytes=24 * MIB),
    )(first, rows, total, table, targets)


def cut_kernel(where_ref, columns_ref, out_ref):
    out_ref[0, 0] = columns_ref[...].astype(out_ref.dtype)


def cut(place, columns):
    width, size = columns.shape
    part = size // (2 * place.nz)
    if part % 128:
        order = jnp.arange(2 * place.nz) ^ (place.z * 2 + place.c)
        parts = columns.astype(jnp.bfloat16).reshape(width, 2 * place.nz, part).transpose(1, 0, 2)
        return jnp.take(parts, order, axis=0).reshape(place.nz, 2, width, part)
    return pl.pallas_call(
        cut_kernel,
        out_shape=jax.ShapeDtypeStruct((place.nz, 2, width, part), jnp.bfloat16),
        grid_spec=pltpu.PrefetchScalarGridSpec(
            num_scalar_prefetch=1,
            grid=(2 * place.nz,),
            in_specs=[
                pl.BlockSpec((width, part), lambda i, where: (0, i ^ (where[0] * 2 + where[1])))
            ],
            out_specs=pl.BlockSpec((1, 1, width, part), lambda i, where: (i // 2, i % 2, 0, 0)),
        ),
        cost_estimate=cost(7e-6),
    )(place.where, columns)


def find_kernel(ids_ref, columns_ref, out_ref, rows_ref, found_ref):
    size = columns_ref.shape[1]

    @pl.when(pl.program_id(0) == 0)
    def _():
        def turn(i, carry):
            at = pl.multiple_of(i * TURN, TURN)
            part = columns_ref[:, pl.ds(at, TURN)].astype(jnp.bfloat16).astype(jnp.float32)
            rows_ref[pl.ds(at, TURN), : part.shape[0]] = part.T
            return carry

        rows_ref[:, columns_ref.shape[0] :] = jnp.zeros(
            (rows_ref.shape[0], LANES - columns_ref.shape[0]), jnp.float32
        )

        lax.fori_loop(0, size // TURN, turn, 0)
        rows_ref[pl.ds(size, 8), :] = jnp.zeros((8, rows_ref.shape[1]), jnp.float32)

    first = pl.program_id(0) * out_ref.shape[0]

    def body(i, carry):
        for u in range(UNROLL):
            t = i * UNROLL + u
            found_ref[pl.ds(t, 1), :] = rows_ref[pl.ds(ids_ref[first + t], 1), :]
        return carry

    lax.fori_loop(0, out_ref.shape[0] // UNROLL, body, 0)
    out_ref[...] = found_ref[...].astype(out_ref.dtype)


def find_rows(ids, columns):
    width, size = columns.shape
    return pl.pallas_call(
        find_kernel,
        out_shape=jax.ShapeDtypeStruct((ids.shape[0], LANES), jnp.bfloat16),
        grid_spec=pltpu.PrefetchScalarGridSpec(
            num_scalar_prefetch=1,
            grid=(ids.shape[0] // ROWS_STEP,),
            in_specs=[pl.BlockSpec(memory_space=pltpu.VMEM)],
            out_specs=pl.BlockSpec((ROWS_STEP, LANES), lambda i, ids: (i, 0)),
            scratch_shapes=[
                pltpu.VMEM((size + 8, LANES), jnp.float32),
                pltpu.VMEM((ROWS_STEP, LANES), jnp.float32),
            ],
        ),
        cost_estimate=cost(18e-6),
        compiler_params=pltpu.CompilerParams(vmem_limit_bytes=24 * MIB),
    )(ids, columns)


def add_kernel(ids_ref, low_ref, more_ref, head_ref, out_ref, rows_ref, *parts):
    step = pl.program_id(0)
    first = step * rows_ref.shape[0]
    size = out_ref.shape[1]
    early = step < pl.num_programs(0) // 2
    rows_ref[...] = jnp.where(early, low_ref[...], more_ref[...]).astype(jnp.float32)

    @pl.when(step == 0)
    def _():
        for part in parts:
            part[...] = jnp.zeros_like(part)

    def body(i, carry):
        for u in range(UNROLL):
            t = i * UNROLL + u
            part = parts[u % len(parts)]
            where = pl.ds(ids_ref[first + t], 1)
            part[where, :] = part[where, :] + rows_ref[pl.ds(t, 1), :]
        return carry

    lax.fori_loop(0, rows_ref.shape[0] // UNROLL, body, 0)

    @pl.when(step == pl.num_programs(0) - 1)
    def _():
        def turn(i, carry):
            at = pl.ds(pl.multiple_of(i * TURN, TURN), TURN)
            total = tree_sum([part[at, :] for part in parts])
            part = head_ref.shape[2]
            head = head_ref[i * TURN // part, :, pl.ds(pl.multiple_of(i * TURN % part, TURN), TURN)]
            out_ref[:, at] = total.T[: out_ref.shape[0]] + head.astype(jnp.float32)
            return carry

        lax.fori_loop(0, size // TURN, turn, 0)


def add_rows(ids, rows, more, head):
    width, size = head.shape[1], head.shape[0] * head.shape[2]
    if head.shape[2] % TURN:
        head = head.transpose(1, 0, 2).reshape(1, width, size)
    steps = rows.shape[0] // ROWS_STEP
    return pl.pallas_call(
        add_kernel,
        out_shape=jax.ShapeDtypeStruct((width, size), jnp.float32),
        grid_spec=pltpu.PrefetchScalarGridSpec(
            num_scalar_prefetch=1,
            grid=(ids.shape[0] // ROWS_STEP,),
            in_specs=[
                pl.BlockSpec((ROWS_STEP, LANES), lambda i, ids: (jnp.minimum(i, steps - 1), 0)),
                pl.BlockSpec((ROWS_STEP, LANES), lambda i, ids: (jnp.maximum(i - steps, 0), 0)),
                pl.BlockSpec(memory_space=pltpu.VMEM),
            ],
            out_specs=pl.BlockSpec(memory_space=pltpu.VMEM),
            scratch_shapes=[pltpu.VMEM((ROWS_STEP, LANES), jnp.float32)]
            + [pltpu.VMEM((size + 8, LANES), jnp.float32)] * 4,
        ),
        cost_estimate=cost(25e-6),
        compiler_params=pltpu.CompilerParams(vmem_limit_bytes=40 * MIB),
    )(ids, rows, more, head)


def norm_apply(stream, gain, shift):
    center = stream - jnp.mean(stream, -1, keepdims=True)
    spread = jnp.mean(center * center, -1, keepdims=True)
    return center * lax.rsqrt(spread + NORM_EPS) * gain + shift


def norm_back(stream, gain, grad):
    center = stream - jnp.mean(stream, -1, keepdims=True)
    scale = lax.rsqrt(jnp.mean(center * center, -1, keepdims=True) + NORM_EPS)
    unit = center * scale
    inner = grad * gain
    part = inner - jnp.mean(inner, -1, keepdims=True)
    part = scale * (part - unit * jnp.mean(inner * unit, -1, keepdims=True))
    return part, jnp.sum(grad * unit, 0, keepdims=True), jnp.sum(grad, 0, keepdims=True)


def gelu_parts(value):
    inner = GELU_SCALE * (value + GELU_CUBE * value * value * value)
    bend = jnp.tanh(inner)
    half = 0.5 * (1.0 + bend)
    slope = GELU_SCALE * (1.0 + 3.0 * GELU_CUBE * value * value)
    return value * half, half + 0.5 * value * (1.0 - bend * bend) * slope


def split_layer(vector_row, model_width, head_size, hidden_width):
    widths = [model_width] * 3 + [head_size] + [model_width] * 3 + [hidden_width, model_width]
    pieces = []
    offset = 0
    for width in widths:
        pieces.append(vector_row[offset : offset + width])
        offset += width
    return pieces


def tree_layout(total, seg_len):
    places = jnp.arange(total, dtype=jnp.int32)
    trunk = 8 * seg_len
    beyond = jnp.maximum(places - trunk, 0) // seg_len
    segment = jnp.where(places < trunk, 0, 1 + beyond)
    offset = places - trunk - beyond * seg_len
    path_depth = jnp.where(
        places < trunk, places, jnp.where(segment <= 4, trunk + offset, trunk + seg_len + offset)
    )
    return (places, segment, path_depth)


def tree_mask(parent_row, places, segment, count):
    labels = jnp.arange(count, dtype=jnp.int32)
    parent_hot = (parent_row[:, None] == labels[None, :]).astype(jnp.float32)
    grand_hot = jnp.dot(parent_hot, parent_hot, precision=HIGHEST)
    ancestor = jnp.eye(count, dtype=jnp.float32) + parent_hot + grand_hot
    seg_hot = (segment[:, None] == labels[None, :]).astype(jnp.float32)
    reach = jnp.dot(jnp.dot(seg_hot, ancestor, precision=HIGHEST), seg_hot.T, precision=HIGHEST)
    return (reach > 0.5) & (places[None, :] <= places[:, None])


def dot_first(left, right):
    return lax.dot_general(
        left, right, (((0,), (0,)), ((), ())), preferred_element_type=jnp.float32
    )


def dot_last(left, right):
    return lax.dot_general(
        left, right, (((1,), (1,)), ((), ())), preferred_element_type=jnp.float32
    )


def column_sum(grad_low):
    return jnp.sum(grad_low.astype(jnp.float32), 0)


def fetch(copies):
    for copy in copies:
        copy.start()
    return copies


def head_probs(mixed_ref, bias, h, keys, size, model_width):
    queries = mixed_ref[:, h * size : (h + 1) * size]
    scores = dot_last(keys, queries) * size ** (-0.5) + bias
    exps = jnp.exp(scores - jnp.max(scores, 0, keepdims=True))
    return queries, exps * (1.0 / jnp.sum(exps, 0, keepdims=True))


def forward_kernel(
    base,
    stream_ref,
    row_ref,
    bias_ref,
    wide_ref,
    down_ref,
    result_ref,
    normed_ref,
    mixed_ref,
    attended_ref,
    middle_ref,
    normed_two_ref,
    hidden_ref,
    active_ref,
    qkv_low,
    out_low,
    up_low,
    down_low,
    sems,
):
    model_width = stream_ref.shape[1]
    size = (qkv_low.shape[1] - model_width) // 2
    cuts = (qkv_low.shape[1], qkv_low.shape[1] + model_width)
    copies = fetch(
        [
            pltpu.make_async_copy(wide_ref.at[:, pl.ds(base, cuts[0])], qkv_low, sems.at[0]),
            pltpu.make_async_copy(
                wide_ref.at[:, pl.ds(base + cuts[0], model_width)], out_low, sems.at[1]
            ),
            pltpu.make_async_copy(
                wide_ref.at[:, pl.ds(base + cuts[1], up_low.shape[1])], up_low, sems.at[2]
            ),
            pltpu.make_async_copy(down_ref, down_low, sems.at[3]),
        ]
    )

    def row(k, width=model_width):
        return row_ref[k : k + 1, :width]

    stream = stream_ref[...]
    normed = norm_apply(stream, row(0), row(1)).astype(jnp.bfloat16)
    normed_ref[...] = normed
    copies[0].wait()
    mixed = jnp.dot(normed, qkv_low[...], preferred_element_type=jnp.float32)
    mixed = (mixed + row(9, mixed.shape[1])).astype(jnp.bfloat16)
    mixed_ref[...] = mixed
    keys, values = mixed[:, model_width : model_width + size], mixed[:, model_width + size :]
    for h in range(model_width // size):
        ignored, probs = head_probs(mixed_ref, bias_ref[...], h, keys, size, model_width)
        attended_ref[:, h * size : (h + 1) * size] = dot_first(
            probs.astype(jnp.bfloat16), values
        ).astype(jnp.bfloat16)
    copies[1].wait()
    middle = stream + jnp.dot(
        attended_ref[...], out_low[...], preferred_element_type=jnp.float32
    )
    middle = middle + row(4)
    middle_ref[...] = middle
    normed_two = norm_apply(middle, row(5), row(6)).astype(jnp.bfloat16)
    normed_two_ref[...] = normed_two
    copies[2].wait()
    copies[3].wait()
    total = middle + row(8)
    for k in range(up_low.shape[1] // model_width):
        at = slice(k * model_width, (k + 1) * model_width)
        hidden = jnp.dot(normed_two, up_low[:, at], preferred_element_type=jnp.float32)
        hidden = hidden + row_ref[7:8, at]
        hidden_ref[:, at] = hidden
        active = gelu_parts(hidden)[0].astype(jnp.bfloat16)
        active_ref[:, at] = active
        total = total + jnp.dot(active, down_low[at, :], preferred_element_type=jnp.float32)
    result_ref[...] = total


def shape_of(shape, kind):
    return jax.ShapeDtypeStruct(shape, kind)


VMEM = pl.BlockSpec(memory_space=pltpu.VMEM)
ANY = pl.BlockSpec(memory_space=pltpu.HBM)


def layer_forward(stream, row, bias, wide, down, base, row_width):
    length, model_width = stream.shape
    hidden_width = down.shape[0]
    mixed_width = row_width
    f32, low = jnp.float32, jnp.bfloat16
    return pl.pallas_call(
        functools.partial(forward_kernel, base),
        out_shape=(
            shape_of((length, model_width), f32),
            shape_of((length, model_width), low),
            shape_of((length, mixed_width), low),
            shape_of((length, model_width), low),
            shape_of((length, model_width), f32),
            shape_of((length, model_width), low),
            shape_of((length, hidden_width), f32),
            shape_of((length, hidden_width), low),
        ),
        in_specs=[VMEM, VMEM, VMEM, ANY, ANY],
        out_specs=(VMEM,) * 8,
        scratch_shapes=[
            pltpu.VMEM((model_width, mixed_width), low),
            pltpu.VMEM((model_width, model_width), low),
            pltpu.VMEM((model_width, hidden_width), low),
            pltpu.VMEM((hidden_width, model_width), low),
            pltpu.SemaphoreType.DMA((4,)),
        ],
        cost_estimate=cost(12e-6),
        compiler_params=pltpu.CompilerParams(vmem_limit_bytes=46 * MIB),
    )(stream, row, bias, wide, down)


def mlp_kernel(
    first,
    grad_ref,
    middle_ref,
    hidden_ref,
    row_ref,
    wide_ref,
    down_ref,
    middle_grad_ref,
    branch_ref,
    hidden_grad_ref,
    vector_ref,
    up_low,
    down_low,
    sems,
):
    model_width = grad_ref.shape[1]
    start = first
    copies = fetch(
        [
            pltpu.make_async_copy(down_ref, down_low, sems.at[0]),
            pltpu.make_async_copy(
                wide_ref.at[:, start : start + up_low.shape[1]], up_low, sems.at[1]
            ),
        ]
    )
    grad = grad_ref[...]
    branch = grad.astype(jnp.bfloat16)
    branch_ref[...] = branch
    vector_ref[...] = jnp.zeros_like(vector_ref)
    vector_ref[3:4, :model_width] = jnp.sum(branch.astype(jnp.float32), 0, keepdims=True)
    copies[0].wait()
    copies[1].wait()
    total = jnp.zeros_like(grad)
    for k in range(up_low.shape[1] // model_width):
        at = slice(k * model_width, (k + 1) * model_width)
        slope = gelu_parts(hidden_ref[:, at])[1]
        hidden_grad = (slope * dot_last(branch, down_low[at, :])).astype(jnp.bfloat16)
        hidden_grad_ref[:, at] = hidden_grad
        vector_ref[2:3, at] = jnp.sum(hidden_grad.astype(jnp.float32), 0, keepdims=True)
        total = total + dot_last(hidden_grad, up_low[:, at])
    part, gain_grad, shift_grad = norm_back(middle_ref[...], row_ref[5:6, :model_width], total)
    vector_ref[0:1, :model_width] = gain_grad
    vector_ref[1:2, :model_width] = shift_grad
    middle_grad_ref[...] = grad + part


def mlp_backward(grad, middle, hidden, row, wide, down, first):
    length, model_width = grad.shape
    hidden_width = down.shape[0]
    f32, low = jnp.float32, jnp.bfloat16
    return pl.pallas_call(
        functools.partial(mlp_kernel, first),
        out_shape=(
            shape_of((length, model_width), f32),
            shape_of((length, model_width), low),
            shape_of((length, hidden_width), low),
            shape_of((8, hidden_width), f32),
        ),
        in_specs=[VMEM, VMEM, VMEM, VMEM, ANY, ANY],
        out_specs=(VMEM,) * 4,
        scratch_shapes=[
            pltpu.VMEM((model_width, hidden_width), low),
            pltpu.VMEM((hidden_width, model_width), low),
            pltpu.SemaphoreType.DMA((2,)),
        ],
        cost_estimate=cost(6.5e-6),
        compiler_params=pltpu.CompilerParams(vmem_limit_bytes=46 * MIB),
    )(grad, middle, hidden, row, wide, down)


def attn_kernel(
    base,
    middle_grad_ref,
    stream_ref,
    mixed_ref,
    row_ref,
    bias_ref,
    wide_ref,
    stream_grad_ref,
    out_grad_ref,
    mixed_grad_ref,
    vector_ref,
    qkv_low,
    out_low,
    attended_ref,
    sems,
):
    model_width = stream_ref.shape[1]
    size = (qkv_low.shape[1] - model_width) // 2
    cut = qkv_low.shape[1]
    copies = fetch(
        [
            pltpu.make_async_copy(
                wide_ref.at[:, pl.ds(base + cut, model_width)], out_low, sems.at[0]
            ),
            pltpu.make_async_copy(wide_ref.at[:, pl.ds(base, cut)], qkv_low, sems.at[1]),
        ]
    )
    middle_grad = middle_grad_ref[...]
    out_grad = middle_grad.astype(jnp.bfloat16)
    out_grad_ref[...] = out_grad
    vector_ref[...] = jnp.zeros_like(vector_ref)
    vector_ref[3:4, :model_width] = jnp.sum(out_grad.astype(jnp.float32), 0, keepdims=True)
    copies[0].wait()
    attended_ref[...] = dot_last(out_grad, out_low[...]).astype(jnp.bfloat16)
    keys = mixed_ref[:, model_width : model_width + size]
    values = mixed_ref[:, model_width + size :]
    keys_grad = jnp.zeros(keys.shape, jnp.float32)
    values_grad = jnp.zeros(values.shape, jnp.float32)
    for h in range(model_width // size):
        at = slice(h * size, (h + 1) * size)
        queries, probs = head_probs(mixed_ref, bias_ref[...], h, keys, size, model_width)
        grad = attended_ref[:, at]
        values_grad = values_grad + jnp.dot(
            probs.astype(jnp.bfloat16), grad, preferred_element_type=jnp.float32
        )
        probs_grad = dot_last(values, grad)
        scores_grad = probs * (probs_grad - jnp.sum(probs * probs_grad, 0, keepdims=True))
        scores_grad = scores_grad.astype(jnp.bfloat16)
        keys_grad = keys_grad + jnp.dot(
            scores_grad, queries, preferred_element_type=jnp.float32
        )
        mixed_grad_ref[:, at] = (dot_first(scores_grad, keys) * size ** (-0.5)).astype(jnp.bfloat16)
    mixed_grad_ref[:, model_width : model_width + size] = (keys_grad * size ** (-0.5)).astype(
        jnp.bfloat16
    )
    mixed_grad_ref[:, model_width + size :] = values_grad.astype(jnp.bfloat16)
    mixed_grad = mixed_grad_ref[...]
    vector_ref[2:3, :] = jnp.sum(mixed_grad.astype(jnp.float32), 0, keepdims=True)
    copies[1].wait()
    total = dot_last(mixed_grad, qkv_low[...])
    part, gain_grad, shift_grad = norm_back(stream_ref[...], row_ref[0:1, :model_width], total)
    vector_ref[0:1, :model_width] = gain_grad
    vector_ref[1:2, :model_width] = shift_grad
    stream_grad_ref[...] = middle_grad + part


def attn_backward(middle_grad, stream, mixed, row, bias, wide, base):
    length, model_width = stream.shape
    mixed_width = mixed.shape[1]
    f32, low = jnp.float32, jnp.bfloat16
    return pl.pallas_call(
        functools.partial(attn_kernel, base),
        out_shape=(
            shape_of((length, model_width), f32),
            shape_of((length, model_width), low),
            shape_of((length, mixed_width), low),
            shape_of((8, mixed_width), f32),
        ),
        in_specs=[VMEM, VMEM, VMEM, VMEM, VMEM, ANY],
        out_specs=(VMEM,) * 4,
        scratch_shapes=[
            pltpu.VMEM((model_width, mixed_width), low),
            pltpu.VMEM((model_width, model_width), low),
            pltpu.VMEM((length, model_width), low),
            pltpu.SemaphoreType.DMA((2,)),
        ],
        cost_estimate=cost(11e-6),
        compiler_params=pltpu.CompilerParams(vmem_limit_bytes=46 * MIB),
    )(middle_grad, stream, mixed, row, bias, wide)


def adam_update(weight, mean, square, grad, rate):
    mean_new = BETA_ONE * mean + (1.0 - BETA_ONE) * grad
    square_new = BETA_TWO * square + (1.0 - BETA_TWO) * grad * grad
    mean_hat = mean_new / (1.0 - BETA_ONE**STEP)
    square_hat = square_new / (1.0 - BETA_TWO**STEP)
    weight_new = weight - rate * (
        mean_hat / (jnp.sqrt(square_hat) + ADAM_EPS) + WEIGHT_DECAY * weight
    )
    return (weight_new, mean_new, square_new)


def per_device(
    token_ids,
    parents,
    comp_pos,
    targets,
    table,
    table_mean,
    table_square,
    qkv_proj,
    qkv_mean,
    qkv_square,
    out_proj,
    out_mean,
    out_square,
    up_proj,
    up_mean,
    up_square,
    down_proj,
    down_mean,
    down_square,
    vectors,
    vec_mean,
    vec_square,
    pos_table,
    pos_mean,
    pos_square,
):
    place = Place()
    nv, nz = place.nv, place.nz
    length = token_ids.shape[0]
    model_width = pos_table.shape[1]
    head_size = (qkv_proj.shape[2] - model_width) // 2
    layer_width = 7 * model_width + head_size + up_proj.shape[2]
    slot_count = comp_pos.shape[1]
    shard_size, own_width = table.shape
    slice_size = shard_size // (2 * nz)
    bits = place.bits
    orders = (bits, list(reversed(bits)))

    own_slots = comp_pos[0]
    live = own_slots >= 0
    cut_one, cut_two = qkv_proj.shape[2], qkv_proj.shape[2] + out_proj.shape[2]
    cut_three = cut_two + up_proj.shape[2]
    shard_rows = qkv_proj.shape[1]
    ranks = down_proj.shape[1] // shard_rows

    everyone = list(range(nz))
    down_low = down_proj.astype(jnp.bfloat16)
    weights = lax.all_gather(
        jnp.concatenate(
            [
                down_low[0, k * shard_rows : (k + 1) * shard_rows]
                for k in range(ranks)
            ]
            + [a[i].astype(jnp.bfloat16) for i in range(L) for a in (qkv_proj, out_proj, up_proj)],
            1,
        ),
        ALL,
        axis=0,
        tiled=True,
    )
    meta = jnp.concatenate([token_ids, jnp.where(live, targets[0], -1)])
    meta = place.gather_v(place.gather_z(place.gather_c(meta)))

    meta, later = tie((meta, down_low[1]))
    masks = list(range(nv))
    all_targets = put(
        place, [meta[:, :, :1, length:], meta[:, :, 1:, length:]], [(0, masks, everyone), (1, masks, everyone)]
    ).reshape(1, -1)
    meta = meta.transpose(2, 0, 1, 3)
    all_ids = meta[..., :length].reshape(-1)
    local_ids = all_ids - place.v * shard_size
    inside = (local_ids >= 0) & (local_ids < shard_size)
    safe_ids = jnp.where(inside, local_ids, shard_size)
    found = find_rows(safe_ids, table.T)
    second = Held(place.gather_z(later))
    found = found.reshape(2, nv, nz, length, LANES)
    found = jnp.stack([place.reduce_v(found[c], orders[c], 0) for c in range(2)])
    found = tie(found, second)
    second = Held(place.spread_v(second.value, orders[1]))
    found = jnp.stack([found[0], place.swap(found[1], c=1)], 1)
    found = [found[0]] + [place.swap(found[m], z=m) for m in range(1, nz)]
    stream = embed(place, found, pos_table)
    stream, columns = tie((stream, table.T), second)
    second = put_blocks(place, second.value).reshape(-1, model_width)
    stream, columns, second = tie((stream, cut(place, columns), second))
    parts = quarters(place, columns)
    parts[0].step()
    stream = tie(stream, parts[0])
    wdowns = [unslab_rows(place, weights, ranks, model_width), second]

    places, segment, path_depth = tree_layout(length, SEG)
    allowed = tree_mask(parents[0], places, segment, NSEG)
    trunk = 8 * SEG
    bias = jnp.where(allowed, 0.0, -1e30).T
    layer_rows = []
    for layer_index in range(L):
        pieces = split_layer(
            vectors[layer_index * layer_width : (layer_index + 1) * layer_width],
            model_width,
            head_size,
            up_proj.shape[2],
        )
        pieces.append(
            jnp.concatenate([pieces[2], jnp.zeros((head_size,), jnp.float32), pieces[3]])
        )
        layer_rows.append(
            jnp.stack([jnp.pad(p, (0, up_proj.shape[2] - p.shape[0])) for p in pieces])
        )
    inputs_kept = []
    matrices = []
    for layer_index in range(L):
        base = ranks * model_width + layer_index * cut_three
        wide = weights
        if layer_index == 0:
            stream, wdowns = tie((stream, wdowns), *parts)
            parts[1].step()
        wdown = wdowns[layer_index]
        matrices.append((wide, wdown, base))
        result, *saved = layer_forward(
            stream, layer_rows[layer_index], bias, wide, wdown, base, cut_one
        )
        inputs_kept.append((stream, saved))
        stream = result
        if layer_index == 0:
            stream = tie(stream, *parts)
            parts[2].step()
    stream = tie(stream, *parts)
    final_gain = vectors[L * layer_width : L * layer_width + model_width]
    final_shift = vectors[L * layer_width + model_width :]
    finished = norm_apply(stream, final_gain, final_shift).astype(jnp.bfloat16)
    slot_hot = own_slots[:, None] == jnp.arange(length, dtype=jnp.int32)[None, :]
    rows = jnp.dot(
        slot_hot.astype(jnp.bfloat16), finished, preferred_element_type=jnp.float32
    ).astype(jnp.bfloat16)

    held = tie(place.gather_z(rows), *parts)
    parts[3].step()
    held = place.spread_halves(held, orders)
    held = tie(held, *parts)
    group_rows = put_blocks(place, held).reshape(-1, model_width)
    parts = joined(parts)
    mine = parts[:, 0]
    theirs = place.swap(parts[:, 1], c=1)
    slice_low = put(place, [mine[None], theirs[None]], [(0, [0], everyone), (1, [0], everyone)], 1)
    slice_low = slice_low.reshape(model_width, slice_size)
    first_entry = place.v * shard_size + (place.z * 2 + place.c) * slice_size
    first_entry = first_entry.astype(jnp.int32).reshape(1)
    stats = head_forward(first_entry, group_rows, slice_low, all_targets)

    def combine(parts):
        top = functools.reduce(jnp.maximum, [p[0] for p in parts])
        return jnp.stack([top, tree_sum([p[1] * jnp.exp(p[0] - top) for p in parts])])

    whole = stats[:2]
    whole = combine([whole, place.swap(whole, c=1)])
    whole = combine([whole] + [place.swap(whole, v=m) for m in range(1, nv)])
    whole = combine([whole] + [place.swap(whole, z=m) for m in range(1, nz)])
    log_total = whole[0] + jnp.log(whole[1])
    own_total = lax.dynamic_slice_in_dim(
        log_total, ((place.z * 2 + place.c) * nv + place.v) * slot_count, slot_count
    )
    loss_local = jnp.sum(jnp.where(live, own_total, 0.0)) - jnp.sum(stats[2])
    count_local = jnp.sum(live.astype(jnp.float32))
    logits_low, rows_part = head_backward(
        first_entry, group_rows, log_total[None], slice_low, all_targets
    )
    rows_part = rows_part.reshape(nz, 2, nv, slot_count, model_width)
    rows_part = as_wide(pick(rows_part, place.c, 1)) + as_wide(
        place.swap(pick(rows_part, 1 - place.c, 1), c=1)
    )
    own_part = Held(rows_part)
    logits_low = tie(logits_low, own_part)
    rows_part = own_part.value
    head_grad = dot_first(group_rows, logits_low).astype(jnp.bfloat16)
    head_grad = head_grad.reshape(nz, 2, own_width, slice_size)
    head_parts = quarters(place, jnp.stack([pick(head_grad, place.z ^ m, 0) for m in range(nz)]))
    head_parts[0].step()
    rows_part = tree_sum(
        [pick(rows_part, place.v, 1)]
        + [as_wide(place.swap(as_low(pick(rows_part, place.v ^ m, 1)), v=m)) for m in range(1, nv)]
    )
    rows_part = tie(rows_part, *head_parts)
    rows_grad = tree_sum(
        [pick(rows_part, place.z, 0)]
        + [as_wide(place.swap(as_low(pick(rows_part, place.z ^ m, 0)), z=m)) for m in range(1, nz)]
    )
    rows_grad = tie(rows_grad, *head_parts)
    finished_grad = lax.dot_general(
        slot_hot.astype(jnp.float32),
        rows_grad,
        (((0,), (0,)), ((), ())),
        precision=HIGHEST,
        preferred_element_type=jnp.float32,
    )

    ignored, final_pull = jax.vjp(norm_apply, stream, final_gain, final_shift)
    stream_grad, grad_final_gain, grad_final_shift = final_pull(finished_grad)
    vector_parts = [None] * L

    def slabs(grad):
        grad = grad.reshape(nz * nv, ranks, shard_rows, model_width)
        return [grad[:, k].reshape(nz * nv * shard_rows, model_width) for k in range(ranks)]

    def unslab(columns):
        return jnp.concatenate(
            [columns[:, k * model_width : (k + 1) * model_width] for k in range(ranks)]
        )

    summed = [None] * L
    for layer_index in reversed(range(L)):
        kept_stream, saved = inputs_kept[layer_index]
        wide, wdown, base = matrices[layer_index]
        normed, mixed, attended, middle, normed_two, hidden, active = saved
        head_parts[1 if layer_index == 1 else 3].step()
        middle_grad, branch_grad, hidden_grad, late_vectors = mlp_backward(
            stream_grad, middle, hidden, layer_rows[layer_index], wide, wdown, base + cut_two
        )
        middle_grad, branch_grad, hidden_grad = tie(
            (middle_grad, branch_grad, hidden_grad), *head_parts
        )
        g_up = pair_grad(place, normed_two, hidden_grad)
        g_down = slabs(pair_grad_wide(place, active, branch_grad))
        g_mlp = Held([g_up] + g_down)
        middle_grad = tie(middle_grad, g_mlp, *head_parts)
        if layer_index == 1:
            head_parts[2].step()
        stream_grad, out_grad, mixed_grad, early_vectors = attn_backward(
            middle_grad, kept_stream, mixed, layer_rows[layer_index], bias, wide, base
        )
        stream_grad, out_grad, mixed_grad = tie((stream_grad, out_grad, mixed_grad), *head_parts)
        grads = Held(
            jnp.concatenate(
                g_mlp.value
                + [
                    pair_grad(place, normed, mixed_grad),
                    pair_grad(place, attended, out_grad),
                ],
                1,
            )
        )
        stream_grad = tie(stream_grad, grads, *head_parts)
        summed[layer_index] = lax.psum_scatter(
            grads.value, "vocab", scatter_dimension=0, tiled=True
        )
        vector_parts[layer_index] = (early_vectors, late_vectors)

    stream_grad, vector_parts = tie((stream_grad, vector_parts))
    vector_grads = [
        jnp.concatenate(
            [
                early_vectors[0, :model_width],
                early_vectors[1, :model_width],
                early_vectors[2, :model_width],
                early_vectors[2, model_width + head_size :],
                early_vectors[3, :model_width],
                late_vectors[0, :model_width],
                late_vectors[1, :model_width],
                late_vectors[2],
                late_vectors[3, :model_width],
            ]
        )
        for early_vectors, late_vectors in vector_parts
    ]
    sent = part_columns(place, stream_grad)
    sent = Traded(place, sent)
    sent.step()
    pos_grad = jnp.concatenate(
        [
            stream_grad[:trunk],
            jnp.sum(stream_grad[trunk : trunk + 4 * SEG].reshape(4, SEG, model_width), 0),
            jnp.sum(stream_grad[trunk + 4 * SEG :].reshape(8, SEG, model_width), 0),
        ]
    )
    vector_grad = jnp.concatenate(vector_grads + [grad_final_gain, grad_final_shift])
    flat = reduce_flat_core(place, vector_grad, pos_grad)
    flat, upper = tie((reduce_flat_plane(place, flat), summed[1]), sent, *head_parts)
    sent = sent.rest()
    sent = [sent[:, 0], place.swap(sent[:, 1], c=1)]
    sent = Held([place.spread_v(a, order) for a, order in zip(sent, orders)])
    flat_own = Held(reduce_flat_z(place, flat))
    upper = tie(upper, flat_own)
    upper = Held(spread_z(place, upper))
    lower = spread_z(place, tie(summed[0], sent, flat_own, upper))
    head_parts = joined(head_parts)
    mine = pick(head_parts, place.c, 1)
    theirs = place.swap(pick(head_parts, 1 - place.c, 1), c=1)
    head_grad = put(place, [mine[None], theirs[None]], [(0, [0], everyone), (1, [0], everyone)], 1)
    table_grad = add_rows(safe_ids, *[a.reshape(-1, LANES) for a in sent.value], head_grad)
    table_grad, lower = tie((table_grad, lower))
    summed = [tree_sum([as_wide(a) for a in parts]) for parts in (lower, upper.value)]
    up_end = up_proj.shape[2]
    down_end = up_end + ranks * model_width
    grad_up = jnp.stack([a[:, :up_end] for a in summed])
    grad_down = jnp.stack([unslab(a[:, up_end:down_end]) for a in summed])
    grad_qkv = jnp.stack([a[:, down_end : down_end + cut_one] for a in summed])
    grad_out = jnp.stack([a[:, down_end + cut_one :] for a in summed])
    owned_squares = (
        jnp.sum(grad_qkv * grad_qkv)
        + jnp.sum(grad_out * grad_out)
        + jnp.sum(grad_up * grad_up)
        + jnp.sum(grad_down * grad_down)
        + jnp.sum(table_grad * table_grad)
        + jnp.sum(flat_own.value * flat_own.value)
    )
    sums, vector_grad, pos_grad = gather_flat(
        place,
        flat_own.value,
        jnp.stack([owned_squares, loss_local, count_local]),
        vector_grad,
        pos_grad,
    )
    loss_sum, loss_count = sums[1], sums[2]
    grad_norm = jnp.sqrt(sums[0])
    factor = jnp.minimum(1.0, CLIP_NORM / grad_norm)
    states = (
        (table.T, table_mean.T, table_square.T, table_grad, LEARN_RATE),
        (qkv_proj, qkv_mean, qkv_square, grad_qkv, LEARN_RATE),
        (out_proj, out_mean, out_square, grad_out, LEARN_RATE),
        (up_proj, up_mean, up_square, grad_up, LEARN_RATE),
        (down_proj, down_mean, down_square, grad_down, LEARN_RATE),
        (vectors, vec_mean, vec_square, vector_grad, RATE_VEC),
        (pos_table, pos_mean, pos_square, pos_grad, LEARN_RATE),
    )
    results = [loss_sum, loss_count, grad_norm]
    for weight, mean, square, grad, rate in states:
        results.extend(adam_update(weight, mean, square, grad * factor, rate))
    results[3:6] = [a.T for a in results[3:6]]
    return tuple(results)


def solution(mesh):
    chips = mesh.devices.reshape(-1, 2, mesh.shape["vocab"])
    mesh = jax.sharding.Mesh(chips, ALL)
    return jax.shard_map(
        per_device,
        mesh=mesh,
        in_specs=(
            P(ALL),
            P(ALL, None),
            P(ALL, None),
            P(ALL, None),
            P("vocab", ("z", "core")),
            P("vocab", ("z", "core")),
            P("vocab", ("z", "core")),
            P(None, ALL, None),
            P(None, ALL, None),
            P(None, ALL, None),
            P(None, ALL, None),
            P(None, ALL, None),
            P(None, ALL, None),
            P(None, ALL, None),
            P(None, ALL, None),
            P(None, ALL, None),
            P(None, ALL, None),
            P(None, ALL, None),
            P(None, ALL, None),
            P(),
            P(),
            P(),
            P(),
            P(),
            P(),
        ),
        out_specs=(
            P(),
            P(),
            P(),
            P("vocab", ("z", "core")),
            P("vocab", ("z", "core")),
            P("vocab", ("z", "core")),
            P(None, ALL, None),
            P(None, ALL, None),
            P(None, ALL, None),
            P(None, ALL, None),
            P(None, ALL, None),
            P(None, ALL, None),
            P(None, ALL, None),
            P(None, ALL, None),
            P(None, ALL, None),
            P(None, ALL, None),
            P(None, ALL, None),
            P(None, ALL, None),
            P(),
            P(),
            P(),
            P(),
            P(),
            P(),
        ),
        check_vma=False,
    )
```

```python
import functools

import jax
import jax.numpy as jnp
from jax import lax
from jax.experimental import pallas as pl
from jax.experimental.pallas import tpu as pltpu
from jax.sharding import PartitionSpec as P

L = 2
NSEG = 13
STEP = 10
SEG = 16


NORM_EPS = 1e-05
BETA_ONE = 0.9
BETA_TWO = 0.999
ADAM_EPS = 1e-08
LEARN_RATE = 0.1
RATE_VEC = 0.5
WEIGHT_DECAY = 0.1
CLIP_NORM = 0.1
HIGHEST = lax.Precision.HIGHEST
GELU_SCALE = 0.7978845608028654
GELU_CUBE = 0.044715
ALL = ("z", "core", "vocab")
ROWS_STEP = 2560
UNROLL = 64
HEAD_ROWS = 512
TURN = 512
MIB = 1024 * 1024
COST_SCALE = 1e15
LANES = 128


class Place:
    def __init__(self):
        self.nv = lax.axis_size("vocab")
        self.nz = lax.axis_size("z")
        self.count = self.nv * self.nz * 2
        self.v = lax.axis_index("vocab")
        self.z = lax.axis_index("z")
        self.c = lax.axis_index("core")
        self.where = jnp.stack([self.z, self.c, self.v]).astype(jnp.int32)
        self.core_alone = jnp.stack([self.z * 0, self.c, self.v * 0]).astype(jnp.int32)
        self.bits = [1 << i for i in range(self.nv.bit_length() - 1)]

    def swap(self, a, v=0, c=0, z=0):
        mask = (z * 2 + c) * self.nv + v
        return lax.ppermute(a, ALL, [(i, i ^ mask) for i in range(self.count)])

    def gather_z(self, a):
        return jnp.stack([a] + [self.swap(a, z=m) for m in range(1, self.nz)])

    def gather_v(self, a):
        return jnp.stack([a] + [self.swap(a, v=m) for m in range(1, self.nv)])

    def gather_c(self, a):
        return jnp.stack([a, self.swap(a, c=1)])

    def spread_v(self, a, order):
        masks = [0]
        held = a[None]
        for bit in order:
            held = jnp.concatenate([held, self.swap(held, v=bit)])
            masks = masks + [m ^ bit for m in masks]
        if masks == sorted(masks):
            return held
        return jnp.stack([held[masks.index(m)] for m in range(self.nv)])

    def spread_halves(self, held, orders):
        half = self.nz // 2
        return jnp.concatenate(
            [self.spread_v(held[:half], orders[0]), self.spread_v(held[half:], orders[1])], 1
        )

    def reduce_v(self, a, order, axis):
        left = list(reversed(self.bits))
        a = a.reshape(a.shape[:axis] + (2,) * len(left) + a.shape[axis + 1 :])
        for bit in order:
            at = axis + left.index(bit)
            a = lax.index_in_dim(a, 0, at, False) + self.swap(
                lax.index_in_dim(a, 1, at, False), v=bit
            )
            left.remove(bit)
        return a


def pick(a, index, axis):
    return lax.dynamic_index_in_dim(a, index, axis, False)


def tree_sum(terms):
    while len(terms) > 1:
        terms = [terms[i] + terms[i + 1] for i in range(0, len(terms), 2)]
    return terms[0]


def cost(seconds):
    return pl.CostEstimate(flops=int(seconds * COST_SCALE), transcendentals=0, bytes_accessed=0)


def put_kernel(slots, nv, where_ref, *refs):
    pieces, out = refs[: len(slots)], refs[-1]
    z, c = where_ref[0], where_ref[1]
    v = where_ref[2] if nv > 1 else 0
    for piece, (core, masks, z_masks) in zip(pieces, slots):
        for k, mask in enumerate(masks):
            for i, m in enumerate(z_masks):
                row = ((z ^ m) * 2 + (c ^ core)) * nv + (v ^ mask)
                out[row] = piece[k, i]


def put(place, pieces, slots, nv=None):
    nv = place.nv if nv is None else nv
    count = 2 * place.nz * nv
    rows, width = pieces[0].shape[2:]
    return pl.pallas_call(
        functools.partial(put_kernel, slots, nv),
        out_shape=jax.ShapeDtypeStruct((count, rows, width), pieces[0].dtype),
        in_specs=[pl.BlockSpec(memory_space=pltpu.SMEM)]
        + [pl.BlockSpec(memory_space=pltpu.VMEM)] * len(pieces),
        out_specs=pl.BlockSpec(memory_space=pltpu.VMEM),
        cost_estimate=cost(3e-6),
        compiler_params=pltpu.CompilerParams(vmem_limit_bytes=4 * count * rows * width + 4 * MIB),
    )(place.where, *pieces)


def owner_hot(where_ref, depth, rows, nv, nz, order):
    part = rows // (nv * nz)
    column = lax.broadcasted_iota(jnp.int32, (1, rows), 1)
    block = jnp.zeros((1, rows), jnp.int32)
    for k in range(1, nv * nz):
        block = block + jnp.where(column >= k * part, 1, 0)
    apart = jnp.zeros((1, rows), jnp.int32)
    for k, bit in enumerate(reversed(order)):
        apart = apart + jnp.where((block & (nz << k)) != 0, bit, 0)
    owner = ((block & (nz - 1)) ^ where_ref[0]) * 2 + where_ref[1]
    owner = owner * nv + (apart ^ where_ref[2])
    row = owner * part + column - block * part
    return (lax.broadcasted_iota(jnp.int32, (depth, rows), 0) == row).astype(jnp.bfloat16)


def pair_kernel(
    nv, nz, order, where_ref, x_ref, other_ref, y_ref, y_other_ref, out_ref, left_ref, left_other_ref
):
    @pl.when(pl.program_id(0) == 0)
    def _():
        hot = owner_hot(where_ref, x_ref.shape[1], left_ref.shape[1], nv, nz, order)
        left_ref[...] = jnp.dot(x_ref[...], hot, preferred_element_type=jnp.float32).astype(
            jnp.bfloat16
        )
        left_other_ref[...] = jnp.dot(
            other_ref[...], hot, preferred_element_type=jnp.float32
        ).astype(jnp.bfloat16)

    out_ref[...] = (
        dot_first(left_ref[...], y_ref[...]) + dot_first(left_other_ref[...], y_other_ref[...])
    ).astype(jnp.bfloat16)


def pair_grad(place, x, y):
    length, depth = x.shape
    rows, width = depth // 2, y.shape[1]
    block = 768 if width % 768 == 0 else width
    whole = pl.BlockSpec((length, depth), lambda i: (0, 0))
    part = pl.BlockSpec((length, block), lambda i: (0, i))
    return pl.pallas_call(
        functools.partial(pair_kernel, place.nv, place.nz, list(reversed(place.bits))),
        out_shape=jax.ShapeDtypeStruct((rows, width), jnp.bfloat16),
        grid=(width // block,),
        in_specs=[pl.BlockSpec(memory_space=pltpu.SMEM), whole, whole, part, part],
        out_specs=pl.BlockSpec((rows, block), lambda i: (0, i)),
        scratch_shapes=[pltpu.VMEM((length, rows), jnp.bfloat16)] * 2,
        cost_estimate=cost(5e-6),
        compiler_params=pltpu.CompilerParams(vmem_limit_bytes=14 * MIB),
    )(place.core_alone, x, place.swap(x, c=1), y, place.swap(y, c=1))


def wide_kernel(nv, order, where_ref, x_ref, other_ref, y_ref, y_other_ref, out_ref):
    total = dot_first(x_ref[...], y_ref[...]) + dot_first(other_ref[...], y_other_ref[...])
    rows = total.shape[0] // nv
    for v in range(nv):
        apart = where_ref[2] ^ v
        position = 0
        for bit in order:
            position = position * 2 + jnp.where((apart & bit) != 0, 1, 0)
        out_ref[position, 0] = total[v * rows : (v + 1) * rows].astype(jnp.bfloat16)


def pair_grad_wide(place, x, y):
    length, depth = x.shape
    width = y.shape[1]
    block = depth // (2 * place.nz)
    rows = block // place.nv
    other = place.swap(x, c=1)
    if block % 128 == 0:
        part = pl.BlockSpec((length, block), lambda i, where: (0, 2 * i + where[1]))
    else:
        x, other = (a.reshape(length, -1, block).transpose(1, 0, 2) for a in (x, other))
        part = pl.BlockSpec((None, length, block), lambda i, where: (2 * i + where[1], 0, 0))
    whole = pl.BlockSpec((length, width), lambda i, where: (0, 0))
    shape, block_shape = (place.nv, place.nz, rows, width), (place.nv, 1, rows, width)
    where_out = lambda i, where: (0, i ^ where[0], 0, 0)
    return pl.pallas_call(
        functools.partial(wide_kernel, place.nv, list(reversed(place.bits))),
        out_shape=jax.ShapeDtypeStruct(shape, jnp.bfloat16),
        grid_spec=pltpu.PrefetchScalarGridSpec(
            num_scalar_prefetch=1,
            grid=(place.nz,),
            in_specs=[part, part, whole, whole],
            out_specs=pl.BlockSpec(block_shape, where_out),
        ),
        cost_estimate=cost(5e-6),
        compiler_params=pltpu.CompilerParams(vmem_limit_bytes=14 * MIB),
    )(place.core_alone, x, other, y, place.swap(y, c=1)).reshape(depth // 2, width)


def tie(main, *steps):
    main, values = lax.optimization_barrier((main, [s.value for s in steps]))
    for s, value in zip(steps, values):
        s.value = value
    return main


class Traded:
    def __init__(self, place, value):
        self.place = place
        self.value = value

    def step(self):
        place, a = self.place, self.value
        self.value = [a[0]] + [place.swap(a[m], z=m) for m in range(1, place.nz)]

    def rest(self):
        return jnp.stack(self.value)


def quarters(place, value):
    part = value.shape[-1] // 4
    return [Traded(place, value[..., k * part : (k + 1) * part]) for k in range(4)]


def spread_z(place, a):
    a = a.reshape(place.nz, -1, a.shape[1])
    return [pick(a, place.z, 0)] + [
        place.swap(pick(a, place.z ^ m, 0), z=m) for m in range(1, place.nz)
    ]


def joined(trades):
    return jnp.concatenate([t.rest() for t in trades], -1)


class Held:
    def __init__(self, value):
        self.value = value


def as_wide(a):
    return a.astype(jnp.float32)


def as_low(a):
    return a.astype(jnp.bfloat16)


def reduce_flat_core(place, vector, table):
    length = vector.shape[0]
    first = -(-length // 1024) * 8
    second = table.size // 128
    rows = -(-(first + second) // (place.count * 8)) * 8
    a = jnp.concatenate(
        [jnp.pad(vector, (0, first * 128 - length)).reshape(first, 128), table.reshape(second, 128)]
    )
    a = jnp.pad(a, ((0, place.count * rows - first - second), (0, 0)))
    a = a.reshape(place.nz, 2, place.nv, rows, 128)
    return pick(a, place.c, 1) + place.swap(pick(a, 1 - place.c, 1), c=1)


def reduce_flat_plane(place, a):
    bits = list(reversed(place.bits))
    a = a.reshape((place.nz,) + (2,) * len(bits) + a.shape[2:])
    for bit in bits:
        mine = (place.v // bit) % 2
        a = pick(a, mine, 1) + place.swap(pick(a, 1 - mine, 1), v=bit)
    return a


def reduce_flat_z(place, a):
    count = place.nz.bit_length() - 1
    a = a.reshape((2,) * count + a.shape[1:])
    for step in reversed(range(count)):
        mine = (place.z >> step) % 2
        a = pick(a, mine, 0) + place.swap(pick(a, 1 - mine, 0), z=1 << step)
    return a


def unslab_kernel(slabs_ref, out_ref):
    ranks = out_ref.shape[1] // slabs_ref.shape[1]
    rows, width = slabs_ref.shape[1], out_ref.shape[2]
    for k in range(ranks):
        out_ref[:, k * rows : (k + 1) * rows, :] = slabs_ref[:, :, k * width : (k + 1) * width]


def unslab_rows(place, gathered, ranks, width):
    count, total = place.count, ranks * width
    rows = gathered.shape[0] // count
    if rows % 8:
        slabs = gathered[:, :total].reshape(count, rows, ranks, width)
        return slabs.transpose(0, 2, 1, 3).reshape(-1, width)
    return pl.pallas_call(
        unslab_kernel,
        out_shape=jax.ShapeDtypeStruct((count, rows * ranks, width), gathered.dtype),
        grid=(count // 4,),
        in_specs=[pl.BlockSpec((4, rows, total), lambda i: (i, 0, 0))],
        out_specs=pl.BlockSpec((4, rows * ranks, width), lambda i: (i, 0, 0)),
        cost_estimate=cost(7e-6),
    )(gathered.reshape(count, rows, -1)).reshape(-1, width)


def gather_flat(place, own, scalars, vector, table):
    length, rows = vector.shape[0], own.shape[0]
    first, second = -(-length // 1024) * 8, table.size // 128
    own = jnp.concatenate([own, jnp.pad(scalars[None], ((0, 7), (0, 128 - scalars.shape[0])))])
    whole = gather_blocks(place, own)
    scalars = jnp.sum(whole[:, rows, : scalars.shape[0]], 0)
    whole = whole[:, :rows].reshape(-1, 128)
    return (
        scalars,
        whole[:first].reshape(-1)[:length],
        whole[first : first + second].reshape(table.shape),
    )


def put_blocks(place, held):
    everyone = list(range(place.nz))
    masks = list(range(place.nv))
    return put(place, [held, place.swap(held, c=1)], [(0, masks, everyone), (1, masks, everyone)])


def gather_blocks(place, block):
    return put_blocks(place, place.gather_v(place.gather_z(block)))


def column_hot(where_ref, part, width, total):
    first = (part ^ (where_ref[0] * 2 + where_ref[1])) * width
    rows = lax.broadcasted_iota(jnp.int32, (width, total), 0) + first
    return (rows == lax.broadcasted_iota(jnp.int32, (width, total), 1)).astype(jnp.bfloat16)


def embed_kernel(where_ref, table_ref, *refs):
    pieces, out_ref = refs[:-1], refs[-1]
    total_width = out_ref.shape[1]
    width = total_width // (2 * len(pieces))
    total = jnp.zeros(out_ref.shape, jnp.float32)
    for m, piece in enumerate(pieces):
        for c in range(2):
            hot = column_hot(where_ref, 2 * m + c, width, total_width)
            total = total + jnp.dot(
                piece[c, :, :width], hot, preferred_element_type=jnp.float32
            )
    out_ref[...] = total
    trunk = 8 * SEG
    out_ref[:trunk, :] += table_ref[:trunk, :]
    for k in range(12):
        at = trunk + k * SEG
        row = trunk if k < 4 else trunk + SEG
        out_ref[at : at + SEG, :] += table_ref[row : row + SEG, :]


def embed(place, pieces, table):
    length, width = pieces[0].shape[1:]
    return pl.pallas_call(
        embed_kernel,
        out_shape=jax.ShapeDtypeStruct((length, table.shape[1]), jnp.float32),
        in_specs=[pl.BlockSpec(memory_space=pltpu.SMEM)]
        + [pl.BlockSpec(memory_space=pltpu.VMEM)] * (1 + len(pieces)),
        out_specs=pl.BlockSpec(memory_space=pltpu.VMEM),
        cost_estimate=cost(1.7e-6),
        compiler_params=pltpu.CompilerParams(vmem_limit_bytes=16 * MIB),
    )(place.where, table, *pieces)


def part_kernel(where_ref, grad_ref, out_ref):
    grad = grad_ref[...].astype(jnp.bfloat16)
    nz = out_ref.shape[0]
    width = grad.shape[1] // (2 * nz)
    out_ref[...] = jnp.zeros_like(out_ref)
    for m in range(nz):
        for c in range(2):
            hot = column_hot(where_ref, 2 * m + c, width, grad.shape[1])
            out_ref[m, c, :, :width] = dot_last(grad, hot).astype(jnp.bfloat16)


def part_columns(place, grad):
    length, total = grad.shape
    return pl.pallas_call(
        part_kernel,
        out_shape=jax.ShapeDtypeStruct((place.nz, 2, length, LANES), jnp.bfloat16),
        in_specs=[
            pl.BlockSpec(memory_space=pltpu.SMEM),
            pl.BlockSpec(memory_space=pltpu.VMEM),
        ],
        out_specs=pl.BlockSpec(memory_space=pltpu.VMEM),
        cost_estimate=cost(1.8e-6),
        compiler_params=pltpu.CompilerParams(vmem_limit_bytes=16 * MIB),
    )(place.where, grad)


def turned(value, axis):
    size = max(value.shape)
    same = lax.broadcasted_iota(jnp.int32, (size, size), 0) == lax.broadcasted_iota(
        jnp.int32, (size, size), 1
    )
    return jnp.sum(jnp.where(same, value, jnp.zeros((), value.dtype)), axis, keepdims=True)


def hits(first_ref, targets_ref, shape):
    column = turned(targets_ref[...], 1) - first_ref[0]
    return column == lax.broadcasted_iota(jnp.int32, shape, 1)


def logits_kernel(first_ref, rows_ref, table_ref, targets_ref, stats_ref):
    logits = jnp.dot(rows_ref[...], table_ref[...], preferred_element_type=jnp.float32)
    top = jnp.max(logits, 1, keepdims=True)
    exps = jnp.exp(logits - top)
    picked = jnp.where(hits(first_ref, targets_ref, logits.shape), logits, 0.0)
    stats_ref[0:1, :] = turned(top, 0)
    stats_ref[1:2, :] = turned(jnp.sum(exps, 1, keepdims=True), 0)
    stats_ref[2:3, :] = turned(jnp.sum(picked, 1, keepdims=True), 0)


def head_forward(first, rows, table, targets):
    count, width = rows.shape
    size = table.shape[1]
    return pl.pallas_call(
        logits_kernel,
        out_shape=jax.ShapeDtypeStruct((3, count), jnp.float32),
        grid=(count // HEAD_ROWS,),
        in_specs=[
            pl.BlockSpec(memory_space=pltpu.SMEM),
            pl.BlockSpec((HEAD_ROWS, width), lambda i: (i, 0)),
            pl.BlockSpec((width, size), lambda i: (0, 0)),
            pl.BlockSpec((1, HEAD_ROWS), lambda i: (0, i)),
        ],
        out_specs=pl.BlockSpec((3, HEAD_ROWS), lambda i: (0, i)),
        cost_estimate=cost(11.6e-6),
        compiler_params=pltpu.CompilerParams(vmem_limit_bytes=24 * MIB),
    )(first, rows, table, targets)


def slopes_kernel(first_ref, rows_in_ref, total_ref, table_ref, targets_ref, slopes_ref, rows_ref):
    logits = jnp.dot(rows_in_ref[...], table_ref[...], preferred_element_type=jnp.float32)
    exps = jnp.exp(logits - turned(total_ref[...], 1))
    hit = hits(first_ref, targets_ref, exps.shape)
    alive = turned(targets_ref[...], 1) >= 0
    slopes = jnp.where(alive, exps - jnp.where(hit, 1.0, 0.0), 0.0).astype(jnp.bfloat16)
    slopes_ref[...] = slopes
    rows_ref[...] = dot_last(slopes, table_ref[...]).astype(jnp.bfloat16)


def head_backward(first, rows, total, table, targets):
    count, width = rows.shape
    size = table.shape[1]
    return pl.pallas_call(
        slopes_kernel,
        out_shape=(
            jax.ShapeDtypeStruct((count, size), jnp.bfloat16),
            jax.ShapeDtypeStruct((count, width), jnp.bfloat16),
        ),
        grid=(count // HEAD_ROWS,),
        in_specs=[
            pl.BlockSpec(memory_space=pltpu.SMEM),
            pl.BlockSpec((HEAD_ROWS, width), lambda i: (i, 0)),
            pl.BlockSpec((1, HEAD_ROWS), lambda i: (0, i)),
            pl.BlockSpec((width, size), lambda i: (0, 0)),
            pl.BlockSpec((1, HEAD_ROWS), lambda i: (0, i)),
        ],
        out_specs=(
            pl.BlockSpec((HEAD_ROWS, size), lambda i: (i, 0)),
            pl.BlockSpec((HEAD_ROWS, width), lambda i: (i, 0)),
        ),
        cost_estimate=cost(16e-6),
        compiler_params=pltpu.CompilerParams(vmem_limit_bytes=24 * MIB),
    )(first, rows, total, table, targets)


def cut_kernel(where_ref, columns_ref, out_ref):
    out_ref[0, 0] = columns_ref[...].astype(out_ref.dtype)


def cut(place, columns):
    width, size = columns.shape
    part = size // (2 * place.nz)
    if part % 128:
        order = jnp.arange(2 * place.nz) ^ (place.z * 2 + place.c)
        parts = columns.astype(jnp.bfloat16).reshape(width, 2 * place.nz, part).transpose(1, 0, 2)
        return jnp.take(parts, order, axis=0).reshape(place.nz, 2, width, part)
    return pl.pallas_call(
        cut_kernel,
        out_shape=jax.ShapeDtypeStruct((place.nz, 2, width, part), jnp.bfloat16),
        grid_spec=pltpu.PrefetchScalarGridSpec(
            num_scalar_prefetch=1,
            grid=(2 * place.nz,),
            in_specs=[
                pl.BlockSpec((width, part), lambda i, where: (0, i ^ (where[0] * 2 + where[1])))
            ],
            out_specs=pl.BlockSpec((1, 1, width, part), lambda i, where: (i // 2, i % 2, 0, 0)),
        ),
        cost_estimate=cost(7e-6),
    )(place.where, columns)


def find_kernel(ids_ref, columns_ref, out_ref, rows_ref, found_ref):
    size = columns_ref.shape[1]

    @pl.when(pl.program_id(0) == 0)
    def _():
        def turn(i, carry):
            at = pl.multiple_of(i * TURN, TURN)
            part = columns_ref[:, pl.ds(at, TURN)].astype(jnp.bfloat16).astype(jnp.float32)
            rows_ref[pl.ds(at, TURN), : part.shape[0]] = part.T
            return carry

        rows_ref[:, columns_ref.shape[0] :] = jnp.zeros(
            (rows_ref.shape[0], LANES - columns_ref.shape[0]), jnp.float32
        )

        lax.fori_loop(0, size // TURN, turn, 0)
        rows_ref[pl.ds(size, 8), :] = jnp.zeros((8, rows_ref.shape[1]), jnp.float32)

    first = pl.program_id(0) * out_ref.shape[0]

    def body(i, carry):
        for u in range(UNROLL):
            t = i * UNROLL + u
            found_ref[pl.ds(t, 1), :] = rows_ref[pl.ds(ids_ref[first + t], 1), :]
        return carry

    lax.fori_loop(0, out_ref.shape[0] // UNROLL, body, 0)
    out_ref[...] = found_ref[...].astype(out_ref.dtype)


def find_rows(ids, columns):
    width, size = columns.shape
    return pl.pallas_call(
        find_kernel,
        out_shape=jax.ShapeDtypeStruct((ids.shape[0], LANES), jnp.bfloat16),
        grid_spec=pltpu.PrefetchScalarGridSpec(
            num_scalar_prefetch=1,
            grid=(ids.shape[0] // ROWS_STEP,),
            in_specs=[pl.BlockSpec(memory_space=pltpu.VMEM)],
            out_specs=pl.BlockSpec((ROWS_STEP, LANES), lambda i, ids: (i, 0)),
            scratch_shapes=[
                pltpu.VMEM((size + 8, LANES), jnp.float32),
                pltpu.VMEM((ROWS_STEP, LANES), jnp.float32),
            ],
        ),
        cost_estimate=cost(18e-6),
        compiler_params=pltpu.CompilerParams(vmem_limit_bytes=24 * MIB),
    )(ids, columns)


def add_kernel(ids_ref, low_ref, more_ref, head_ref, out_ref, rows_ref, *parts):
    step = pl.program_id(0)
    first = step * rows_ref.shape[0]
    size = out_ref.shape[1]
    early = step < pl.num_programs(0) // 2
    rows_ref[...] = jnp.where(early, low_ref[...], more_ref[...]).astype(jnp.float32)

    @pl.when(step == 0)
    def _():
        for part in parts:
            part[...] = jnp.zeros_like(part)

    def body(i, carry):
        for u in range(UNROLL):
            t = i * UNROLL + u
            part = parts[u % len(parts)]
            where = pl.ds(ids_ref[first + t], 1)
            part[where, :] = part[where, :] + rows_ref[pl.ds(t, 1), :]
        return carry

    lax.fori_loop(0, rows_ref.shape[0] // UNROLL, body, 0)

    @pl.when(step == pl.num_programs(0) - 1)
    def _():
        def turn(i, carry):
            at = pl.ds(pl.multiple_of(i * TURN, TURN), TURN)
            total = tree_sum([part[at, :] for part in parts])
            part = head_ref.shape[2]
            head = head_ref[i * TURN // part, :, pl.ds(pl.multiple_of(i * TURN % part, TURN), TURN)]
            out_ref[:, at] = total.T[: out_ref.shape[0]] + head.astype(jnp.float32)
            return carry

        lax.fori_loop(0, size // TURN, turn, 0)


def add_rows(ids, rows, more, head):
    width, size = head.shape[1], head.shape[0] * head.shape[2]
    if head.shape[2] % TURN:
        head = head.transpose(1, 0, 2).reshape(1, width, size)
    steps = rows.shape[0] // ROWS_STEP
    return pl.pallas_call(
        add_kernel,
        out_shape=jax.ShapeDtypeStruct((width, size), jnp.float32),
        grid_spec=pltpu.PrefetchScalarGridSpec(
            num_scalar_prefetch=1,
            grid=(ids.shape[0] // ROWS_STEP,),
            in_specs=[
                pl.BlockSpec((ROWS_STEP, LANES), lambda i, ids: (jnp.minimum(i, steps - 1), 0)),
                pl.BlockSpec((ROWS_STEP, LANES), lambda i, ids: (jnp.maximum(i - steps, 0), 0)),
                pl.BlockSpec(memory_space=pltpu.VMEM),
            ],
            out_specs=pl.BlockSpec(memory_space=pltpu.VMEM),
            scratch_shapes=[pltpu.VMEM((ROWS_STEP, LANES), jnp.float32)]
            + [pltpu.VMEM((size + 8, LANES), jnp.float32)] * 4,
        ),
        cost_estimate=cost(25e-6),
        compiler_params=pltpu.CompilerParams(vmem_limit_bytes=40 * MIB),
    )(ids, rows, more, head)


def norm_apply(stream, gain, shift):
    center = stream - jnp.mean(stream, -1, keepdims=True)
    spread = jnp.mean(center * center, -1, keepdims=True)
    return center * lax.rsqrt(spread + NORM_EPS) * gain + shift


def norm_back(stream, gain, grad):
    center = stream - jnp.mean(stream, -1, keepdims=True)
    scale = lax.rsqrt(jnp.mean(center * center, -1, keepdims=True) + NORM_EPS)
    unit = center * scale
    inner = grad * gain
    part = inner - jnp.mean(inner, -1, keepdims=True)
    part = scale * (part - unit * jnp.mean(inner * unit, -1, keepdims=True))
    return part, jnp.sum(grad * unit, 0, keepdims=True), jnp.sum(grad, 0, keepdims=True)


def gelu_parts(value):
    inner = GELU_SCALE * (value + GELU_CUBE * value * value * value)
    bend = jnp.tanh(inner)
    half = 0.5 * (1.0 + bend)
    slope = GELU_SCALE * (1.0 + 3.0 * GELU_CUBE * value * value)
    return value * half, half + 0.5 * value * (1.0 - bend * bend) * slope


def split_layer(vector_row, model_width, head_size, hidden_width):
    widths = [model_width] * 3 + [head_size] + [model_width] * 3 + [hidden_width, model_width]
    pieces = []
    offset = 0
    for width in widths:
        pieces.append(vector_row[offset : offset + width])
        offset += width
    return pieces


def tree_layout(total, seg_len):
    places = jnp.arange(total, dtype=jnp.int32)
    trunk = 8 * seg_len
    beyond = jnp.maximum(places - trunk, 0) // seg_len
    segment = jnp.where(places < trunk, 0, 1 + beyond)
    offset = places - trunk - beyond * seg_len
    path_depth = jnp.where(
        places < trunk, places, jnp.where(segment <= 4, trunk + offset, trunk + seg_len + offset)
    )
    return (places, segment, path_depth)


def tree_mask(parent_row, places, segment, count):
    labels = jnp.arange(count, dtype=jnp.int32)
    parent_hot = (parent_row[:, None] == labels[None, :]).astype(jnp.float32)
    grand_hot = jnp.dot(parent_hot, parent_hot, precision=HIGHEST)
    ancestor = jnp.eye(count, dtype=jnp.float32) + parent_hot + grand_hot
    seg_hot = (segment[:, None] == labels[None, :]).astype(jnp.float32)
    reach = jnp.dot(jnp.dot(seg_hot, ancestor, precision=HIGHEST), seg_hot.T, precision=HIGHEST)
    return (reach > 0.5) & (places[None, :] <= places[:, None])


def dot_first(left, right):
    return lax.dot_general(
        left, right, (((0,), (0,)), ((), ())), preferred_element_type=jnp.float32
    )


def dot_last(left, right):
    return lax.dot_general(
        left, right, (((1,), (1,)), ((), ())), preferred_element_type=jnp.float32
    )


def column_sum(grad_low):
    return jnp.sum(grad_low.astype(jnp.float32), 0)


def fetch(copies):
    for copy in copies:
        copy.start()
    return copies


def head_probs(mixed_ref, bias, h, keys, size, model_width):
    queries = mixed_ref[:, h * size : (h + 1) * size]
    scores = dot_last(keys, queries) * size ** (-0.5) + bias
    exps = jnp.exp(scores - jnp.max(scores, 0, keepdims=True))
    return queries, exps * (1.0 / jnp.sum(exps, 0, keepdims=True))


def forward_kernel(
    base,
    stream_ref,
    row_ref,
    bias_ref,
    wide_ref,
    down_ref,
    result_ref,
    normed_ref,
    mixed_ref,
    attended_ref,
    middle_ref,
    normed_two_ref,
    hidden_ref,
    active_ref,
    qkv_low,
    out_low,
    up_low,
    down_low,
    sems,
):
    model_width = stream_ref.shape[1]
    size = (qkv_low.shape[1] - model_width) // 2
    cuts = (qkv_low.shape[1], qkv_low.shape[1] + model_width)
    copies = fetch(
        [
            pltpu.make_async_copy(wide_ref.at[:, pl.ds(base, cuts[0])], qkv_low, sems.at[0]),
            pltpu.make_async_copy(
                wide_ref.at[:, pl.ds(base + cuts[0], model_width)], out_low, sems.at[1]
            ),
            pltpu.make_async_copy(
                wide_ref.at[:, pl.ds(base + cuts[1], up_low.shape[1])], up_low, sems.at[2]
            ),
            pltpu.make_async_copy(down_ref, down_low, sems.at[3]),
        ]
    )

    def row(k, width=model_width):
        return row_ref[k : k + 1, :width]

    stream = stream_ref[...]
    normed = norm_apply(stream, row(0), row(1)).astype(jnp.bfloat16)
    normed_ref[...] = normed
    copies[0].wait()
    mixed = jnp.dot(normed, qkv_low[...], preferred_element_type=jnp.float32)
    mixed = (mixed + row(9, mixed.shape[1])).astype(jnp.bfloat16)
    mixed_ref[...] = mixed
    keys, values = mixed[:, model_width : model_width + size], mixed[:, model_width + size :]
    for h in range(model_width // size):
        ignored, probs = head_probs(mixed_ref, bias_ref[...], h, keys, size, model_width)
        attended_ref[:, h * size : (h + 1) * size] = dot_first(
            probs.astype(jnp.bfloat16), values
        ).astype(jnp.bfloat16)
    copies[1].wait()
    middle = stream + jnp.dot(
        attended_ref[...], out_low[...], preferred_element_type=jnp.float32
    )
    middle = middle + row(4)
    middle_ref[...] = middle
    normed_two = norm_apply(middle, row(5), row(6)).astype(jnp.bfloat16)
    normed_two_ref[...] = normed_two
    copies[2].wait()
    copies[3].wait()
    total = middle + row(8)
    for k in range(up_low.shape[1] // model_width):
        at = slice(k * model_width, (k + 1) * model_width)
        hidden = jnp.dot(normed_two, up_low[:, at], preferred_element_type=jnp.float32)
        hidden = hidden + row_ref[7:8, at]
        hidden_ref[:, at] = hidden
        active = gelu_parts(hidden)[0].astype(jnp.bfloat16)
        active_ref[:, at] = active
        total = total + jnp.dot(active, down_low[at, :], preferred_element_type=jnp.float32)
    result_ref[...] = total


def shape_of(shape, kind):
    return jax.ShapeDtypeStruct(shape, kind)


VMEM = pl.BlockSpec(memory_space=pltpu.VMEM)
ANY = pl.BlockSpec(memory_space=pltpu.HBM)


def layer_forward(stream, row, bias, wide, down, base, row_width):
    length, model_width = stream.shape
    hidden_width = down.shape[0]
    mixed_width = row_width
    f32, low = jnp.float32, jnp.bfloat16
    return pl.pallas_call(
        functools.partial(forward_kernel, base),
        out_shape=(
            shape_of((length, model_width), f32),
            shape_of((length, model_width), low),
            shape_of((length, mixed_width), low),
            shape_of((length, model_width), low),
            shape_of((length, model_width), f32),
            shape_of((length, model_width), low),
            shape_of((length, hidden_width), f32),
            shape_of((length, hidden_width), low),
        ),
        in_specs=[VMEM, VMEM, VMEM, ANY, ANY],
        out_specs=(VMEM,) * 8,
        scratch_shapes=[
            pltpu.VMEM((model_width, mixed_width), low),
            pltpu.VMEM((model_width, model_width), low),
            pltpu.VMEM((model_width, hidden_width), low),
            pltpu.VMEM((hidden_width, model_width), low),
            pltpu.SemaphoreType.DMA((4,)),
        ],
        cost_estimate=cost(12e-6),
        compiler_params=pltpu.CompilerParams(vmem_limit_bytes=46 * MIB),
    )(stream, row, bias, wide, down)


def mlp_kernel(
    first,
    grad_ref,
    middle_ref,
    hidden_ref,
    row_ref,
    wide_ref,
    down_ref,
    middle_grad_ref,
    branch_ref,
    hidden_grad_ref,
    vector_ref,
    up_low,
    down_low,
    sems,
):
    model_width = grad_ref.shape[1]
    start = first
    copies = fetch(
        [
            pltpu.make_async_copy(down_ref, down_low, sems.at[0]),
            pltpu.make_async_copy(
                wide_ref.at[:, start : start + up_low.shape[1]], up_low, sems.at[1]
            ),
        ]
    )
    grad = grad_ref[...]
    branch = grad.astype(jnp.bfloat16)
    branch_ref[...] = branch
    vector_ref[...] = jnp.zeros_like(vector_ref)
    vector_ref[3:4, :model_width] = jnp.sum(branch.astype(jnp.float32), 0, keepdims=True)
    copies[0].wait()
    copies[1].wait()
    total = jnp.zeros_like(grad)
    for k in range(up_low.shape[1] // model_width):
        at = slice(k * model_width, (k + 1) * model_width)
        slope = gelu_parts(hidden_ref[:, at])[1]
        hidden_grad = (slope * dot_last(branch, down_low[at, :])).astype(jnp.bfloat16)
        hidden_grad_ref[:, at] = hidden_grad
        vector_ref[2:3, at] = jnp.sum(hidden_grad.astype(jnp.float32), 0, keepdims=True)
        total = total + dot_last(hidden_grad, up_low[:, at])
    part, gain_grad, shift_grad = norm_back(middle_ref[...], row_ref[5:6, :model_width], total)
    vector_ref[0:1, :model_width] = gain_grad
    vector_ref[1:2, :model_width] = shift_grad
    middle_grad_ref[...] = grad + part


def mlp_backward(grad, middle, hidden, row, wide, down, first):
    length, model_width = grad.shape
    hidden_width = down.shape[0]
    f32, low = jnp.float32, jnp.bfloat16
    return pl.pallas_call(
        functools.partial(mlp_kernel, first),
        out_shape=(
            shape_of((length, model_width), f32),
            shape_of((length, model_width), low),
            shape_of((length, hidden_width), low),
            shape_of((8, hidden_width), f32),
        ),
        in_specs=[VMEM, VMEM, VMEM, VMEM, ANY, ANY],
        out_specs=(VMEM,) * 4,
        scratch_shapes=[
            pltpu.VMEM((model_width, hidden_width), low),
            pltpu.VMEM((hidden_width, model_width), low),
            pltpu.SemaphoreType.DMA((2,)),
        ],
        cost_estimate=cost(6.5e-6),
        compiler_params=pltpu.CompilerParams(vmem_limit_bytes=46 * MIB),
    )(grad, middle, hidden, row, wide, down)


def attn_kernel(
    base,
    middle_grad_ref,
    stream_ref,
    mixed_ref,
    row_ref,
    bias_ref,
    wide_ref,
    stream_grad_ref,
    out_grad_ref,
    mixed_grad_ref,
    vector_ref,
    qkv_low,
    out_low,
    attended_ref,
    sems,
):
    model_width = stream_ref.shape[1]
    size = (qkv_low.shape[1] - model_width) // 2
    cut = qkv_low.shape[1]
    copies = fetch(
        [
            pltpu.make_async_copy(
                wide_ref.at[:, pl.ds(base + cut, model_width)], out_low, sems.at[0]
            ),
            pltpu.make_async_copy(wide_ref.at[:, pl.ds(base, cut)], qkv_low, sems.at[1]),
        ]
    )
    middle_grad = middle_grad_ref[...]
    out_grad = middle_grad.astype(jnp.bfloat16)
    out_grad_ref[...] = out_grad
    vector_ref[...] = jnp.zeros_like(vector_ref)
    vector_ref[3:4, :model_width] = jnp.sum(out_grad.astype(jnp.float32), 0, keepdims=True)
    copies[0].wait()
    attended_ref[...] = dot_last(out_grad, out_low[...]).astype(jnp.bfloat16)
    keys = mixed_ref[:, model_width : model_width + size]
    values = mixed_ref[:, model_width + size :]
    keys_grad = jnp.zeros(keys.shape, jnp.float32)
    values_grad = jnp.zeros(values.shape, jnp.float32)
    for h in range(model_width // size):
        at = slice(h * size, (h + 1) * size)
        queries, probs = head_probs(mixed_ref, bias_ref[...], h, keys, size, model_width)
        grad = attended_ref[:, at]
        values_grad = values_grad + jnp.dot(
            probs.astype(jnp.bfloat16), grad, preferred_element_type=jnp.float32
        )
        probs_grad = dot_last(values, grad)
        scores_grad = probs * (probs_grad - jnp.sum(probs * probs_grad, 0, keepdims=True))
        scores_grad = scores_grad.astype(jnp.bfloat16)
        keys_grad = keys_grad + jnp.dot(
            scores_grad, queries, preferred_element_type=jnp.float32
        )
        mixed_grad_ref[:, at] = (dot_first(scores_grad, keys) * size ** (-0.5)).astype(jnp.bfloat16)
    mixed_grad_ref[:, model_width : model_width + size] = (keys_grad * size ** (-0.5)).astype(
        jnp.bfloat16
    )
    mixed_grad_ref[:, model_width + size :] = values_grad.astype(jnp.bfloat16)
    mixed_grad = mixed_grad_ref[...]
    vector_ref[2:3, :] = jnp.sum(mixed_grad.astype(jnp.float32), 0, keepdims=True)
    copies[1].wait()
    total = dot_last(mixed_grad, qkv_low[...])
    part, gain_grad, shift_grad = norm_back(stream_ref[...], row_ref[0:1, :model_width], total)
    vector_ref[0:1, :model_width] = gain_grad
    vector_ref[1:2, :model_width] = shift_grad
    stream_grad_ref[...] = middle_grad + part


def attn_backward(middle_grad, stream, mixed, row, bias, wide, base):
    length, model_width = stream.shape
    mixed_width = mixed.shape[1]
    f32, low = jnp.float32, jnp.bfloat16
    return pl.pallas_call(
        functools.partial(attn_kernel, base),
        out_shape=(
            shape_of((length, model_width), f32),
            shape_of((length, model_width), low),
            shape_of((length, mixed_width), low),
            shape_of((8, mixed_width), f32),
        ),
        in_specs=[VMEM, VMEM, VMEM, VMEM, VMEM, ANY],
        out_specs=(VMEM,) * 4,
        scratch_shapes=[
            pltpu.VMEM((model_width, mixed_width), low),
            pltpu.VMEM((model_width, model_width), low),
            pltpu.VMEM((length, model_width), low),
            pltpu.SemaphoreType.DMA((2,)),
        ],
        cost_estimate=cost(11e-6),
        compiler_params=pltpu.CompilerParams(vmem_limit_bytes=46 * MIB),
    )(middle_grad, stream, mixed, row, bias, wide)


def adam_update(weight, mean, square, grad, rate):
    mean_new = BETA_ONE * mean + (1.0 - BETA_ONE) * grad
    square_new = BETA_TWO * square + (1.0 - BETA_TWO) * grad * grad
    mean_hat = mean_new / (1.0 - BETA_ONE**STEP)
    square_hat = square_new / (1.0 - BETA_TWO**STEP)
    weight_new = weight - rate * (
        mean_hat / (jnp.sqrt(square_hat) + ADAM_EPS) + WEIGHT_DECAY * weight
    )
    return (weight_new, mean_new, square_new)


def per_device(
    token_ids,
    parents,
    comp_pos,
    targets,
    table,
    table_mean,
    table_square,
    qkv_proj,
    qkv_mean,
    qkv_square,
    out_proj,
    out_mean,
    out_square,
    up_proj,
    up_mean,
    up_square,
    down_proj,
    down_mean,
    down_square,
    vectors,
    vec_mean,
    vec_square,
    pos_table,
    pos_mean,
    pos_square,
):
    place = Place()
    nv, nz = place.nv, place.nz
    length = token_ids.shape[0]
    model_width = pos_table.shape[1]
    head_size = (qkv_proj.shape[2] - model_width) // 2
    layer_width = 7 * model_width + head_size + up_proj.shape[2]
    slot_count = comp_pos.shape[1]
    shard_size, own_width = table.shape
    slice_size = shard_size // (2 * nz)
    bits = place.bits
    orders = (bits, list(reversed(bits)))

    own_slots = comp_pos[0]
    live = own_slots >= 0
    cut_one, cut_two = qkv_proj.shape[2], qkv_proj.shape[2] + out_proj.shape[2]
    cut_three = cut_two + up_proj.shape[2]
    shard_rows = qkv_proj.shape[1]
    ranks = down_proj.shape[1] // shard_rows

    everyone = list(range(nz))
    down_low = down_proj.astype(jnp.bfloat16)
    weights = lax.all_gather(
        jnp.concatenate(
            [
                down_low[0, k * shard_rows : (k + 1) * shard_rows]
                for k in range(ranks)
            ]
            + [a[i].astype(jnp.bfloat16) for i in range(L) for a in (qkv_proj, out_proj, up_proj)],
            1,
        ),
        ALL,
        axis=0,
        tiled=True,
    )
    meta = jnp.concatenate([token_ids, jnp.where(live, targets[0], -1)])
    meta = place.gather_v(place.gather_z(place.gather_c(meta)))

    meta, later = tie((meta, down_low[1]))
    masks = list(range(nv))
    all_targets = put(
        place, [meta[:, :, :1, length:], meta[:, :, 1:, length:]], [(0, masks, everyone), (1, masks, everyone)]
    ).reshape(1, -1)
    meta = meta.transpose(2, 0, 1, 3)
    all_ids = meta[..., :length].reshape(-1)
    local_ids = all_ids - place.v * shard_size
    inside = (local_ids >= 0) & (local_ids < shard_size)
    safe_ids = jnp.where(inside, local_ids, shard_size)
    found = find_rows(safe_ids, table.T)
    second = Held(place.gather_z(later))
    found = found.reshape(2, nv, nz, length, LANES)
    found = jnp.stack([place.reduce_v(found[c], orders[c], 0) for c in range(2)])
    found = tie(found, second)
    second = Held(place.spread_v(second.value, orders[1]))
    found = jnp.stack([found[0], place.swap(found[1], c=1)], 1)
    found = [found[0]] + [place.swap(found[m], z=m) for m in range(1, nz)]
    stream = embed(place, found, pos_table)
    stream, columns = tie((stream, table.T), second)
    second = put_blocks(place, second.value).reshape(-1, model_width)
    stream, columns, second = tie((stream, cut(place, columns), second))
    parts = quarters(place, columns)
    parts[0].step()
    stream = tie(stream, parts[0])
    wdowns = [unslab_rows(place, weights, ranks, model_width), second]

    places, segment, path_depth = tree_layout(length, SEG)
    allowed = tree_mask(parents[0], places, segment, NSEG)
    trunk = 8 * SEG
    bias = jnp.where(allowed, 0.0, -1e30).T
    layer_rows = []
    for layer_index in range(L):
        pieces = split_layer(
            vectors[layer_index * layer_width : (layer_index + 1) * layer_width],
            model_width,
            head_size,
            up_proj.shape[2],
        )
        pieces.append(
            jnp.concatenate([pieces[2], jnp.zeros((head_size,), jnp.float32), pieces[3]])
        )
        layer_rows.append(
            jnp.stack([jnp.pad(p, (0, up_proj.shape[2] - p.shape[0])) for p in pieces])
        )
    inputs_kept = []
    matrices = []
    for layer_index in range(L):
        base = ranks * model_width + layer_index * cut_three
        wide = weights
        if layer_index == 0:
            stream, wdowns = tie((stream, wdowns), *parts)
            parts[1].step()
        wdown = wdowns[layer_index]
        matrices.append((wide, wdown, base))
        result, *saved = layer_forward(
            stream, layer_rows[layer_index], bias, wide, wdown, base, cut_one
        )
        inputs_kept.append((stream, saved))
        stream = result
        if layer_index == 0:
            stream = tie(stream, *parts)
            parts[2].step()
    stream = tie(stream, *parts)
    final_gain = vectors[L * layer_width : L * layer_width + model_width]
    final_shift = vectors[L * layer_width + model_width :]
    finished = norm_apply(stream, final_gain, final_shift).astype(jnp.bfloat16)
    slot_hot = own_slots[:, None] == jnp.arange(length, dtype=jnp.int32)[None, :]
    rows = jnp.dot(
        slot_hot.astype(jnp.bfloat16), finished, preferred_element_type=jnp.float32
    ).astype(jnp.bfloat16)

    held = tie(place.gather_z(rows), *parts)
    parts[3].step()
    held = place.spread_halves(held, orders)
    held = tie(held, *parts)
    group_rows = put_blocks(place, held).reshape(-1, model_width)
    parts = joined(parts)
    mine = parts[:, 0]
    theirs = place.swap(parts[:, 1], c=1)
    slice_low = put(place, [mine[None], theirs[None]], [(0, [0], everyone), (1, [0], everyone)], 1)
    slice_low = slice_low.reshape(model_width, slice_size)
    first_entry = place.v * shard_size + (place.z * 2 + place.c) * slice_size
    first_entry = first_entry.astype(jnp.int32).reshape(1)
    stats = head_forward(first_entry, group_rows, slice_low, all_targets)

    def combine(parts):
        top = functools.reduce(jnp.maximum, [p[0] for p in parts])
        return jnp.stack([top, tree_sum([p[1] * jnp.exp(p[0] - top) for p in parts])])

    whole = stats[:2]
    whole = combine([whole, place.swap(whole, c=1)])
    whole = combine([whole] + [place.swap(whole, v=m) for m in range(1, nv)])
    whole = combine([whole] + [place.swap(whole, z=m) for m in range(1, nz)])
    log_total = whole[0] + jnp.log(whole[1])
    own_total = lax.dynamic_slice_in_dim(
        log_total, ((place.z * 2 + place.c) * nv + place.v) * slot_count, slot_count
    )
    loss_local = jnp.sum(jnp.where(live, own_total, 0.0)) - jnp.sum(stats[2])
    count_local = jnp.sum(live.astype(jnp.float32))
    logits_low, rows_part = head_backward(
        first_entry, group_rows, log_total[None], slice_low, all_targets
    )
    rows_part = rows_part.reshape(nz, 2, nv, slot_count, model_width)
    rows_part = as_wide(pick(rows_part, place.c, 1)) + as_wide(
        place.swap(pick(rows_part, 1 - place.c, 1), c=1)
    )
    own_part = Held(rows_part)
    logits_low = tie(logits_low, own_part)
    rows_part = own_part.value
    head_grad = dot_first(group_rows, logits_low).astype(jnp.bfloat16)
    head_grad = head_grad.reshape(nz, 2, own_width, slice_size)
    head_parts = quarters(place, jnp.stack([pick(head_grad, place.z ^ m, 0) for m in range(nz)]))
    head_parts[0].step()
    rows_part = tree_sum(
        [pick(rows_part, place.v, 1)]
        + [as_wide(place.swap(as_low(pick(rows_part, place.v ^ m, 1)), v=m)) for m in range(1, nv)]
    )
    rows_part = tie(rows_part, *head_parts)
    rows_grad = tree_sum(
        [pick(rows_part, place.z, 0)]
        + [as_wide(place.swap(as_low(pick(rows_part, place.z ^ m, 0)), z=m)) for m in range(1, nz)]
    )
    rows_grad = tie(rows_grad, *head_parts)
    finished_grad = lax.dot_general(
        slot_hot.astype(jnp.float32),
        rows_grad,
        (((0,), (0,)), ((), ())),
        precision=HIGHEST,
        preferred_element_type=jnp.float32,
    )

    ignored, final_pull = jax.vjp(norm_apply, stream, final_gain, final_shift)
    stream_grad, grad_final_gain, grad_final_shift = final_pull(finished_grad)
    vector_parts = [None] * L

    def slabs(grad):
        grad = grad.reshape(nz * nv, ranks, shard_rows, model_width)
        return [grad[:, k].reshape(nz * nv * shard_rows, model_width) for k in range(ranks)]

    def unslab(columns):
        return jnp.concatenate(
            [columns[:, k * model_width : (k + 1) * model_width] for k in range(ranks)]
        )

    summed = [None] * L
    for layer_index in reversed(range(L)):
        kept_stream, saved = inputs_kept[layer_index]
        wide, wdown, base = matrices[layer_index]
        normed, mixed, attended, middle, normed_two, hidden, active = saved
        head_parts[1 if layer_index == 1 else 3].step()
        middle_grad, branch_grad, hidden_grad, late_vectors = mlp_backward(
            stream_grad, middle, hidden, layer_rows[layer_index], wide, wdown, base + cut_two
        )
        middle_grad, branch_grad, hidden_grad = tie(
            (middle_grad, branch_grad, hidden_grad), *head_parts
        )
        g_up = pair_grad(place, normed_two, hidden_grad)
        g_down = slabs(pair_grad_wide(place, active, branch_grad))
        g_mlp = Held([g_up] + g_down)
        middle_grad = tie(middle_grad, g_mlp, *head_parts)
        if layer_index == 1:
            head_parts[2].step()
        stream_grad, out_grad, mixed_grad, early_vectors = attn_backward(
            middle_grad, kept_stream, mixed, layer_rows[layer_index], bias, wide, base
        )
        stream_grad, out_grad, mixed_grad = tie((stream_grad, out_grad, mixed_grad), *head_parts)
        grads = Held(
            jnp.concatenate(
                g_mlp.value
                + [
                    pair_grad(place, normed, mixed_grad),
                    pair_grad(place, attended, out_grad),
                ],
                1,
            )
        )
        stream_grad = tie(stream_grad, grads, *head_parts)
        summed[layer_index] = lax.psum_scatter(
            grads.value, "vocab", scatter_dimension=0, tiled=True
        )
        vector_parts[layer_index] = (early_vectors, late_vectors)

    stream_grad, vector_parts = tie((stream_grad, vector_parts))
    vector_grads = [
        jnp.concatenate(
            [
                early_vectors[0, :model_width],
                early_vectors[1, :model_width],
                early_vectors[2, :model_width],
                early_vectors[2, model_width + head_size :],
                early_vectors[3, :model_width],
                late_vectors[0, :model_width],
                late_vectors[1, :model_width],
                late_vectors[2],
                late_vectors[3, :model_width],
            ]
        )
        for early_vectors, late_vectors in vector_parts
    ]
    sent = part_columns(place, stream_grad)
    sent = Traded(place, sent)
    sent.step()
    pos_grad = jnp.concatenate(
        [
            stream_grad[:trunk],
            jnp.sum(stream_grad[trunk : trunk + 4 * SEG].reshape(4, SEG, model_width), 0),
            jnp.sum(stream_grad[trunk + 4 * SEG :].reshape(8, SEG, model_width), 0),
        ]
    )
    vector_grad = jnp.concatenate(vector_grads + [grad_final_gain, grad_final_shift])
    flat = reduce_flat_core(place, vector_grad, pos_grad)
    flat, upper = tie((reduce_flat_plane(place, flat), summed[1]), sent, *head_parts)
    sent = sent.rest()
    sent = [sent[:, 0], place.swap(sent[:, 1], c=1)]
    sent = Held([place.spread_v(a, order) for a, order in zip(sent, orders)])
    flat_own = Held(reduce_flat_z(place, flat))
    upper = tie(upper, flat_own)
    upper = Held(spread_z(place, upper))
    lower = spread_z(place, tie(summed[0], sent, flat_own, upper))
    head_parts = joined(head_parts)
    mine = pick(head_parts, place.c, 1)
    theirs = place.swap(pick(head_parts, 1 - place.c, 1), c=1)
    head_grad = put(place, [mine[None], theirs[None]], [(0, [0], everyone), (1, [0], everyone)], 1)
    table_grad = add_rows(safe_ids, *[a.reshape(-1, LANES) for a in sent.value], head_grad)
    table_grad, lower = tie((table_grad, lower))
    summed = [tree_sum([as_wide(a) for a in parts]) for parts in (lower, upper.value)]
    up_end = up_proj.shape[2]
    down_end = up_end + ranks * model_width
    grad_up = jnp.stack([a[:, :up_end] for a in summed])
    grad_down = jnp.stack([unslab(a[:, up_end:down_end]) for a in summed])
    grad_qkv = jnp.stack([a[:, down_end : down_end + cut_one] for a in summed])
    grad_out = jnp.stack([a[:, down_end + cut_one :] for a in summed])
    owned_squares = (
        jnp.sum(grad_qkv * grad_qkv)
        + jnp.sum(grad_out * grad_out)
        + jnp.sum(grad_up * grad_up)
        + jnp.sum(grad_down * grad_down)
        + jnp.sum(table_grad * table_grad)
        + jnp.sum(flat_own.value * flat_own.value)
    )
    sums, vector_grad, pos_grad = gather_flat(
        place,
        flat_own.value,
        jnp.stack([owned_squares, loss_local, count_local]),
        vector_grad,
        pos_grad,
    )
    loss_sum, loss_count = sums[1], sums[2]
    grad_norm = jnp.sqrt(sums[0])
    factor = jnp.minimum(1.0, CLIP_NORM / grad_norm)
    states = (
        (table.T, table_mean.T, table_square.T, table_grad, LEARN_RATE),
        (qkv_proj, qkv_mean, qkv_square, grad_qkv, LEARN_RATE),
        (out_proj, out_mean, out_square, grad_out, LEARN_RATE),
        (up_proj, up_mean, up_square, grad_up, LEARN_RATE),
        (down_proj, down_mean, down_square, grad_down, LEARN_RATE),
        (vectors, vec_mean, vec_square, vector_grad, RATE_VEC),
        (pos_table, pos_mean, pos_square, pos_grad, LEARN_RATE),
    )
    results = [loss_sum, loss_count, grad_norm]
    for weight, mean, square, grad, rate in states:
        results.extend(adam_update(weight, mean, square, grad * factor, rate))
    results[3:6] = [a.T for a in results[3:6]]
    return tuple(results)


def solution(mesh):
    chips = mesh.devices.reshape(-1, 2, mesh.shape["vocab"])
    mesh = jax.sharding.Mesh(chips, ALL)
    return jax.shard_map(
        per_device,
        mesh=mesh,
        in_specs=(
            P(ALL),
            P(ALL, None),
            P(ALL, None),
            P(ALL, None),
            P("vocab", ("z", "core")),
            P("vocab", ("z", "core")),
            P("vocab", ("z", "core")),
            P(None, ALL, None),
            P(None, ALL, None),
            P(None, ALL, None),
            P(None, ALL, None),
            P(None, ALL, None),
            P(None, ALL, None),
            P(None, ALL, None),
            P(None, ALL, None),
            P(None, ALL, None),
            P(None, ALL, None),
            P(None, ALL, None),
            P(None, ALL, None),
            P(),
            P(),
            P(),
            P(),
            P(),
            P(),
        ),
        out_specs=(
            P(),
            P(),
            P(),
            P("vocab", ("z", "core")),
            P("vocab", ("z", "core")),
            P("vocab", ("z", "core")),
            P(None, ALL, None),
            P(None, ALL, None),
            P(None, ALL, None),
            P(None, ALL, None),
            P(None, ALL, None),
            P(None, ALL, None),
            P(None, ALL, None),
            P(None, ALL, None),
            P(None, ALL, None),
            P(None, ALL, None),
            P(None, ALL, None),
            P(None, ALL, None),
            P(),
            P(),
            P(),
            P(),
            P(),
            P(),
        ),
        check_vma=False,
    )
```
